512 devices in a mesh: dp: 64 (over y, x, core), mp: 8 (over z).
Axes of the slice: x: 4, y: 8, z: 8, core: 2. Of those that a mesh axis runs over, the one named last changes fastest.
Arguments:
- x_input: bfloat16 [64, 1536, 2048], P('dp', None, 'mp'), may hold values from -24 to 24
- dy_grad: bfloat16 [64, 1536, 2048], P('dp', 'mp'), may hold values from -0.15625 to 0.15625
- error_in: bfloat16 [64, 2048, 2048], P('dp', 'mp'), may hold values from -6 to 6
- q_init: float32 [2048, 64], replicated, may hold values from -0.125 to 0.125
Outputs:
- p_panel: float32 [2048, 64], P('mp')
- q_panel: float32 [2048, 64], replicated
- error_out: bfloat16 [64, 2048, 2048], P('dp', 'mp')
The draws below stay inside these ranges and needn't reach their ends.
All inputs are finite; a program needn't handle non-finite values.
Results may differ from the reference program's by a relative error of at most 0.0011.
Values may be sent and summed in bfloat16 or wider, within the bound.
A program may use at most 64 MiB of HBM per device.

```python
import math
import jax
import jax.numpy as jnp
from jax import lax

DIN = 2048
DOUT = 2048
RANK = 64
SEQ = 1536
N_DP = 64


def draw_x_input(key, part):
    key = jax.random.fold_in(key, 11)
    key_noise, key_scale = jax.random.split(key, 2)
    noise_base = jnp.clip(jax.random.normal(key_noise, (N_DP, SEQ, DIN), jnp.float32), -4.0, 4.0)
    scales = 0.4 * jnp.exp(jax.random.uniform(key_scale, (1, 1, DIN), jnp.float32, 0.0, math.log(10.0)))
    values = noise_base * scales
    return jnp.clip(values, -24.0, 24.0).astype(jnp.bfloat16)


def level_of(rng, dims, shards, least, top_value):
    loudness, own = 1.0, jax.random.fold_in(rng, 6)
    for axis_at, shards_of in shards:
        steps = jnp.exp(jax.random.uniform(jax.random.fold_in(own, axis_at), (shards_of,), jnp.float32, least / len(shards), top_value / len(shards)))
        loudness = loudness * jnp.repeat(steps, dims[axis_at] // shards_of).reshape([-1 if axis == axis_at else 1 for axis in range(len(dims))])
    return loudness


def noise(rng, shape, width, most, cuts=(), held_as=jnp.bfloat16):
    level = level_of(rng, shape, cuts, -0.22, 0.18) if cuts else 1.0
    array = jax.random.normal(rng, shape, jnp.float32) * width * level
    return jnp.minimum(jnp.maximum(array, -most), most).astype(held_as)


def setup_inputs(seed: int = 0) -> dict:
    arg_keys = jax.random.split(jax.random.key(seed), 5)
    return {
        "x_input": draw_x_input(jax.random.fold_in(arg_keys[4], 71), 0),
        "dy_grad": noise(arg_keys[1], (N_DP, SEQ, DOUT), SEQ ** -0.5, 0.15625, ((0, 64), (1, 8))),
        "error_in": noise(arg_keys[2], (N_DP, DIN, DOUT), 1.0, 6.0, ((0, 64), (1, 8))),
        "q_init": noise(arg_keys[3], (DOUT, RANK), DOUT ** -0.5, 0.125, (), jnp.float32),
    }


def reference(x_input, dy_grad, error_in, q_init):
    highest = lax.Precision.HIGHEST

    def one_replica(replica_inputs):
        features, out_grads, errors = replica_inputs
        grad_block = jnp.dot(features.T.astype(jnp.float32), out_grads.astype(jnp.float32), preferred_element_type=jnp.float32)
        return grad_block + errors.astype(jnp.float32)
    corrected = lax.map(one_replica, (x_input, dy_grad, error_in))
    p_sum = jnp.einsum('rij,jk->ik', corrected, q_init, precision=highest)
    gram_matrix = jnp.dot(p_sum.T, p_sum, precision=highest)
    factor = jnp.linalg.cholesky(gram_matrix)
    p_panel = jax.scipy.linalg.solve_triangular(factor, p_sum.T, lower=True).T
    q_panel = jnp.einsum('rij,ik->jk', corrected, p_panel, precision=highest)
    approx = jnp.dot(p_panel, q_panel.T, precision=highest)
    error_out = (corrected - approx[None]).astype(jnp.bfloat16)
    return (p_panel, q_panel, error_out)
```

```python
import jax
import jax.numpy as jnp
from jax import lax
from jax.experimental import pallas as pl
from jax.experimental.pallas import tpu as pltpu
from jax.sharding import PartitionSpec as P

F32, BF16 = jnp.float32, jnp.bfloat16
HIGHEST = lax.Precision.HIGHEST
NZ, NY, NX = 8, 8, 4
NJ = 2 * NX
TOK, FEAT, DOUT, RANK = 192, 256, 2048, 64
CHUNKS = 4
PIECE = TOK // CHUNKS
TILE = 512
N_SEMS = 128

NN = (((1,), (0,)), ((), ()))
NT = (((1,), (1,)), ((), ()))
TN = (((0,), (0,)), ((), ()))


def mm(a, b, dims, precision=None):
    return lax.dot_general(a, b, dims, precision=precision, preferred_element_type=F32)


def split_rows(v):
    high = v.astype(BF16)
    low = (v - high.astype(F32)).astype(BF16)
    return high, low


def split_lanes(v):
    both = v + pltpu.roll(v, RANK, axis=1)
    high = both.astype(BF16).astype(F32)
    lane = lax.broadcasted_iota(jnp.int32, both.shape, 1)
    return jnp.where(lane < RANK, high, both - high).astype(BF16)


def inverse_factor(gram2):
    lane = lax.broadcasted_iota(jnp.int32, gram2.shape, 1)
    row = lax.broadcasted_iota(jnp.int32, gram2.shape, 0)
    rows = lax.broadcasted_iota(jnp.int32, (RANK, 1), 0)
    a = jnp.where(lane < RANK, gram2, jnp.where(lane - RANK == row, 1.0, 0.0))
    for k in range(RANK - 1):
        pivot_row = a[k : k + 1, :]
        scaled = pivot_row * (1.0 / a[k : k + 1, k : k + 1])
        below = jnp.where(rows > k, a[:, k : k + 1], 0.0)
        a = a - below * scaled
    diagonal = jnp.sum(jnp.where(lane == row, a, 0.0), axis=1, keepdims=True)
    root = lax.rsqrt(diagonal)
    root = root * (1.5 - 0.5 * (diagonal * root) * root)
    return jnp.where(lane < RANK, 0.0, a * root)


def kernel(
    x_ref, dy_ref, e_ref, q_ref, p_out, q_out, err_out,
    dyg, xv, ev, qv, yq, acc, part_p, in_pj, in_py, all_p, in_g, all_g, part_x, in_x,
    q_part, in_qc, q_core, in_qx, q_y, in_qy, in_qz, all_qy, all_q, p_keep, err_v,
    send_sem, recv_sem, load_sem,
):
    dp, z = lax.axis_index("dp"), lax.axis_index("mp")
    y, j = lax.div(dp, NJ), lax.rem(dp, NJ)
    x, core = lax.div(j, 2), lax.rem(j, 2)
    counter = iter(range(N_SEMS))
    unsent = []

    at_z = lambda k: (dp, lax.rem(z + k + NZ, NZ))
    at_y = lambda k: (lax.rem(y + k, NY) * NJ + j, z)
    at_j = lambda k: (y * NJ + lax.rem(j + k, NJ), z)
    at_x = lambda k: (y * NJ + lax.rem(x + k, NX) * 2 + core, z)
    at_core = (y * NJ + x * 2 + 1 - core, z)

    def send(src, dst, device):
        n = next(counter)
        copy = pltpu.make_async_remote_copy(
            src_ref=src, dst_ref=dst, send_sem=send_sem.at[n], recv_sem=recv_sem.at[n],
            device_id=device, device_id_type=pl.DeviceIdType.MESH,
        )
        copy.start()
        unsent.append(copy)
        return copy

    loads = [
        pltpu.make_async_copy(src, dst, load_sem.at[n])
        for n, (src, dst) in enumerate(((dy_ref, dyg.at[z]), (q_ref, qv), (x_ref, xv), (e_ref, ev)))
    ]
    for load in loads:
        load.start()

    barrier = pltpu.get_barrier_semaphore()
    peers = [at_z(k) for k in range(1, NZ)] + [at_y(k) for k in range(1, NY)] + [at_j(k) for k in range(1, NJ)]
    for peer in peers:
        pl.semaphore_signal(barrier, inc=1, device_id=peer, device_id_type=pl.DeviceIdType.MESH)

    loads[0].wait()
    loads[1].wait()
    q_halves = jnp.concatenate(split_rows(qv[...]), axis=0)
    yq[z] = split_lanes(mm(dyg[z], q_halves, NT))
    pl.semaphore_wait(barrier, len(peers))

    flows = {
        1: [(h, c) for h in (1, 2, 3) for c in range(CHUNKS)] + [(4, 0), (4, 1)],
        -1: [(h, c) for h in (1, 2, 3) for c in range(CHUNKS)] + [(4, 2), (4, 3)],
    }
    bulk = {}

    def bulk_send(way, hop, c):
        block = lax.rem(z - way * (hop - 1) + NZ, NZ)
        ref = dyg.at[block, pl.ds(c * PIECE, PIECE)]
        bulk[way, hop, c] = send(ref, ref, at_z(way))

    def bulk_forward(n):
        for way in (1, -1):
            hop, c = flows[way][n]
            bulk[way, hop, c].wait_recv()
            if (hop + 1, c) in flows[way]:
                bulk_send(way, hop + 1, c)

    def add_grad(block):
        @pl.loop(0, DOUT // TILE)
        def _(t):
            cols = pl.ds(pl.multiple_of(t * TILE, TILE), TILE)
            acc[:, cols] += mm(xv[block], dyg[block, :, cols], TN)

    right = send(yq.at[z], yq.at[z], at_z(1))
    left = send(yq.at[z], yq.at[z], at_z(-1))
    for c in (0, 1):
        bulk_send(1, 1, c)
        bulk_send(-1, 1, c)
    loads[2].wait()
    loads[3].wait()
    total = mm(q_halves, ev[...], NT) + mm(yq[z], xv[z], TN)
    for hop in (1, 2, 3, 4):
        from_left, from_right = lax.rem(z - hop + NZ, NZ), lax.rem(z + hop, NZ)
        right.wait_recv()
        if hop < 4:
            right = send(yq.at[from_left], yq.at[from_left], at_z(1))
            left.wait_recv()
            if hop < 3:
                left = send(yq.at[from_right], yq.at[from_right], at_z(-1))
            total += mm(yq[from_right], xv[from_right], TN)
        total += mm(yq[from_left], xv[from_left], TN)
    for c in (2, 3):
        bulk_send(1, 1, c)
        bulk_send(-1, 1, c)
    total = total[:RANK] + total[RANK:]

    for k in range(NJ):
        part_p[k] = total[k * 8 : k * 8 + 8]
    copies = [send(part_p.at[lax.rem(j + k, NJ)], in_pj.at[j], at_j(k)) for k in range(1, NJ)]
    in_pj[j] = part_p[j]

    @pl.loop(0, DOUT // TILE)
    def _(t):
        cols = pl.ds(pl.multiple_of(t * TILE, TILE), TILE)
        acc[:, cols] = ev[:, cols].astype(F32) + mm(xv[z], dyg[z, :, cols], TN)

    for copy in copies:
        copy.wait_recv()
    in_py[y] = sum(in_pj[k] for k in range(1, NJ)) + in_pj[0]
    copies = [send(in_py.at[y], in_py.at[y], at_y(k)) for k in range(1, NY)]
    bulk_forward(0)
    for copy in copies:
        copy.wait_recv()
    all_p[j] = sum(in_py[k] for k in range(1, NY)) + in_py[0]
    copies = [send(all_p.at[j], all_p.at[j], at_j(k)) for k in range(1, NJ)]
    for copy in copies:
        copy.wait_recv()
    p_sum = all_p[...].reshape(RANK, FEAT)
    p_twice = jnp.concatenate([p_sum, p_sum], axis=0)

    in_g[z] = mm(all_p[j], p_twice, NT, HIGHEST)
    copies = [send(in_g.at[z], in_g.at[z], at_z(k)) for k in range(1, NZ)]
    bulk_forward(1)
    for copy in copies:
        copy.wait_recv()
    all_g[j] = sum(in_g[k] for k in range(1, NZ)) + in_g[0]
    copies = [send(all_g.at[j], all_g.at[j], at_j(k)) for k in range(1, NJ)]
    bulk_forward(2)
    for copy in copies:
        copy.wait_recv()
    inverse = inverse_factor(all_g[...].reshape(RANK, 2 * RANK))
    p_t = mm(inverse, p_twice, NN, HIGHEST)
    p_keep[...] = p_t
    p_store = pltpu.make_async_copy(p_keep, p_out, load_sem.at[4])
    p_store.start()
    p_high, p_low = split_rows(p_t)
    p_halves = jnp.concatenate([p_high, p_low], axis=0)

    copies = []
    for k in (4, 3, 5, 2, 6, 1, 7):
        block = lax.rem(z + k, NZ)
        part_x[block] = split_lanes(mm(xv[block], p_halves, NT))
        copies.append(send(part_x.at[block], in_x.at[z], at_z(k)))
    in_x[z] = split_lanes(mm(xv[z], p_halves, NT))
    bulk_forward(3)
    add_grad(lax.rem(z + NZ - 1, NZ))
    add_grad(lax.rem(z + 1, NZ))
    bulk_forward(4)
    for copy in copies:
        copy.wait_recv()
    xp = split_lanes(sum(in_x[k].astype(F32) for k in range(1, NZ)) + in_x[0].astype(F32))
    bulk_forward(5)

    for t in range(DOUT // TILE):
        cols = slice(t * TILE, t * TILE + TILE)
        tile = mm(xp, dyg[z, :, cols], TN) + mm(p_halves, ev[:, cols], NN)
        tile = tile[:RANK] + tile[RANK:]
        for k in range(8):
            q_part[k // 4, k % 4, :, cols] = tile[k * 8 : k * 8 + 8]
    copy = send(q_part.at[1 - core], in_qc, at_core)
    bulk_forward(6)
    copy.wait_recv()
    for k in range(NX):
        q_core[k] = q_part[core, k] + in_qc[k]
    copies = [send(q_core.at[lax.rem(x + k, NX)], in_qx.at[x], at_x(k)) for k in range(1, NX)]
    in_qx[x] = q_core[x]
    bulk_forward(7)
    for copy in copies:
        copy.wait_recv()
    rows = (in_qx[0] + in_qx[1]) + (in_qx[2] + in_qx[3])
    for k in range(NY):
        q_y[k] = rows[:, k * 256 : k * 256 + 256]
    copies = [send(q_y.at[lax.rem(y + k, NY)], in_qy.at[y], at_y(k)) for k in range(1, NY)]
    in_qy[y] = q_y[y]
    for copy in copies:
        copy.wait_recv()
    in_qz[z] = sum(in_qy[k] for k in range(1, NY)) + in_qy[0]
    copies = [send(in_qz.at[z], in_qz.at[z], at_z(k)) for k in range(1, NZ)]
    add_grad(lax.rem(z + NZ - 2, NZ))
    add_grad(lax.rem(z + 2, NZ))
    bulk_forward(8)
    for copy in copies:
        copy.wait_recv()
    all_qy[y] = sum(in_qz[k] for k in range(1, NZ)) + in_qz[0]
    copies = [send(all_qy.at[y], all_qy.at[y], at_y(k)) for k in range(1, NY)]
    bulk_forward(9)
    for copy in copies:
        copy.wait_recv()
    mine = core * NX + x
    for k in range(NY):
        all_q[mine, :, k * 256 : k * 256 + 256] = all_qy[k]
    copies = [send(all_q.at[mine], all_q.at[mine], at_x(k)) for k in range(1, NX)]
    across = [send(all_q.at[mine], all_q.at[mine], at_core)]
    for k, copy in enumerate(copies):
        copy.wait_recv()
        slot = core * NX + lax.rem(x - (k + 1) + NX, NX)
        across.append(send(all_q.at[slot], all_q.at[slot], at_core))
    bulk_forward(10)
    bulk_forward(11)
    for copy in across:
        copy.wait_recv()
    q_store = pltpu.make_async_copy(all_q, q_out, load_sem.at[5])
    q_store.start()
    p_cat = jnp.concatenate([p_high, p_high, p_low], axis=0)

    @pl.loop(0, DOUT // TILE)
    def _(t):
        cols = pl.ds(pl.multiple_of(t * TILE, TILE), TILE)
        q_high, q_low = split_rows(all_q[:, :, cols].reshape(RANK, TILE))
        acc[:, cols] -= mm(p_cat, jnp.concatenate([q_high, q_low, q_high], axis=0), TN)

    add_grad(lax.rem(z + NZ - 3, NZ))
    add_grad(lax.rem(z + 3, NZ))
    bulk_forward(12)
    bulk_forward(13)
    far = lax.rem(z + 4, NZ)
    stores = []
    for t in range(DOUT // TILE):
        cols = slice(t * TILE, t * TILE + TILE)
        err_v[:, cols] = (acc[:, cols] + mm(xv[far], dyg[far, :, cols], TN)).astype(BF16)
        store = pltpu.make_async_copy(err_v.at[:, cols], err_out.at[:, cols], load_sem.at[6 + t])
        store.start()
        stores.append(store)
    for copy in unsent:
        copy.wait_send()
    p_store.wait()
    q_store.wait()
    for store in stores:
        store.wait()


def local(x_input, dy_grad, error_in, q_init):
    anywhere = pl.BlockSpec(memory_space=pl.ANY)
    vmem = lambda *shape, dtype=F32: pltpu.VMEM(shape, dtype)
    p_t, q_t, err = pl.pallas_call(
        kernel,
        out_shape=(
            jax.ShapeDtypeStruct((RANK, FEAT), F32),
            jax.ShapeDtypeStruct((8, 8, DOUT), F32),
            jax.ShapeDtypeStruct((FEAT, DOUT), BF16),
        ),
        in_specs=[anywhere] * 4,
        out_specs=(anywhere,) * 3,
        scratch_shapes=[
            vmem(NZ, TOK, DOUT, dtype=BF16),
            vmem(NZ, TOK, FEAT, dtype=BF16),
            vmem(FEAT, DOUT, dtype=BF16),
            vmem(RANK, DOUT),
            vmem(NZ, TOK, 2 * RANK, dtype=BF16),
            vmem(FEAT, DOUT),
            vmem(NJ, 8, FEAT), vmem(NJ, 8, FEAT), vmem(NY, 8, FEAT), vmem(NJ, 8, FEAT),
            vmem(NZ, 8, 2 * RANK), vmem(NJ, 8, 2 * RANK),
            vmem(NZ, TOK, 2 * RANK, dtype=BF16), vmem(NZ, TOK, 2 * RANK, dtype=BF16),
            vmem(2, NX, 8, DOUT), vmem(NX, 8, DOUT), vmem(NX, 8, DOUT), vmem(NX, 8, DOUT),
            vmem(NY, 8, FEAT), vmem(NY, 8, FEAT), vmem(NZ, 8, FEAT), vmem(NY, 8, FEAT),
            vmem(8, 8, DOUT),
            vmem(RANK, FEAT),
            vmem(FEAT, DOUT, dtype=BF16),
            pltpu.SemaphoreType.DMA((N_SEMS,)),
            pltpu.SemaphoreType.DMA((N_SEMS,)),
            pltpu.SemaphoreType.DMA((10,)),
        ],
        compiler_params=pltpu.CompilerParams(
            collective_id=0, has_side_effects=True, vmem_limit_bytes=48 * 1024 * 1024
        ),
        cost_estimate=pl.CostEstimate(flops=2 * 10**9, bytes_accessed=6 * 10**6, transcendentals=0),
    )(x_input.reshape(NZ, TOK, FEAT), dy_grad[0], error_in[0], q_init.T)
    return p_t.T, q_t.reshape(RANK, DOUT).T, err[None]


def solution(mesh):
    in_specs = (P("dp", None, "mp"), P("dp", "mp", None), P("dp", "mp", None), P())
    out_specs = (P("mp", None), P(), P("dp", "mp", None))
    return jax.shard_map(local, mesh=mesh, in_specs=in_specs, out_specs=out_specs, check_vma=False)
```

```python
import jax
import jax.numpy as jnp
from jax import lax
from jax.experimental import pallas as pl
from jax.experimental.pallas import tpu as pltpu
from jax.sharding import PartitionSpec as P

F32, BF16 = jnp.float32, jnp.bfloat16
HIGHEST = lax.Precision.HIGHEST
NZ, NY, NX = 8, 8, 4
NJ = 2 * NX
TOK, FEAT, DOUT, RANK = 192, 256, 2048, 64
CHUNKS = 4
PIECE = TOK // CHUNKS
TILE = 512
N_SEMS = 128
NEAR = 2

NN = (((1,), (0,)), ((), ()))
NT = (((1,), (1,)), ((), ()))
TN = (((0,), (0,)), ((), ()))


def mm(a, b, dims, precision=None):
    return lax.dot_general(a, b, dims, precision=precision, preferred_element_type=F32)


def split_rows(v):
    high = v.astype(BF16)
    low = (v - high.astype(F32)).astype(BF16)
    return high, low


def split_lanes(v):
    both = v + pltpu.roll(v, RANK, axis=1)
    high = both.astype(BF16).astype(F32)
    lane = lax.broadcasted_iota(jnp.int32, both.shape, 1)
    return jnp.where(lane < RANK, high, both - high).astype(BF16)


def inverse_factor(gram2, between):
    lane = lax.broadcasted_iota(jnp.int32, gram2.shape, 1)
    row = lax.broadcasted_iota(jnp.int32, gram2.shape, 0)
    rows = lax.broadcasted_iota(jnp.int32, (RANK, 1), 0)
    a = jnp.where(lane < RANK, gram2, jnp.where(lane - RANK == row, 1.0, 0.0))
    for k in range(RANK - 1):
        pivot_row = a[k : k + 1, :]
        scaled = pivot_row * (1.0 / a[k : k + 1, k : k + 1])
        below = jnp.where(rows > k, a[:, k : k + 1], 0.0)
        a = a - below * scaled
        between(k)
    diagonal = jnp.sum(jnp.where(lane == row, a, 0.0), axis=1, keepdims=True)
    root = lax.rsqrt(diagonal)
    root = root * (1.5 - 0.5 * (diagonal * root) * root)
    return jnp.where(lane < RANK, 0.0, a * root)


def kernel(
    x_ref, dy_ref, e_ref, q_ref, p_out, q_out, err_out,
    dyg, xv, ev, qv, yq, acc, part_p, in_pj, in_py, all_p, in_g, all_g, part_x, in_x,
    q_part, in_qc, q_core, in_qx, q_y, in_qy, in_qz, all_qy, all_q, p_keep, err_v,
    send_sem, recv_sem, load_sem,
):
    dp, z = lax.axis_index("dp"), lax.axis_index("mp")
    y, j = lax.div(dp, NJ), lax.rem(dp, NJ)
    x, core = lax.div(j, 2), lax.rem(j, 2)
    counter = iter(range(N_SEMS))
    unsent = []

    at_z = lambda k: (dp, lax.rem(z + k + NZ, NZ))
    at_y = lambda k: (lax.rem(y + k, NY) * NJ + j, z)
    at_j = lambda k: (y * NJ + lax.rem(j + k, NJ), z)
    at_x = lambda k: (y * NJ + lax.rem(x + k, NX) * 2 + core, z)
    at_core = (y * NJ + x * 2 + 1 - core, z)

    def send(src, dst, device):
        n = next(counter)
        copy = pltpu.make_async_remote_copy(
            src_ref=src, dst_ref=dst, send_sem=send_sem.at[n], recv_sem=recv_sem.at[n],
            device_id=device, device_id_type=pl.DeviceIdType.MESH,
        )
        copy.start()
        unsent.append(copy)
        return copy

    loads = [
        pltpu.make_async_copy(src, dst, load_sem.at[n])
        for n, (src, dst) in enumerate(((dy_ref, dyg.at[z]), (q_ref, qv), (x_ref, xv), (e_ref, ev)))
    ]
    for load in loads:
        load.start()

    barrier = pltpu.get_barrier_semaphore()
    peers = [at_z(k) for k in range(1, NZ)] + [at_y(k) for k in range(1, NY)] + [at_j(k) for k in range(1, NJ)]
    for peer in peers:
        pl.semaphore_signal(barrier, inc=1, device_id=peer, device_id_type=pl.DeviceIdType.MESH)

    loads[0].wait()
    loads[1].wait()
    q_halves = jnp.concatenate(split_rows(qv[...]), axis=0)
    yq[z] = split_lanes(mm(dyg[z], q_halves, NT))
    pl.semaphore_wait(barrier, len(peers))

    flows = {
        1: [(h, c) for h in (1, 2, 3) for c in range(CHUNKS)] + [(4, 0), (4, 1)],
        -1: [(h, c) for h in (1, 2, 3) for c in range(CHUNKS)] + [(4, 2), (4, 3)],
    }
    bulk = {}

    def bulk_send(way, hop, c):
        block = lax.rem(z - way * (hop - 1) + NZ, NZ)
        ref = dyg.at[block, pl.ds(c * PIECE, PIECE)]
        bulk[way, hop, c] = send(ref, ref, at_z(way))

    def bulk_forward(n):
        for way in (1, -1):
            hop, c = flows[way][n]
            bulk[way, hop, c].wait_recv()
            if (hop + 1, c) in flows[way]:
                bulk_send(way, hop + 1, c)

    def add_grad(block):
        @pl.loop(0, DOUT // TILE)
        def _(t):
            cols = pl.ds(pl.multiple_of(t * TILE, TILE), TILE)
            acc[:, cols] += mm(xv[block], dyg[block, :, cols], TN)

    copies = [send(yq.at[z], yq.at[z], at_z(k)) for k in (4, 3, 5, 2, 6, 1, 7)]
    for c in range(CHUNKS):
        bulk_send(1, 1, c)
        bulk_send(-1, 1, c)
    loads[2].wait()
    loads[3].wait()
    total = mm(q_halves, ev[...], NT) + mm(yq[z], xv[z], TN)
    for k, copy in reversed(list(zip((4, 3, 5, 2, 6, 1, 7), copies))):
        copy.wait_recv()
        block = lax.rem(z - k + NZ, NZ)
        total += mm(yq[block], xv[block], TN)
    total = total[:RANK] + total[RANK:]

    for k in range(NJ):
        part_p[k] = total[k * 8 : k * 8 + 8]
    copies = [send(part_p.at[lax.rem(j + k, NJ)], in_pj.at[j], at_j(k)) for k in range(1, NJ)]
    in_pj[j] = part_p[j]

    @pl.loop(0, DOUT // TILE)
    def _(t):
        cols = pl.ds(pl.multiple_of(t * TILE, TILE), TILE)
        acc[:, cols] = ev[:, cols].astype(F32) + mm(xv[z], dyg[z, :, cols], TN)

    bulk_forward(0)
    for copy in copies:
        copy.wait_recv()
    in_py[y] = sum(in_pj[k] for k in range(1, NJ)) + in_pj[0]
    copies = [send(in_py.at[y], in_py.at[y], at_y(k)) for k in range(1, NY)]
    bulk_forward(1)
    for copy in copies:
        copy.wait_recv()
    all_p[j] = sum(in_py[k] for k in range(1, NY)) + in_py[0]
    copies = [send(all_p.at[j], all_p.at[j], at_j(k)) for k in range(1, NJ)]
    bulk_forward(2)
    for copy in copies:
        copy.wait_recv()
    p_sum = all_p[...].reshape(RANK, FEAT)
    p_twice = jnp.concatenate([p_sum, p_sum], axis=0)

    in_g[z] = mm(all_p[j], p_twice, NT, HIGHEST)
    copies = [send(in_g.at[z], in_g.at[z], at_z(k)) for k in range(1, NZ)]
    bulk_forward(3)
    add_grad(lax.rem(z + NZ - 1, NZ))
    add_grad(lax.rem(z + 1, NZ))
    for copy in copies:
        copy.wait_recv()
    all_g[j] = sum(in_g[k] for k in range(1, NZ)) + in_g[0]
    copies = [send(all_g.at[j], all_g.at[j], at_j(k)) for k in range(1, NJ)]
    bulk_forward(4)
    for copy in copies:
        copy.wait_recv()
    steps = {20: 5, 40: 6}
    between = lambda k: bulk_forward(steps[k]) if k in steps else None
    inverse = inverse_factor(all_g[...].reshape(RANK, 2 * RANK), between)
    p_t = mm(inverse, p_twice, NN, HIGHEST)
    p_keep[...] = p_t
    p_store = pltpu.make_async_copy(p_keep, p_out, load_sem.at[4])
    p_store.start()
    p_high, p_low = split_rows(p_t)
    p_halves = jnp.concatenate([p_high, p_low], axis=0)

    far_steps = [k for k in (4, 3, 5, 2, 6, 1, 7) if min(k, NZ - k) > NEAR]
    copies = []
    for k in far_steps:
        block = lax.rem(z + k, NZ)
        part_x[block] = split_lanes(mm(xv[block], p_halves, NT))
        copies.append(send(part_x.at[block], in_x.at[z], at_z(k)))
    bulk_forward(7)
    for hop in range(2, NEAR + 1):
        add_grad(lax.rem(z + NZ - hop, NZ))
        add_grad(lax.rem(z + hop, NZ))
    for copy in copies:
        copy.wait_recv()
    xp = split_lanes(sum(in_x[lax.rem(z + NZ - k, NZ)].astype(F32) for k in far_steps))

    for t in range(DOUT // TILE):
        cols = slice(t * TILE, t * TILE + TILE)
        near_high, near_low = split_rows(acc[:, cols])
        tile = mm(xp, dyg[z, :, cols], TN) + mm(p_halves, near_high, NN)
        tile = tile[:RANK] + tile[RANK:] + mm(p_high, near_low, NN)
        for k in range(8):
            q_part[k // 4, k % 4, :, cols] = tile[k * 8 : k * 8 + 8]
    copy = send(q_part.at[1 - core], in_qc, at_core)
    bulk_forward(8)
    copy.wait_recv()
    for k in range(NX):
        q_core[k] = q_part[core, k] + in_qc[k]
    copies = [send(q_core.at[lax.rem(x + k, NX)], in_qx.at[x], at_x(k)) for k in range(1, NX)]
    in_qx[x] = q_core[x]
    for copy in copies:
        copy.wait_recv()
    rows = (in_qx[0] + in_qx[1]) + (in_qx[2] + in_qx[3])
    for k in range(NY):
        q_y[k] = rows[:, k * 256 : k * 256 + 256]
    copies = [send(q_y.at[lax.rem(y + k, NY)], in_qy.at[y], at_y(k)) for k in range(1, NY)]
    in_qy[y] = q_y[y]
    bulk_forward(9)
    for copy in copies:
        copy.wait_recv()
    in_qz[z] = sum(in_qy[k] for k in range(1, NY)) + in_qy[0]
    copies = [send(in_qz.at[z], in_qz.at[z], at_z(k)) for k in range(1, NZ)]
    bulk_forward(10)
    bulk_forward(11)
    for copy in copies:
        copy.wait_recv()
    all_qy[y] = sum(in_qz[k] for k in range(1, NZ)) + in_qz[0]
    copies = [send(all_qy.at[y], all_qy.at[y], at_y(k)) for k in range(1, NY)]
    for hop in range(NEAR + 1, 4):
        add_grad(lax.rem(z + NZ - hop, NZ))
        add_grad(lax.rem(z + hop, NZ))
    for copy in copies:
        copy.wait_recv()
    mine = core * NX + x
    for k in range(NY):
        all_q[mine, :, k * 256 : k * 256 + 256] = all_qy[k]
    copies = [send(all_q.at[mine], all_q.at[mine], at_x(k)) for k in range(1, NX)]
    across = [send(all_q.at[mine], all_q.at[mine], at_core)]
    for k, copy in enumerate(copies):
        copy.wait_recv()
        slot = core * NX + lax.rem(x - (k + 1) + NX, NX)
        across.append(send(all_q.at[slot], all_q.at[slot], at_core))
    bulk_forward(12)
    bulk_forward(13)
    add_grad(lax.rem(z + 4, NZ))
    for copy in across:
        copy.wait_recv()
    q_store = pltpu.make_async_copy(all_q, q_out, load_sem.at[5])
    q_store.start()
    p_cat = jnp.concatenate([p_high, p_high, p_low], axis=0)
    stores = []
    for t in range(DOUT // TILE):
        cols = slice(t * TILE, t * TILE + TILE)
        q_high, q_low = split_rows(all_q[:, :, cols].reshape(RANK, TILE))
        approx = mm(p_cat, jnp.concatenate([q_high, q_low, q_high], axis=0), TN)
        err_v[:, cols] = (acc[:, cols] - approx).astype(BF16)
        store = pltpu.make_async_copy(err_v.at[:, cols], err_out.at[:, cols], load_sem.at[6 + t])
        store.start()
        stores.append(store)
    for copy in unsent:
        copy.wait_send()
    p_store.wait()
    q_store.wait()
    for store in stores:
        store.wait()


def local(x_input, dy_grad, error_in, q_init):
    anywhere = pl.BlockSpec(memory_space=pl.ANY)
    vmem = lambda *shape, dtype=F32: pltpu.VMEM(shape, dtype)
    p_t, q_t, err = pl.pallas_call(
        kernel,
        out_shape=(
            jax.ShapeDtypeStruct((RANK, FEAT), F32),
            jax.ShapeDtypeStruct((8, 8, DOUT), F32),
            jax.ShapeDtypeStruct((FEAT, DOUT), BF16),
        ),
        in_specs=[anywhere] * 4,
        out_specs=(anywhere,) * 3,
        scratch_shapes=[
            vmem(NZ, TOK, DOUT, dtype=BF16),
            vmem(NZ, TOK, FEAT, dtype=BF16),
            vmem(FEAT, DOUT, dtype=BF16),
            vmem(RANK, DOUT),
            vmem(NZ, TOK, 2 * RANK, dtype=BF16),
            vmem(FEAT, DOUT),
            vmem(NJ, 8, FEAT), vmem(NJ, 8, FEAT), vmem(NY, 8, FEAT), vmem(NJ, 8, FEAT),
            vmem(NZ, 8, 2 * RANK), vmem(NJ, 8, 2 * RANK),
            vmem(NZ, TOK, 2 * RANK, dtype=BF16), vmem(NZ, TOK, 2 * RANK, dtype=BF16),
            vmem(2, NX, 8, DOUT), vmem(NX, 8, DOUT), vmem(NX, 8, DOUT), vmem(NX, 8, DOUT),
            vmem(NY, 8, FEAT), vmem(NY, 8, FEAT), vmem(NZ, 8, FEAT), vmem(NY, 8, FEAT),
            vmem(8, 8, DOUT),
            vmem(RANK, FEAT),
            vmem(FEAT, DOUT, dtype=BF16),
            pltpu.SemaphoreType.DMA((N_SEMS,)),
            pltpu.SemaphoreType.DMA((N_SEMS,)),
            pltpu.SemaphoreType.DMA((10,)),
        ],
        compiler_params=pltpu.CompilerParams(
            collective_id=0, has_side_effects=True, vmem_limit_bytes=60 * 1024 * 1024
        ),
        cost_estimate=pl.CostEstimate(flops=2 * 10**9, bytes_accessed=6 * 10**6, transcendentals=0),
    )(x_input.reshape(NZ, TOK, FEAT), dy_grad[0], error_in[0], q_init.T)
    return p_t.T, q_t.reshape(RANK, DOUT).T, err[None]


def solution(mesh):
    in_specs = (P("dp", None, "mp"), P("dp", "mp", None), P("dp", "mp", None), P())
    out_specs = (P("mp", None), P(), P("dp", "mp", None))
    return jax.shard_map(local, mesh=mesh, in_specs=in_specs, out_specs=out_specs, check_vma=False)
```

```python
import jax
import jax.numpy as jnp
from jax import lax
from jax.experimental import pallas as pl
from jax.experimental.pallas import tpu as pltpu
from jax.sharding import PartitionSpec as P

F32, BF16 = jnp.float32, jnp.bfloat16
HIGHEST = lax.Precision.HIGHEST
NZ, NY, NX = 8, 8, 4
NJ = 2 * NX
TOK, FEAT, DOUT, RANK = 192, 256, 2048, 64
CHUNKS = 4
PIECE = TOK // CHUNKS
TILE = 512
PIVOTS = 4
N_SEMS = 128
NEAR = 2

NN = (((1,), (0,)), ((), ()))
NT = (((1,), (1,)), ((), ()))
TN = (((0,), (0,)), ((), ()))


def mm(a, b, dims, precision=None):
    return lax.dot_general(a, b, dims, precision=precision, preferred_element_type=F32)


def split_rows(v):
    high = v.astype(BF16)
    low = (v - high.astype(F32)).astype(BF16)
    return high, low


def split_lanes(v):
    both = v + pltpu.roll(v, RANK, axis=1)
    high = both.astype(BF16).astype(F32)
    lane = lax.broadcasted_iota(jnp.int32, both.shape, 1)
    return jnp.where(lane < RANK, high, both - high).astype(BF16)


def inverse_factor(gram2, between):
    lane = lax.broadcasted_iota(jnp.int32, gram2.shape, 1)
    row = lax.broadcasted_iota(jnp.int32, gram2.shape, 0)
    rows = lax.broadcasted_iota(jnp.int32, (RANK, 1), 0)
    a = jnp.where(lane < RANK, gram2, jnp.where(lane - RANK == row, 1.0, 0.0))
    for k in range(0, RANK, PIVOTS):
        columns = [jnp.broadcast_to(a[:, k + i : k + i + 1], a.shape) for i in range(PIVOTS)]
        lines = [a[k + i : k + i + 1, :] for i in range(PIVOTS)]
        for i in range(PIVOTS):
            here = slice(k + i, k + i + 1)
            factor = jnp.where(rows > k + i, columns[i] * (1.0 / columns[i][here]), 0.0)
            for later in range(i + 1, PIVOTS):
                columns[later] = columns[later] - factor * columns[later][here]
                lines[later] = lines[later] - factor[k + later : k + later + 1] * lines[i]
            a = a - factor * lines[i]
        between(k)
    diagonal = jnp.sum(jnp.where(lane == row, a, 0.0), axis=1, keepdims=True)
    root = lax.rsqrt(diagonal)
    root = root * (1.5 - 0.5 * (diagonal * root) * root)
    return jnp.where(lane < RANK, 0.0, a * root)


def kernel(
    x_ref, dy_ref, e_ref, q_ref, p_out, q_out, err_out,
    dyg, xv, ev, qv, yq, acc, part_p, in_pj, in_py, all_p, in_g, all_g, part_x, in_x,
    q_part, in_qc, q_core, in_qx, q_y, in_qy, in_qz, all_qy, all_q, p_keep, err_v,
    send_sem, recv_sem, load_sem,
):
    dp, z = lax.axis_index("dp"), lax.axis_index("mp")
    y, j = lax.div(dp, NJ), lax.rem(dp, NJ)
    x, core = lax.div(j, 2), lax.rem(j, 2)
    counter = iter(range(N_SEMS))
    unsent = []

    at_z = lambda k: (dp, lax.rem(z + k + NZ, NZ))
    at_y = lambda k: (lax.rem(y + k, NY) * NJ + j, z)
    at_j = lambda k: (y * NJ + lax.rem(j + k, NJ), z)
    at_x = lambda k: (y * NJ + lax.rem(x + k, NX) * 2 + core, z)
    at_core = (y * NJ + x * 2 + 1 - core, z)

    def send(src, dst, device):
        n = next(counter)
        copy = pltpu.make_async_remote_copy(
            src_ref=src, dst_ref=dst, send_sem=send_sem.at[n], recv_sem=recv_sem.at[n],
            device_id=device, device_id_type=pl.DeviceIdType.MESH,
        )
        copy.start()
        unsent.append(copy)
        return copy

    def receive(copies):
        while len(unsent) > len(copies):
            unsent.pop(0).wait_send()
        for copy in copies:
            copy.wait_recv()

    loads = [
        pltpu.make_async_copy(src, dst, load_sem.at[n])
        for n, (src, dst) in enumerate(((dy_ref, dyg.at[z]), (q_ref, qv), (x_ref, xv), (e_ref, ev)))
    ]
    for load in loads:
        load.start()

    barrier = pltpu.get_barrier_semaphore()
    peers = [at_z(k) for k in range(1, NZ)] + [at_y(k) for k in range(1, NY)] + [at_j(k) for k in range(1, NJ)]
    for peer in peers:
        pl.semaphore_signal(barrier, inc=1, device_id=peer, device_id_type=pl.DeviceIdType.MESH)

    loads[0].wait()
    loads[1].wait()
    q_halves = jnp.concatenate(split_rows(qv[...]), axis=0)
    yq[z] = split_lanes(mm(dyg[z], q_halves, NT))
    pl.semaphore_wait(barrier, len(peers))

    flows = {
        1: [(h, c) for h in (1, 2, 3) for c in range(CHUNKS)] + [(4, 0), (4, 1)],
        -1: [(h, c) for h in (1, 2, 3) for c in range(CHUNKS)] + [(4, 2), (4, 3)],
    }
    bulk = {}

    def bulk_send(way, hop, c):
        block = lax.rem(z - way * (hop - 1) + NZ, NZ)
        ref = dyg.at[block, pl.ds(c * PIECE, PIECE)]
        bulk[way, hop, c] = send(ref, ref, at_z(way))
        unsent.pop()

    def bulk_forward(n):
        for way in (1, -1):
            hop, c = flows[way][n]
            bulk[way, hop, c].wait_recv()
            if (hop + 1, c) in flows[way]:
                bulk_send(way, hop + 1, c)
            if n >= 2:
                bulk[(way, *flows[way][n - 2])].wait_send()

    def add_grad(block):
        @pl.loop(0, DOUT // TILE)
        def _(t):
            cols = pl.ds(pl.multiple_of(t * TILE, TILE), TILE)
            acc[:, cols] += mm(xv[block], dyg[block, :, cols], TN)

    copies = [send(yq.at[z], yq.at[z], at_z(k)) for k in (4, 3, 5, 2, 6, 1, 7)]
    for c in range(CHUNKS):
        bulk_send(1, 1, c)
        bulk_send(-1, 1, c)
    loads[2].wait()
    loads[3].wait()
    total = mm(q_halves, ev[...], NT) + mm(yq[z], xv[z], TN)
    for k, copy in reversed(list(zip((4, 3, 5, 2, 6, 1, 7), copies))):
        copy.wait_recv()
        block = lax.rem(z - k + NZ, NZ)
        total += mm(yq[block], xv[block], TN)
    total = total[:RANK] + total[RANK:]

    for k in range(NJ):
        part_p[k] = total[k * 8 : k * 8 + 8]
    copies = [send(part_p.at[lax.rem(j + k, NJ)], in_pj.at[j], at_j(k)) for k in range(1, NJ)]
    in_pj[j] = part_p[j]

    @pl.loop(0, DOUT // TILE)
    def _(t):
        cols = pl.ds(pl.multiple_of(t * TILE, TILE), TILE)
        acc[:, cols] = ev[:, cols].astype(F32) + mm(xv[z], dyg[z, :, cols], TN)

    bulk_forward(0)
    receive(copies)
    in_py[y] = sum(in_pj[k] for k in range(1, NJ)) + in_pj[0]
    copies = [send(in_py.at[y], in_py.at[y], at_y(k)) for k in range(1, NY)]
    bulk_forward(1)
    receive(copies)
    all_p[j] = sum(in_py[k] for k in range(1, NY)) + in_py[0]
    copies = [send(all_p.at[j], all_p.at[j], at_j(k)) for k in range(1, NJ)]
    bulk_forward(2)
    receive(copies)
    p_sum = all_p[...].reshape(RANK, FEAT)
    p_twice = jnp.concatenate([p_sum, p_sum], axis=0)

    in_g[z] = mm(all_p[j], p_twice, NT, HIGHEST)
    copies = [send(in_g.at[z], in_g.at[z], at_z(k)) for k in range(1, NZ)]
    bulk_forward(3)
    add_grad(lax.rem(z + NZ - 1, NZ))
    add_grad(lax.rem(z + 1, NZ))
    receive(copies)
    all_g[j] = sum(in_g[k] for k in range(1, NZ)) + in_g[0]
    copies = [send(all_g.at[j], all_g.at[j], at_j(k)) for k in range(1, NJ)]
    bulk_forward(4)
    receive(copies)
    steps = {20: 5, 40: 6}
    between = lambda k: bulk_forward(steps[k]) if k in steps else None
    inverse = inverse_factor(all_g[...].reshape(RANK, 2 * RANK), between)
    p_t = mm(inverse, p_twice, NN, HIGHEST)
    p_keep[...] = p_t
    p_store = pltpu.make_async_copy(p_keep, p_out, load_sem.at[4])
    p_store.start()
    p_high, p_low = split_rows(p_t)
    p_halves = jnp.concatenate([p_high, p_low], axis=0)

    far_steps = [k for k in (4, 3, 5, 2, 6, 1, 7) if min(k, NZ - k) > NEAR]
    copies = []
    for k in far_steps:
        block = lax.rem(z + k, NZ)
        part_x[block] = split_lanes(mm(xv[block], p_halves, NT))
        copies.append(send(part_x.at[block], in_x.at[z], at_z(k)))
    bulk_forward(7)
    for hop in range(2, NEAR + 1):
        add_grad(lax.rem(z + NZ - hop, NZ))
        add_grad(lax.rem(z + hop, NZ))
    receive(copies)
    xp = split_lanes(sum(in_x[lax.rem(z + NZ - k, NZ)].astype(F32) for k in far_steps))

    for t in range(DOUT // TILE):
        cols = slice(t * TILE, t * TILE + TILE)
        near_high, near_low = split_rows(acc[:, cols])
        tile = mm(xp, dyg[z, :, cols], TN) + mm(p_halves, near_high, NN)
        tile = tile[:RANK] + tile[RANK:] + mm(p_high, near_low, NN)
        for k in range(8):
            q_part[k // 4, k % 4, :, cols] = tile[k * 8 : k * 8 + 8]
    copy = send(q_part.at[1 - core], in_qc, at_core)
    bulk_forward(8)
    receive([copy])
    for k in range(NX):
        q_core[k] = q_part[core, k] + in_qc[k]
    copies = [send(q_core.at[lax.rem(x + k, NX)], in_qx.at[x], at_x(k)) for k in range(1, NX)]
    in_qx[x] = q_core[x]
    receive(copies)
    rows = (in_qx[0] + in_qx[1]) + (in_qx[2] + in_qx[3])
    for k in range(NY):
        q_y[k] = rows[:, k * 256 : k * 256 + 256]
    copies = [send(q_y.at[lax.rem(y + k, NY)], in_qy.at[y], at_y(k)) for k in range(1, NY)]
    in_qy[y] = q_y[y]
    bulk_forward(9)
    receive(copies)
    in_qz[z] = sum(in_qy[k] for k in range(1, NY)) + in_qy[0]
    copies = [send(in_qz.at[z], in_qz.at[z], at_z(k)) for k in range(1, NZ)]
    bulk_forward(10)
    bulk_forward(11)
    receive(copies)
    all_qy[y] = sum(in_qz[k] for k in range(1, NZ)) + in_qz[0]
    copies = [send(all_qy.at[y], all_qy.at[y], at_y(k)) for k in range(1, NY)]
    for hop in range(NEAR + 1, 4):
        add_grad(lax.rem(z + NZ - hop, NZ))
        add_grad(lax.rem(z + hop, NZ))
    receive(copies)
    mine = core * NX + x
    for k in range(NY):
        all_q[mine, :, k * 256 : k * 256 + 256] = all_qy[k]
    copies = [send(all_q.at[mine], all_q.at[mine], at_x(k)) for k in range(1, NX)]
    across = [send(all_q.at[mine], all_q.at[mine], at_core)]
    for k, copy in enumerate(copies):
        copy.wait_recv()
        slot = core * NX + lax.rem(x - (k + 1) + NX, NX)
        across.append(send(all_q.at[slot], all_q.at[slot], at_core))
    bulk_forward(12)
    bulk_forward(13)
    add_grad(lax.rem(z + 4, NZ))
    receive(across)
    q_store = pltpu.make_async_copy(all_q, q_out, load_sem.at[5])
    q_store.start()
    p_cat = jnp.concatenate([p_high, p_high, p_low], axis=0)
    stores = []
    for t in range(DOUT // TILE):
        cols = slice(t * TILE, t * TILE + TILE)
        q_high, q_low = split_rows(all_q[:, :, cols].reshape(RANK, TILE))
        approx = mm(p_cat, jnp.concatenate([q_high, q_low, q_high], axis=0), TN)
        err_v[:, cols] = (acc[:, cols] - approx).astype(BF16)
        store = pltpu.make_async_copy(err_v.at[:, cols], err_out.at[:, cols], load_sem.at[6 + t])
        store.start()
        stores.append(store)
    for way in (1, -1):
        for piece in flows[way][-2:]:
            bulk[(way, *piece)].wait_send()
    receive([])
    p_store.wait()
    q_store.wait()
    for store in stores:
        store.wait()


def local(x_input, dy_grad, error_in, q_init):
    anywhere = pl.BlockSpec(memory_space=pl.ANY)
    vmem = lambda *shape, dtype=F32: pltpu.VMEM(shape, dtype)
    p_t, q_t, err = pl.pallas_call(
        kernel,
        out_shape=(
            jax.ShapeDtypeStruct((RANK, FEAT), F32),
            jax.ShapeDtypeStruct((8, 8, DOUT), F32),
            jax.ShapeDtypeStruct((FEAT, DOUT), BF16),
        ),
        in_specs=[pl.BlockSpec(memory_space=pltpu.HBM)] * 4,
        out_specs=(anywhere,) * 3,
        scratch_shapes=[
            vmem(NZ, TOK, DOUT, dtype=BF16),
            vmem(NZ, TOK, FEAT, dtype=BF16),
            vmem(FEAT, DOUT, dtype=BF16),
            vmem(RANK, DOUT),
            vmem(NZ, TOK, 2 * RANK, dtype=BF16),
            vmem(FEAT, DOUT),
            vmem(NJ, 8, FEAT), vmem(NJ, 8, FEAT), vmem(NY, 8, FEAT), vmem(NJ, 8, FEAT),
            vmem(NZ, 8, 2 * RANK), vmem(NJ, 8, 2 * RANK),
            vmem(NZ, TOK, 2 * RANK, dtype=BF16), vmem(NZ, TOK, 2 * RANK, dtype=BF16),
            vmem(2, NX, 8, DOUT), vmem(NX, 8, DOUT), vmem(NX, 8, DOUT), vmem(NX, 8, DOUT),
            vmem(NY, 8, FEAT), vmem(NY, 8, FEAT), vmem(NZ, 8, FEAT), vmem(NY, 8, FEAT),
            vmem(8, 8, DOUT),
            vmem(RANK, FEAT),
            vmem(FEAT, DOUT, dtype=BF16),
            pltpu.SemaphoreType.DMA((N_SEMS,)),
            pltpu.SemaphoreType.DMA((N_SEMS,)),
            pltpu.SemaphoreType.DMA((10,)),
        ],
        compiler_params=pltpu.CompilerParams(
            collective_id=0, has_side_effects=True, vmem_limit_bytes=48 * 1024 * 1024
        ),
        cost_estimate=pl.CostEstimate(flops=2 * 10**9, bytes_accessed=6 * 10**6, transcendentals=0),
    )(*(pltpu.with_memory_space_constraint(v, pltpu.HBM) for v in (x_input.reshape(NZ, TOK, FEAT), dy_grad[0], error_in[0], q_init.T)))
    return p_t.T, q_t.reshape(RANK, DOUT).T, err[None]


def solution(mesh):
    in_specs = (P("dp", None, "mp"), P("dp", "mp", None), P("dp", "mp", None), P())
    out_specs = (P("mp", None), P(), P("dp", "mp", None))
    return jax.shard_map(local, mesh=mesh, in_specs=in_specs, out_specs=out_specs, check_vma=False)
```

```python
import jax
import jax.numpy as jnp
from jax import lax
from jax.experimental import pallas as pl
from jax.experimental.pallas import tpu as pltpu
from jax.sharding import PartitionSpec as P

F32, BF16 = jnp.float32, jnp.bfloat16
HIGHEST = lax.Precision.HIGHEST
NZ, NY, NX = 8, 8, 4
NJ = 2 * NX
TOK, FEAT, DOUT, RANK = 192, 256, 2048, 64
CHUNKS = 4
PIECE = TOK // CHUNKS
TILE = 512
PIVOTS = 4
N_SEMS = 128
NEAR = 2

NN = (((1,), (0,)), ((), ()))
NT = (((1,), (1,)), ((), ()))
TN = (((0,), (0,)), ((), ()))


def mm(a, b, dims, precision=None):
    return lax.dot_general(a, b, dims, precision=precision, preferred_element_type=F32)


def split_rows(v):
    high = v.astype(BF16)
    low = (v - high.astype(F32)).astype(BF16)
    return high, low


def split_lanes(v):
    both = v + pltpu.roll(v, RANK, axis=1)
    high = both.astype(BF16).astype(F32)
    lane = lax.broadcasted_iota(jnp.int32, both.shape, 1)
    return jnp.where(lane < RANK, high, both - high).astype(BF16)


def inverse_factor(gram2, between):
    lane = lax.broadcasted_iota(jnp.int32, gram2.shape, 1)
    row = lax.broadcasted_iota(jnp.int32, gram2.shape, 0)
    rows = lax.broadcasted_iota(jnp.int32, (RANK, 1), 0)
    a = jnp.where(lane < RANK, gram2, jnp.where(lane - RANK == row, 1.0, 0.0))
    for k in range(0, RANK, PIVOTS):
        columns = [jnp.broadcast_to(a[:, k + i : k + i + 1], a.shape) for i in range(PIVOTS)]
        lines = [a[k + i : k + i + 1, :] for i in range(PIVOTS)]
        for i in range(PIVOTS):
            here = slice(k + i, k + i + 1)
            factor = jnp.where(rows > k + i, columns[i] * (1.0 / columns[i][here]), 0.0)
            for later in range(i + 1, PIVOTS):
                columns[later] = columns[later] - factor * columns[later][here]
                lines[later] = lines[later] - factor[k + later : k + later + 1] * lines[i]
            a = a - factor * lines[i]
        between(k)
    diagonal = jnp.sum(jnp.where(lane == row, a, 0.0), axis=1, keepdims=True)
    root = lax.rsqrt(diagonal)
    root = root * (1.5 - 0.5 * (diagonal * root) * root)
    return jnp.where(lane < RANK, 0.0, a * root)


def kernel(
    x_ref, dy_ref, e_ref, q_ref, p_out, q_out, err_out,
    dyg, xv, ev, qv, yq, acc, part_p, in_pj, in_py, all_p, in_g, all_g, part_x, in_x,
    q_part, in_qc, q_core, in_qx, q_y, in_qy, in_qz, all_qy, all_q, p_keep, err_v,
    send_sem, recv_sem, load_sem,
):
    dp, z = lax.axis_index("dp"), lax.axis_index("mp")
    y, j = lax.div(dp, NJ), lax.rem(dp, NJ)
    x, core = lax.div(j, 2), lax.rem(j, 2)
    counter = iter(range(N_SEMS))
    unsent = []

    at_z = lambda k: (dp, lax.rem(z + k + NZ, NZ))
    at_y = lambda k: (lax.rem(y + k, NY) * NJ + j, z)
    at_j = lambda k: (y * NJ + lax.rem(j + k, NJ), z)
    at_x = lambda k: (y * NJ + lax.rem(x + k, NX) * 2 + core, z)
    at_core = (y * NJ + x * 2 + 1 - core, z)

    def send(src, dst, device):
        n = next(counter)
        copy = pltpu.make_async_remote_copy(
            src_ref=src, dst_ref=dst, send_sem=send_sem.at[n], recv_sem=recv_sem.at[n],
            device_id=device, device_id_type=pl.DeviceIdType.MESH,
        )
        copy.start()
        unsent.append(copy)
        return copy

    def receive(copies):
        while len(unsent) > len(copies):
            unsent.pop(0).wait_send()
        for copy in copies:
            copy.wait_recv()

    loads = [
        pltpu.make_async_copy(src, dst, load_sem.at[n])
        for n, (src, dst) in enumerate(((dy_ref, dyg.at[z]), (q_ref, qv), (x_ref, xv), (e_ref, ev)))
    ]
    for load in loads:
        load.start()

    barrier = pltpu.get_barrier_semaphore()
    peers = [at_z(k) for k in range(1, NZ)] + [at_y(k) for k in range(1, NY)] + [at_j(k) for k in range(1, NJ)]
    for peer in peers:
        pl.semaphore_signal(barrier, inc=1, device_id=peer, device_id_type=pl.DeviceIdType.MESH)

    pl.semaphore_wait(barrier, len(peers))

    flows = {
        1: [(h, c) for h in (1, 2, 3) for c in range(CHUNKS)] + [(4, 0), (4, 1)],
        -1: [(h, c) for h in (1, 2, 3) for c in range(CHUNKS)] + [(4, 2), (4, 3)],
    }
    bulk = {}

    def bulk_send(way, hop, c):
        block = lax.rem(z - way * (hop - 1) + NZ, NZ)
        ref = dyg.at[block, pl.ds(c * PIECE, PIECE)]
        source = dy_ref.at[pl.ds(c * PIECE, PIECE)] if hop == 1 else ref
        bulk[way, hop, c] = send(source, ref, at_z(way))
        unsent.pop()

    def bulk_forward(n):
        for way in (1, -1):
            hop, c = flows[way][n]
            bulk[way, hop, c].wait_recv()
            if (hop + 1, c) in flows[way]:
                bulk_send(way, hop + 1, c)
            if n >= 2:
                bulk[(way, *flows[way][n - 2])].wait_send()

    def add_grad(block):
        @pl.loop(0, DOUT // TILE)
        def _(t):
            cols = pl.ds(pl.multiple_of(t * TILE, TILE), TILE)
            acc[:, cols] += mm(xv[block], dyg[block, :, cols], TN)

    bulk_send(1, 1, 0)
    bulk_send(-1, 1, 0)
    loads[0].wait()
    loads[1].wait()
    q_halves = jnp.concatenate(split_rows(qv[...]), axis=0)
    yq[z] = split_lanes(mm(dyg[z], q_halves, NT))
    right = send(yq.at[z], yq.at[z], at_z(1))
    left = send(yq.at[z], yq.at[z], at_z(-1))
    bulk_send(1, 1, 1)
    bulk_send(-1, 1, 1)
    loads[2].wait()
    loads[3].wait()
    total = mm(q_halves, ev[...], NT) + mm(yq[z], xv[z], TN)
    for hop in (1, 2, 3, 4):
        from_left, from_right = lax.rem(z - hop + NZ, NZ), lax.rem(z + hop, NZ)
        right.wait_recv()
        if hop < 4:
            right = send(yq.at[from_left], yq.at[from_left], at_z(1))
            left.wait_recv()
            if hop < 3:
                left = send(yq.at[from_right], yq.at[from_right], at_z(-1))
            if hop > 1:
                bulk_send(1, 1, hop)
                bulk_send(-1, 1, hop)
            total += mm(yq[from_right], xv[from_right], TN)
        total += mm(yq[from_left], xv[from_left], TN)
    total = total[:RANK] + total[RANK:]

    for k in range(NJ):
        part_p[k] = total[k * 8 : k * 8 + 8]
    copies = [send(part_p.at[lax.rem(j + k, NJ)], in_pj.at[j], at_j(k)) for k in range(1, NJ)]
    in_pj[j] = part_p[j]

    @pl.loop(0, DOUT // TILE)
    def _(t):
        cols = pl.ds(pl.multiple_of(t * TILE, TILE), TILE)
        acc[:, cols] = ev[:, cols].astype(F32) + mm(xv[z], dyg[z, :, cols], TN)

    bulk_forward(0)
    receive(copies)
    in_py[y] = sum(in_pj[k] for k in range(1, NJ)) + in_pj[0]
    copies = [send(in_py.at[y], in_py.at[y], at_y(k)) for k in range(1, NY)]
    bulk_forward(1)
    receive(copies)
    all_p[j] = sum(in_py[k] for k in range(1, NY)) + in_py[0]
    copies = [send(all_p.at[j], all_p.at[j], at_j(k)) for k in range(1, NJ)]
    bulk_forward(2)
    receive(copies)
    p_sum = all_p[...].reshape(RANK, FEAT)
    p_twice = jnp.concatenate([p_sum, p_sum], axis=0)

    in_g[z] = mm(all_p[j], p_twice, NT, HIGHEST)
    copies = [send(in_g.at[z], in_g.at[z], at_z(k)) for k in range(1, NZ)]
    bulk_forward(3)
    receive(copies)
    all_g[j] = sum(in_g[k] for k in range(1, NZ)) + in_g[0]
    copies = [send(all_g.at[j], all_g.at[j], at_j(k)) for k in range(1, NJ)]
    bulk_forward(4)
    receive(copies)
    steps = {32: 5}
    between = lambda k: bulk_forward(steps[k]) if k in steps else None
    inverse = inverse_factor(all_g[...].reshape(RANK, 2 * RANK), between)
    p_t = mm(inverse, p_twice, NN, HIGHEST)
    p_keep[...] = p_t
    p_store = pltpu.make_async_copy(p_keep, p_out, load_sem.at[4])
    p_store.start()
    p_high, p_low = split_rows(p_t)
    p_halves = jnp.concatenate([p_high, p_low], axis=0)

    far_steps = [k for k in (4, 3, 5, 2, 6, 1, 7) if min(k, NZ - k) > NEAR]
    copies = []
    for k in far_steps:
        block = lax.rem(z + k, NZ)
        part_x[block] = split_lanes(mm(xv[block], p_halves, NT))
        copies.append(send(part_x.at[block], in_x.at[z], at_z(k)))
    bulk_forward(6)
    bulk_forward(7)
    for hop in range(1, NEAR + 1):
        add_grad(lax.rem(z + NZ - hop, NZ))
        add_grad(lax.rem(z + hop, NZ))
    receive(copies)
    xp = split_lanes(sum(in_x[lax.rem(z + NZ - k, NZ)].astype(F32) for k in far_steps))

    for t in range(DOUT // TILE):
        cols = slice(t * TILE, t * TILE + TILE)
        near_high, near_low = split_rows(acc[:, cols])
        tile = mm(xp, dyg[z, :, cols], TN) + mm(p_halves, near_high, NN)
        tile = tile[:RANK] + tile[RANK:] + mm(p_high, near_low, NN)
        for k in range(8):
            q_part[k // 4, k % 4, :, cols] = tile[k * 8 : k * 8 + 8]
    copy = send(q_part.at[1 - core], in_qc, at_core)
    bulk_forward(8)
    receive([copy])
    for k in range(NX):
        q_core[k] = q_part[core, k] + in_qc[k]
    copies = [send(q_core.at[lax.rem(x + k, NX)], in_qx.at[x], at_x(k)) for k in range(1, NX)]
    in_qx[x] = q_core[x]
    receive(copies)
    rows = (in_qx[0] + in_qx[1]) + (in_qx[2] + in_qx[3])
    for k in range(NY):
        q_y[k] = rows[:, k * 256 : k * 256 + 256]
    copies = [send(q_y.at[lax.rem(y + k, NY)], in_qy.at[y], at_y(k)) for k in range(1, NY)]
    in_qy[y] = q_y[y]
    bulk_forward(9)
    receive(copies)
    in_qz[z] = sum(in_qy[k] for k in range(1, NY)) + in_qy[0]
    copies = [send(in_qz.at[z], in_qz.at[z], at_z(k)) for k in range(1, NZ)]
    bulk_forward(10)
    receive(copies)
    all_qy[y] = sum(in_qz[k] for k in range(1, NZ)) + in_qz[0]
    copies = [send(all_qy.at[y], all_qy.at[y], at_y(k)) for k in range(1, NY)]
    receive(copies)
    mine = core * NX + x
    for k in range(NY):
        all_q[mine, :, k * 256 : k * 256 + 256] = all_qy[k]
    copies = [send(all_q.at[mine], all_q.at[mine], at_x(k)) for k in range(1, NX)]
    across = [send(all_q.at[mine], all_q.at[mine], at_core)]
    for k, copy in enumerate(copies):
        copy.wait_recv()
        slot = core * NX + lax.rem(x - (k + 1) + NX, NX)
        across.append(send(all_q.at[slot], all_q.at[slot], at_core))
    bulk_forward(11)
    for hop in range(NEAR + 1, 4):
        add_grad(lax.rem(z + NZ - hop, NZ))
        add_grad(lax.rem(z + hop, NZ))
    bulk_forward(12)
    bulk_forward(13)
    add_grad(lax.rem(z + 4, NZ))
    receive(across)
    q_store = pltpu.make_async_copy(all_q, q_out, load_sem.at[5])
    q_store.start()
    p_cat = jnp.concatenate([p_high, p_high, p_low], axis=0)
    stores = []
    for t in range(DOUT // TILE):
        cols = slice(t * TILE, t * TILE + TILE)
        q_high, q_low = split_rows(all_q[:, :, cols].reshape(RANK, TILE))
        approx = mm(p_cat, jnp.concatenate([q_high, q_low, q_high], axis=0), TN)
        err_v[:, cols] = (acc[:, cols] - approx).astype(BF16)
        store = pltpu.make_async_copy(err_v.at[:, cols], err_out.at[:, cols], load_sem.at[6 + t])
        store.start()
        stores.append(store)
    for way in (1, -1):
        for piece in flows[way][-2:]:
            bulk[(way, *piece)].wait_send()
    receive([])
    p_store.wait()
    q_store.wait()
    for store in stores:
        store.wait()


def local(x_input, dy_grad, error_in, q_init):
    anywhere = pl.BlockSpec(memory_space=pl.ANY)
    vmem = lambda *shape, dtype=F32: pltpu.VMEM(shape, dtype)
    p_t, q_t, err = pl.pallas_call(
        kernel,
        out_shape=(
            jax.ShapeDtypeStruct((RANK, FEAT), F32),
            jax.ShapeDtypeStruct((8, 8, DOUT), F32),
            jax.ShapeDtypeStruct((FEAT, DOUT), BF16),
        ),
        in_specs=[pl.BlockSpec(memory_space=pltpu.HBM)] * 4,
        out_specs=(anywhere,) * 3,
        scratch_shapes=[
            vmem(NZ, TOK, DOUT, dtype=BF16),
            vmem(NZ, TOK, FEAT, dtype=BF16),
            vmem(FEAT, DOUT, dtype=BF16),
            vmem(RANK, DOUT),
            vmem(NZ, TOK, 2 * RANK, dtype=BF16),
            vmem(FEAT, DOUT),
            vmem(NJ, 8, FEAT), vmem(NJ, 8, FEAT), vmem(NY, 8, FEAT), vmem(NJ, 8, FEAT),
            vmem(NZ, 8, 2 * RANK), vmem(NJ, 8, 2 * RANK),
            vmem(NZ, TOK, 2 * RANK, dtype=BF16), vmem(NZ, TOK, 2 * RANK, dtype=BF16),
            vmem(2, NX, 8, DOUT), vmem(NX, 8, DOUT), vmem(NX, 8, DOUT), vmem(NX, 8, DOUT),
            vmem(NY, 8, FEAT), vmem(NY, 8, FEAT), vmem(NZ, 8, FEAT), vmem(NY, 8, FEAT),
            vmem(8, 8, DOUT),
            vmem(RANK, FEAT),
            vmem(FEAT, DOUT, dtype=BF16),
            pltpu.SemaphoreType.DMA((N_SEMS,)),
            pltpu.SemaphoreType.DMA((N_SEMS,)),
            pltpu.SemaphoreType.DMA((10,)),
        ],
        compiler_params=pltpu.CompilerParams(
            collective_id=0, has_side_effects=True, vmem_limit_bytes=48 * 1024 * 1024
        ),
        cost_estimate=pl.CostEstimate(flops=2 * 10**9, bytes_accessed=6 * 10**6, transcendentals=0),
    )(*(pltpu.with_memory_space_constraint(v, pltpu.HBM) for v in (x_input.reshape(NZ, TOK, FEAT), dy_grad[0], error_in[0], q_init.T)))
    return p_t.T, q_t.reshape(RANK, DOUT).T, err[None]


def solution(mesh):
    in_specs = (P("dp", None, "mp"), P("dp", "mp", None), P("dp", "mp", None), P())
    out_specs = (P("mp", None), P(), P("dp", "mp", None))
    return jax.shard_map(local, mesh=mesh, in_specs=in_specs, out_specs=out_specs, check_vma=False)
```

```python
import jax
import jax.numpy as jnp
from jax import lax
from jax.experimental import pallas as pl
from jax.experimental.pallas import tpu as pltpu
from jax.sharding import PartitionSpec as P

F32, BF16 = jnp.float32, jnp.bfloat16
HIGHEST = lax.Precision.HIGHEST
NZ, NY, NX = 8, 8, 4
NJ = 2 * NX
TOK, FEAT, DOUT, RANK = 192, 256, 2048, 64
CHUNKS = 4
PIECE = TOK // CHUNKS
TILE = 512
PIVOTS = 4
N_SEMS = 128
NEAR = 2

NN = (((1,), (0,)), ((), ()))
NT = (((1,), (1,)), ((), ()))
TN = (((0,), (0,)), ((), ()))


def mm(a, b, dims, precision=None):
    return lax.dot_general(a, b, dims, precision=precision, preferred_element_type=F32)


def split_rows(v):
    high = v.astype(BF16)
    low = (v - high.astype(F32)).astype(BF16)
    return high, low


def split_lanes(v):
    both = v + pltpu.roll(v, RANK, axis=1)
    high = both.astype(BF16).astype(F32)
    lane = lax.broadcasted_iota(jnp.int32, both.shape, 1)
    return jnp.where(lane < RANK, high, both - high).astype(BF16)


def inverse_factor(gram2, between):
    lane = lax.broadcasted_iota(jnp.int32, gram2.shape, 1)
    row = lax.broadcasted_iota(jnp.int32, gram2.shape, 0)
    rows = lax.broadcasted_iota(jnp.int32, (RANK, 1), 0)
    a = jnp.where(lane < RANK, gram2, jnp.where(lane - RANK == row, 1.0, 0.0))
    for k in range(0, RANK, PIVOTS):
        columns = [jnp.broadcast_to(a[:, k + i : k + i + 1], a.shape) for i in range(PIVOTS)]
        lines = [a[k + i : k + i + 1, :] for i in range(PIVOTS)]
        for i in range(PIVOTS):
            here = slice(k + i, k + i + 1)
            factor = jnp.where(rows > k + i, columns[i] * (1.0 / columns[i][here]), 0.0)
            for later in range(i + 1, PIVOTS):
                columns[later] = columns[later] - factor * columns[later][here]
                lines[later] = lines[later] - factor[k + later : k + later + 1] * lines[i]
            a = a - factor * lines[i]
        between(k)
    diagonal = jnp.sum(jnp.where(lane == row, a, 0.0), axis=1, keepdims=True)
    root = lax.rsqrt(diagonal)
    root = root * (1.5 - 0.5 * (diagonal * root) * root)
    return jnp.where(lane < RANK, 0.0, a * root)


def kernel(
    x_ref, dy_ref, e_ref, q_ref, p_out, q_out, err_out,
    dyg, xv, ev, qv, yq, acc, part_p, in_pj, in_py, all_p, in_g, all_g, part_x, in_x,
    q_part, in_qc, q_core, in_qx, q_y, in_qy, in_qz, all_qy, all_q, p_keep,
    send_sem, recv_sem, load_sem,
):
    dp, z = lax.axis_index("dp"), lax.axis_index("mp")
    y, j = lax.div(dp, NJ), lax.rem(dp, NJ)
    x, core = lax.div(j, 2), lax.rem(j, 2)
    counter = iter(range(N_SEMS))
    unsent = []

    at_z = lambda k: (dp, lax.rem(z + k + NZ, NZ))
    at_y = lambda k: (lax.rem(y + k, NY) * NJ + j, z)
    at_j = lambda k: (y * NJ + lax.rem(j + k, NJ), z)
    at_x = lambda k: (y * NJ + lax.rem(x + k, NX) * 2 + core, z)
    at_core = (y * NJ + x * 2 + 1 - core, z)

    def send(src, dst, device):
        n = next(counter)
        copy = pltpu.make_async_remote_copy(
            src_ref=src, dst_ref=dst, send_sem=send_sem.at[n], recv_sem=recv_sem.at[n],
            device_id=device, device_id_type=pl.DeviceIdType.MESH,
        )
        copy.start()
        unsent.append(copy)
        return copy

    def receive(copies):
        while len(unsent) > len(copies):
            unsent.pop(0).wait_send()
        for copy in copies:
            copy.wait_recv()

    loads = [
        pltpu.make_async_copy(src, dst, load_sem.at[n])
        for n, (src, dst) in enumerate(((dy_ref, dyg.at[z]), (q_ref, qv), (x_ref, xv), (e_ref, ev)))
    ]
    for load in loads:
        load.start()

    barrier = pltpu.get_barrier_semaphore()
    peers = [at_z(k) for k in range(1, NZ)] + [at_y(k) for k in range(1, NY)] + [at_j(k) for k in range(1, NJ)]
    for peer in peers:
        pl.semaphore_signal(barrier, inc=1, device_id=peer, device_id_type=pl.DeviceIdType.MESH)

    pl.semaphore_wait(barrier, len(peers))

    flows = {
        1: [(h, c) for h in (1, 2, 3) for c in range(CHUNKS)] + [(4, 0), (4, 1)],
        -1: [(h, c) for h in (1, 2, 3) for c in (2, 3, 0, 1)] + [(4, 2), (4, 3)],
    }
    bulk = {}

    def bulk_send(way, hop, c):
        block = lax.rem(z - way * (hop - 1) + NZ, NZ)
        ref = dyg.at[block, pl.ds(c * PIECE, PIECE)]
        source = dy_ref.at[pl.ds(c * PIECE, PIECE)] if hop == 1 else ref
        bulk[way, hop, c] = send(source, ref, at_z(way))
        unsent.pop()

    def first_sends(n):
        for way in (1, -1):
            bulk_send(way, *flows[way][n])

    def bulk_forward(n):
        for way in (1, -1):
            hop, c = flows[way][n]
            bulk[way, hop, c].wait_recv()
            if (hop + 1, c) in flows[way]:
                bulk_send(way, hop + 1, c)
            if n >= 2:
                bulk[(way, *flows[way][n - 2])].wait_send()

    def add_grad(block):
        @pl.loop(0, DOUT // TILE)
        def _(t):
            cols = pl.ds(pl.multiple_of(t * TILE, TILE), TILE)
            acc[:, cols] += mm(xv[block], dyg[block, :, cols], TN)

    first_sends(0)
    loads[0].wait()
    loads[1].wait()
    q_halves = jnp.concatenate(split_rows(qv[...]), axis=0)
    yq[z] = split_lanes(mm(dyg[z], q_halves, NT))
    right = send(yq.at[z], yq.at[z], at_z(1))
    left = send(yq.at[z], yq.at[z], at_z(-1))
    first_sends(1)
    loads[2].wait()
    loads[3].wait()
    total = mm(q_halves, ev[...], NT) + mm(yq[z], xv[z], TN)
    for hop in (1, 2, 3, 4):
        from_left, from_right = lax.rem(z - hop + NZ, NZ), lax.rem(z + hop, NZ)
        right.wait_recv()
        if hop < 4:
            right = send(yq.at[from_left], yq.at[from_left], at_z(1))
            left.wait_recv()
            if hop < 3:
                left = send(yq.at[from_right], yq.at[from_right], at_z(-1))
            if hop > 1:
                first_sends(hop)
            total += mm(yq[from_right], xv[from_right], TN)
        total += mm(yq[from_left], xv[from_left], TN)
    total = total[:RANK] + total[RANK:]

    for k in range(NJ):
        part_p[k] = total[k * 8 : k * 8 + 8]
    copies = [send(part_p.at[lax.rem(j + k, NJ)], in_pj.at[j], at_j(k)) for k in range(1, NJ)]
    in_pj[j] = part_p[j]

    @pl.loop(0, DOUT // TILE)
    def _(t):
        cols = pl.ds(pl.multiple_of(t * TILE, TILE), TILE)
        acc[:, cols] = ev[:, cols].astype(F32) + mm(xv[z], dyg[z, :, cols], TN)

    bulk_forward(0)
    receive(copies)
    in_py[y] = sum(in_pj[k] for k in range(1, NJ)) + in_pj[0]
    copies = [send(in_py.at[y], in_py.at[y], at_y(k)) for k in range(1, NY)]
    bulk_forward(1)
    receive(copies)
    all_p[j] = sum(in_py[k] for k in range(1, NY)) + in_py[0]
    copies = [send(all_p.at[j], all_p.at[j], at_j(k)) for k in range(1, NJ)]
    bulk_forward(2)
    receive(copies)
    p_sum = all_p[...].reshape(RANK, FEAT)
    p_twice = jnp.concatenate([p_sum, p_sum], axis=0)

    in_g[z] = mm(all_p[j], p_twice, NT, HIGHEST)
    copies = [send(in_g.at[z], in_g.at[z], at_z(k)) for k in range(1, NZ)]
    bulk_forward(3)
    receive(copies)
    all_g[j] = sum(in_g[k] for k in range(1, NZ)) + in_g[0]
    copies = [send(all_g.at[j], all_g.at[j], at_j(k)) for k in range(1, NJ)]
    bulk_forward(4)
    receive(copies)
    steps = {32: 5}
    between = lambda k: bulk_forward(steps[k]) if k in steps else None
    inverse = inverse_factor(all_g[...].reshape(RANK, 2 * RANK), between)
    p_t = mm(inverse, p_twice, NN, HIGHEST)
    p_keep[...] = p_t
    p_store = pltpu.make_async_copy(p_keep, p_out, load_sem.at[4])
    p_store.start()
    p_high, p_low = split_rows(p_t)
    p_halves = jnp.concatenate([p_high, p_low], axis=0)

    far_steps = [k for k in (4, 3, 5, 2, 6, 1, 7) if min(k, NZ - k) > NEAR]
    copies = []
    for k in far_steps:
        block = lax.rem(z + k, NZ)
        part_x[block] = split_lanes(mm(xv[block], p_halves, NT))
        copies.append(send(part_x.at[block], in_x.at[z], at_z(k)))
    bulk_forward(6)
    bulk_forward(7)
    for hop in range(1, NEAR + 1):
        add_grad(lax.rem(z + NZ - hop, NZ))
        add_grad(lax.rem(z + hop, NZ))
    receive(copies)
    xp = split_lanes(sum(in_x[lax.rem(z + NZ - k, NZ)].astype(F32) for k in far_steps))

    for t in range(DOUT // TILE):
        cols = slice(t * TILE, t * TILE + TILE)
        near_high, near_low = split_rows(acc[:, cols])
        tile = mm(xp, dyg[z, :, cols], TN) + mm(p_halves, near_high, NN)
        tile = tile[:RANK] + tile[RANK:] + mm(p_high, near_low, NN)
        for k in range(8):
            q_part[k // 4, k % 4, :, cols] = tile[k * 8 : k * 8 + 8]
    copy = send(q_part.at[1 - core], in_qc, at_core)
    bulk_forward(8)
    receive([copy])
    for k in range(NX):
        q_core[k] = q_part[core, k] + in_qc[k]
    copies = [send(q_core.at[lax.rem(x + k, NX)], in_qx.at[x], at_x(k)) for k in range(1, NX)]
    in_qx[x] = q_core[x]
    bulk_forward(9)
    receive(copies)
    rows = (in_qx[0] + in_qx[1]) + (in_qx[2] + in_qx[3])
    for k in range(NY):
        q_y[k] = rows[:, k * 256 : k * 256 + 256]
    copies = [send(q_y.at[lax.rem(y + k, NY)], in_qy.at[y], at_y(k)) for k in range(1, NY)]
    in_qy[y] = q_y[y]
    receive(copies)
    in_qz[z] = sum(in_qy[k] for k in range(1, NY)) + in_qy[0]
    copies = [send(in_qz.at[z], in_qz.at[z], at_z(k)) for k in range(1, NZ)]
    receive(copies)
    all_qy[y] = sum(in_qz[k] for k in range(1, NZ)) + in_qz[0]
    copies = [send(all_qy.at[y], all_qy.at[y], at_y(k)) for k in range(1, NY)]
    receive(copies)
    mine = core * NX + x
    for k in range(NY):
        all_q[mine, :, k * 256 : k * 256 + 256] = all_qy[k]
    copies = [send(all_q.at[mine], all_q.at[mine], at_x(k)) for k in range(1, NX)]
    across = [send(all_q.at[mine], all_q.at[mine], at_core)]
    for k, copy in enumerate(copies):
        copy.wait_recv()
        slot = core * NX + lax.rem(x - (k + 1) + NX, NX)
        across.append(send(all_q.at[slot], all_q.at[slot], at_core))
    receive(across)
    q_store = pltpu.make_async_copy(all_q, q_out, load_sem.at[5])
    q_store.start()
    p_cat = jnp.concatenate([p_high, p_high, p_low], axis=0)

    @pl.loop(0, DOUT // TILE)
    def _(t):
        cols = pl.ds(pl.multiple_of(t * TILE, TILE), TILE)
        q_high, q_low = split_rows(all_q[:, :, cols].reshape(RANK, TILE))
        acc[:, cols] -= mm(p_cat, jnp.concatenate([q_high, q_low, q_high], axis=0), TN)

    bulk_forward(10)
    bulk_forward(11)
    for hop in range(NEAR + 1, 4):
        add_grad(lax.rem(z + NZ - hop, NZ))
        add_grad(lax.rem(z + hop, NZ))
    bulk_forward(12)
    bulk_forward(13)
    far = lax.rem(z + 4, NZ)
    for t in range(DOUT // TILE):
        cols = slice(t * TILE, t * TILE + TILE)
        err_out[:, cols] = (acc[:, cols] + mm(xv[far], dyg[far, :, cols], TN)).astype(BF16)
    for way in (1, -1):
        for piece in flows[way][-2:]:
            bulk[(way, *piece)].wait_send()
    receive([])
    p_store.wait()
    q_store.wait()


def local(x_input, dy_grad, error_in, q_init):
    anywhere = pl.BlockSpec(memory_space=pl.ANY)
    vmem = lambda *shape, dtype=F32: pltpu.VMEM(shape, dtype)
    p_t, q_t, err = pl.pallas_call(
        kernel,
        out_shape=(
            jax.ShapeDtypeStruct((RANK, FEAT), F32),
            jax.ShapeDtypeStruct((8, 8, DOUT), F32),
            jax.ShapeDtypeStruct((FEAT, DOUT), BF16),
        ),
        in_specs=[pl.BlockSpec(memory_space=pltpu.HBM)] * 4,
        out_specs=(anywhere, anywhere, pl.BlockSpec(memory_space=pltpu.VMEM)),
        scratch_shapes=[
            vmem(NZ, TOK, DOUT, dtype=BF16),
            vmem(NZ, TOK, FEAT, dtype=BF16),
            vmem(FEAT, DOUT, dtype=BF16),
            vmem(RANK, DOUT),
            vmem(NZ, TOK, 2 * RANK, dtype=BF16),
            vmem(FEAT, DOUT),
            vmem(NJ, 8, FEAT), vmem(NJ, 8, FEAT), vmem(NY, 8, FEAT), vmem(NJ, 8, FEAT),
            vmem(NZ, 8, 2 * RANK), vmem(NJ, 8, 2 * RANK),
            vmem(NZ, TOK, 2 * RANK, dtype=BF16), vmem(NZ, TOK, 2 * RANK, dtype=BF16),
            vmem(2, NX, 8, DOUT), vmem(NX, 8, DOUT), vmem(NX, 8, DOUT), vmem(NX, 8, DOUT),
            vmem(NY, 8, FEAT), vmem(NY, 8, FEAT), vmem(NZ, 8, FEAT), vmem(NY, 8, FEAT),
            vmem(8, 8, DOUT),
            vmem(RANK, FEAT),
            pltpu.SemaphoreType.DMA((N_SEMS,)),
            pltpu.SemaphoreType.DMA((N_SEMS,)),
            pltpu.SemaphoreType.DMA((6,)),
        ],
        compiler_params=pltpu.CompilerParams(
            collective_id=0, has_side_effects=True, vmem_limit_bytes=48 * 1024 * 1024
        ),
        cost_estimate=pl.CostEstimate(flops=2 * 10**9, bytes_accessed=6 * 10**6, transcendentals=0),
    )(*(pltpu.with_memory_space_constraint(v, pltpu.HBM) for v in (x_input.reshape(NZ, TOK, FEAT), dy_grad[0], error_in[0], q_init.T)))
    return p_t.T, q_t.reshape(RANK, DOUT).T, err[None]


def solution(mesh):
    in_specs = (P("dp", None, "mp"), P("dp", "mp", None), P("dp", "mp", None), P())
    out_specs = (P("mp", None), P(), P("dp", "mp", None))
    return jax.shard_map(local, mesh=mesh, in_specs=in_specs, out_specs=out_specs, check_vma=False)
```

```python
import jax
import jax.numpy as jnp
from jax import lax
from jax.experimental import pallas as pl
from jax.experimental.pallas import tpu as pltpu
from jax.sharding import PartitionSpec as P

F32, BF16 = jnp.float32, jnp.bfloat16
HIGHEST = lax.Precision.HIGHEST
NZ, NY, NX = 8, 8, 4
NJ = 2 * NX
TOK, FEAT, DOUT, RANK = 192, 256, 2048, 64
CHUNKS = 4
PIECE = TOK // CHUNKS
TILE = 512
PIVOTS = 4
ORDER = (4, 3, 5, 2, 6, 1, 7)
N_SEMS = 128
NEAR = 2

NN = (((1,), (0,)), ((), ()))
NT = (((1,), (1,)), ((), ()))
TN = (((0,), (0,)), ((), ()))


def mm(a, b, dims, precision=None):
    return lax.dot_general(a, b, dims, precision=precision, preferred_element_type=F32)


def split_rows(v):
    high = v.astype(BF16)
    low = (v - high.astype(F32)).astype(BF16)
    return high, low


def split_lanes(v):
    both = v + pltpu.roll(v, RANK, axis=1)
    high = both.astype(BF16).astype(F32)
    lane = lax.broadcasted_iota(jnp.int32, both.shape, 1)
    return jnp.where(lane < RANK, high, both - high).astype(BF16)


def inverse_factor(gram2, between):
    lane = lax.broadcasted_iota(jnp.int32, gram2.shape, 1)
    row = lax.broadcasted_iota(jnp.int32, gram2.shape, 0)
    rows = lax.broadcasted_iota(jnp.int32, (RANK, 1), 0)
    a = jnp.where(lane < RANK, gram2, jnp.where(lane - RANK == row, 1.0, 0.0))
    for k in range(0, RANK, PIVOTS):
        columns = [jnp.broadcast_to(a[:, k + i : k + i + 1], a.shape) for i in range(PIVOTS)]
        lines = [a[k + i : k + i + 1, :] for i in range(PIVOTS)]
        for i in range(PIVOTS):
            here = slice(k + i, k + i + 1)
            factor = jnp.where(rows > k + i, columns[i] * (1.0 / columns[i][here]), 0.0)
            for later in range(i + 1, PIVOTS):
                columns[later] = columns[later] - factor * columns[later][here]
                lines[later] = lines[later] - factor[k + later : k + later + 1] * lines[i]
            a = a - factor * lines[i]
        between(k)
    diagonal = jnp.sum(jnp.where(lane == row, a, 0.0), axis=1, keepdims=True)
    root = lax.rsqrt(diagonal)
    root = root * (1.5 - 0.5 * (diagonal * root) * root)
    return jnp.where(lane < RANK, 0.0, a * root)


def kernel(
    x_ref, dy_ref, e_ref, q_ref, p_out, q_out, err_out,
    dyg, xv, ev, qv, yq, acc, part_p, in_pj, in_py, all_p, in_g, all_g, part_x, in_x,
    q_part, in_qc, q_core, in_qx, q_y, in_qy, in_qz, all_qy, all_q, p_keep, q_near,
    send_sem, recv_sem, load_sem,
):
    dp, z = lax.axis_index("dp"), lax.axis_index("mp")
    y, j = lax.div(dp, NJ), lax.rem(dp, NJ)
    x, core = lax.div(j, 2), lax.rem(j, 2)
    counter = iter(range(N_SEMS))
    unsent = []

    at_z = lambda k: (dp, lax.rem(z + k + NZ, NZ))
    at_y = lambda k: (lax.rem(y + k, NY) * NJ + j, z)
    at_j = lambda k: (y * NJ + lax.rem(j + k, NJ), z)
    at_x = lambda k: (y * NJ + lax.rem(x + k, NX) * 2 + core, z)
    at_core = (y * NJ + x * 2 + 1 - core, z)

    def send(src, dst, device):
        n = next(counter)
        copy = pltpu.make_async_remote_copy(
            src_ref=src, dst_ref=dst, send_sem=send_sem.at[n], recv_sem=recv_sem.at[n],
            device_id=device, device_id_type=pl.DeviceIdType.MESH,
        )
        copy.start()
        unsent.append(copy)
        return copy

    def receive(copies):
        while len(unsent) > len(copies):
            unsent.pop(0).wait_send()
        for copy in copies:
            copy.wait_recv()

    loads = [
        pltpu.make_async_copy(src, dst, load_sem.at[n])
        for n, (src, dst) in enumerate(((dy_ref, dyg.at[z]), (q_ref, qv), (x_ref, xv), (e_ref, ev)))
    ]
    for load in loads:
        load.start()

    barrier = pltpu.get_barrier_semaphore()
    peers = [at_z(k) for k in range(1, NZ)] + [at_y(k) for k in range(1, NY)] + [at_j(k) for k in range(1, NJ)]
    for peer in peers:
        pl.semaphore_signal(barrier, inc=1, device_id=peer, device_id_type=pl.DeviceIdType.MESH)

    pl.semaphore_wait(barrier, len(peers))

    flows = {
        1: [(h, c) for h in (1, 2, 3) for c in range(CHUNKS)] + [(4, 0), (4, 1)],
        -1: [(h, c) for h in (1, 2, 3) for c in (2, 3, 0, 1)] + [(4, 2), (4, 3)],
    }
    bulk = {}

    def bulk_send(way, hop, c):
        block = lax.rem(z - way * (hop - 1) + NZ, NZ)
        ref = dyg.at[block, pl.ds(c * PIECE, PIECE)]
        source = dy_ref.at[pl.ds(c * PIECE, PIECE)] if hop == 1 else ref
        bulk[way, hop, c] = send(source, ref, at_z(way))
        unsent.pop()

    def first_sends(n):
        for way in (1, -1):
            bulk_send(way, *flows[way][n])

    def bulk_forward(n):
        for way in (1, -1):
            hop, c = flows[way][n]
            bulk[way, hop, c].wait_recv()
            if (hop + 1, c) in flows[way]:
                bulk_send(way, hop + 1, c)
            if n >= 2:
                bulk[(way, *flows[way][n - 2])].wait_send()

    def add_grad(block):
        @pl.loop(0, DOUT // TILE)
        def _(t):
            cols = pl.ds(pl.multiple_of(t * TILE, TILE), TILE)
            acc[:, cols] += mm(xv[block], dyg[block, :, cols], TN)

    first_sends(0)
    loads[0].wait()
    loads[1].wait()
    q_halves = jnp.concatenate(split_rows(qv[...]), axis=0)
    yq[z] = split_lanes(mm(dyg[z], q_halves, NT))
    right = send(yq.at[z], yq.at[z], at_z(1))
    left = send(yq.at[z], yq.at[z], at_z(-1))
    first_sends(1)
    loads[2].wait()
    loads[3].wait()
    total = mm(q_halves, ev[...], NT) + mm(yq[z], xv[z], TN)
    for hop in (1, 2, 3, 4):
        from_left, from_right = lax.rem(z - hop + NZ, NZ), lax.rem(z + hop, NZ)
        right.wait_recv()
        if hop < 4:
            right = send(yq.at[from_left], yq.at[from_left], at_z(1))
            left.wait_recv()
            if hop < 3:
                left = send(yq.at[from_right], yq.at[from_right], at_z(-1))
            if hop > 1:
                first_sends(hop)
            total += mm(yq[from_right], xv[from_right], TN)
        total += mm(yq[from_left], xv[from_left], TN)
    total = total[:RANK] + total[RANK:]

    for k in range(NJ):
        part_p[k] = total[k * 8 : k * 8 + 8]
    copies = [send(part_p.at[lax.rem(j + k, NJ)], in_pj.at[j], at_j(k)) for k in ORDER]
    in_pj[j] = part_p[j]

    @pl.loop(0, DOUT // TILE)
    def _(t):
        cols = pl.ds(pl.multiple_of(t * TILE, TILE), TILE)
        acc[:, cols] = ev[:, cols].astype(F32) + mm(xv[z], dyg[z, :, cols], TN)

    bulk_forward(0)
    receive(copies)
    in_py[y] = sum(in_pj[k] for k in range(1, NJ)) + in_pj[0]
    copies = [send(in_py.at[y], in_py.at[y], at_y(k)) for k in ORDER]
    bulk_forward(1)
    receive(copies)
    all_p[j] = sum(in_py[k] for k in range(1, NY)) + in_py[0]
    copies = [send(all_p.at[j], all_p.at[j], at_j(k)) for k in ORDER]
    bulk_forward(2)
    receive(copies)
    p_sum = all_p[...].reshape(RANK, FEAT)
    p_twice = jnp.concatenate([p_sum, p_sum], axis=0)

    in_g[z] = mm(all_p[j], p_twice, NT, HIGHEST)
    copies = [send(in_g.at[z], in_g.at[z], at_z(k)) for k in ORDER]
    bulk_forward(3)
    add_grad(lax.rem(z + NZ - 1, NZ))
    add_grad(lax.rem(z + 1, NZ))
    receive(copies)
    all_g[j] = sum(in_g[k] for k in range(1, NZ)) + in_g[0]
    copies = [send(all_g.at[j], all_g.at[j], at_j(k)) for k in ORDER]
    bulk_forward(4)
    receive(copies)
    steps = {32: 5}
    between = lambda k: bulk_forward(steps[k]) if k in steps else None
    inverse = inverse_factor(all_g[...].reshape(RANK, 2 * RANK), between)
    p_t = mm(inverse, p_twice, NN, HIGHEST)
    p_keep[...] = p_t
    p_store = pltpu.make_async_copy(p_keep, p_out, load_sem.at[4])
    p_store.start()
    p_high, p_low = split_rows(p_t)
    p_halves = jnp.concatenate([p_high, p_low], axis=0)

    far_steps = [k for k in ORDER if min(k, NZ - k) > NEAR]
    copies = []
    for k in far_steps:
        block = lax.rem(z + k, NZ)
        part_x[block] = split_lanes(mm(xv[block], p_halves, NT))
        copies.append(send(part_x.at[block], in_x.at[z], at_z(k)))
    bulk_forward(6)
    bulk_forward(7)
    for hop in range(2, NEAR + 1):
        add_grad(lax.rem(z + NZ - hop, NZ))
        add_grad(lax.rem(z + hop, NZ))

    @pl.loop(0, DOUT // TILE)
    def _(t):
        cols = pl.ds(pl.multiple_of(t * TILE, TILE), TILE)
        near_high, near_low = split_rows(acc[:, cols])
        tile = mm(p_halves, near_high, NN)
        q_near[:, cols] = tile[:RANK] + tile[RANK:] + mm(p_high, near_low, NN)

    receive(copies)
    xp = split_lanes(sum(in_x[lax.rem(z + NZ - k, NZ)].astype(F32) for k in far_steps))
    copies = []
    for t in range(DOUT // TILE):
        cols = slice(t * TILE, t * TILE + TILE)
        tile = mm(xp, dyg[z, :, cols], TN)
        tile = tile[:RANK] + tile[RANK:] + q_near[:, cols]
        for k in range(8):
            q_part[k // 4, k % 4, :, cols] = tile[k * 8 : k * 8 + 8]
        copies.append(send(q_part.at[1 - core, :, :, cols], in_qc.at[:, :, cols], at_core))
    receive(copies)
    for k in range(NX):
        q_core[k] = q_part[core, k] + in_qc[k]
    copies = [send(q_core.at[lax.rem(x + k, NX)], in_qx.at[x], at_x(k)) for k in range(1, NX)]
    in_qx[x] = q_core[x]
    receive(copies)
    rows = (in_qx[0] + in_qx[1]) + (in_qx[2] + in_qx[3])
    for k in range(NY):
        q_y[k] = rows[:, k * 256 : k * 256 + 256]
    copies = [send(q_y.at[lax.rem(y + k, NY)], in_qy.at[y], at_y(k)) for k in ORDER]
    in_qy[y] = q_y[y]
    bulk_forward(8)
    receive(copies)
    in_qz[z] = sum(in_qy[k] for k in range(1, NY)) + in_qy[0]
    copies = [send(in_qz.at[z], in_qz.at[z], at_z(k)) for k in ORDER]
    bulk_forward(9)
    receive(copies)
    all_qy[y] = sum(in_qz[k] for k in range(1, NZ)) + in_qz[0]
    copies = [send(all_qy.at[y], all_qy.at[y], at_y(k)) for k in ORDER]
    receive(copies)
    mine = core * NX + x
    for k in range(NY):
        all_q[mine, :, k * 256 : k * 256 + 256] = all_qy[k]
    copies = [send(all_q.at[mine], all_q.at[mine], at_x(k)) for k in range(1, NX)]
    across = [send(all_q.at[mine], all_q.at[mine], at_core)]
    for k, copy in enumerate(copies):
        copy.wait_recv()
        slot = core * NX + lax.rem(x - (k + 1) + NX, NX)
        across.append(send(all_q.at[slot], all_q.at[slot], at_core))
    receive(across)
    q_store = pltpu.make_async_copy(all_q, q_out, load_sem.at[5])
    q_store.start()
    p_cat = jnp.concatenate([p_high, p_high, p_low], axis=0)

    @pl.loop(0, DOUT // TILE)
    def _(t):
        cols = pl.ds(pl.multiple_of(t * TILE, TILE), TILE)
        q_high, q_low = split_rows(all_q[:, :, cols].reshape(RANK, TILE))
        acc[:, cols] -= mm(p_cat, jnp.concatenate([q_high, q_low, q_high], axis=0), TN)

    bulk_forward(10)
    bulk_forward(11)
    for hop in range(NEAR + 1, 4):
        add_grad(lax.rem(z + NZ - hop, NZ))
        add_grad(lax.rem(z + hop, NZ))
    bulk_forward(12)
    bulk_forward(13)
    far = lax.rem(z + 4, NZ)
    for t in range(DOUT // TILE):
        cols = slice(t * TILE, t * TILE + TILE)
        err_out[:, cols] = (acc[:, cols] + mm(xv[far], dyg[far, :, cols], TN)).astype(BF16)
    for way in (1, -1):
        for piece in flows[way][-2:]:
            bulk[(way, *piece)].wait_send()
    receive([])
    p_store.wait()
    q_store.wait()


def local(x_input, dy_grad, error_in, q_init):
    anywhere = pl.BlockSpec(memory_space=pl.ANY)
    vmem = lambda *shape, dtype=F32: pltpu.VMEM(shape, dtype)
    p_t, q_t, err = pl.pallas_call(
        kernel,
        out_shape=(
            jax.ShapeDtypeStruct((RANK, FEAT), F32),
            jax.ShapeDtypeStruct((8, 8, DOUT), F32),
            jax.ShapeDtypeStruct((FEAT, DOUT), BF16),
        ),
        in_specs=[pl.BlockSpec(memory_space=pltpu.HBM)] * 4,
        out_specs=(anywhere, anywhere, pl.BlockSpec(memory_space=pltpu.VMEM)),
        scratch_shapes=[
            vmem(NZ, TOK, DOUT, dtype=BF16),
            vmem(NZ, TOK, FEAT, dtype=BF16),
            vmem(FEAT, DOUT, dtype=BF16),
            vmem(RANK, DOUT),
            vmem(NZ, TOK, 2 * RANK, dtype=BF16),
            vmem(FEAT, DOUT),
            vmem(NJ, 8, FEAT), vmem(NJ, 8, FEAT), vmem(NY, 8, FEAT), vmem(NJ, 8, FEAT),
            vmem(NZ, 8, 2 * RANK), vmem(NJ, 8, 2 * RANK),
            vmem(NZ, TOK, 2 * RANK, dtype=BF16), vmem(NZ, TOK, 2 * RANK, dtype=BF16),
            vmem(2, NX, 8, DOUT), vmem(NX, 8, DOUT), vmem(NX, 8, DOUT), vmem(NX, 8, DOUT),
            vmem(NY, 8, FEAT), vmem(NY, 8, FEAT), vmem(NZ, 8, FEAT), vmem(NY, 8, FEAT),
            vmem(8, 8, DOUT),
            vmem(RANK, FEAT),
            vmem(RANK, DOUT),
            pltpu.SemaphoreType.DMA((N_SEMS,)),
            pltpu.SemaphoreType.DMA((N_SEMS,)),
            pltpu.SemaphoreType.DMA((6,)),
        ],
        compiler_params=pltpu.CompilerParams(
            collective_id=0, has_side_effects=True, vmem_limit_bytes=48 * 1024 * 1024
        ),
        cost_estimate=pl.CostEstimate(flops=2 * 10**9, bytes_accessed=6 * 10**6, transcendentals=0),
    )(*(pltpu.with_memory_space_constraint(v, pltpu.HBM) for v in (x_input.reshape(NZ, TOK, FEAT), dy_grad[0], error_in[0], q_init.T)))
    return p_t.T, q_t.reshape(RANK, DOUT).T, err[None]


def solution(mesh):
    in_specs = (P("dp", None, "mp"), P("dp", "mp", None), P("dp", "mp", None), P())
    out_specs = (P("mp", None), P(), P("dp", "mp", None))
    return jax.shard_map(local, mesh=mesh, in_specs=in_specs, out_specs=out_specs, check_vma=False)
```

```python
import jax
import jax.numpy as jnp
from jax import lax
from jax.experimental import pallas as pl
from jax.experimental.pallas import tpu as pltpu
from jax.sharding import PartitionSpec as P

F32, BF16 = jnp.float32, jnp.bfloat16
HIGHEST = lax.Precision.HIGHEST
NZ, NY, NX = 8, 8, 4
NJ = 2 * NX
TOK, FEAT, DOUT, RANK = 192, 256, 2048, 64
CHUNKS = 4
PIECE = TOK // CHUNKS
TILE = 512
PIVOTS = 4
ORDER = (4, 3, 5, 2, 6, 1, 7)
N_SEMS = 128
NEAR = 2

NN = (((1,), (0,)), ((), ()))
NT = (((1,), (1,)), ((), ()))
TN = (((0,), (0,)), ((), ()))


def mm(a, b, dims, precision=None):
    return lax.dot_general(a, b, dims, precision=precision, preferred_element_type=F32)


def split_rows(v):
    high = v.astype(BF16)
    low = (v - high.astype(F32)).astype(BF16)
    return high, low


def split_lanes(v):
    both = v + pltpu.roll(v, RANK, axis=1)
    high = both.astype(BF16).astype(F32)
    lane = lax.broadcasted_iota(jnp.int32, both.shape, 1)
    return jnp.where(lane < RANK, high, both - high).astype(BF16)


def fold(twice):
    half = RANK // 2
    lane = lax.broadcasted_iota(jnp.int32, (half, 2 * RANK), 1)
    return jnp.where(lane < RANK, twice[:half], twice[half:])


def unfold(folded):
    lane = lax.broadcasted_iota(jnp.int32, folded.shape, 1)
    other = pltpu.roll(folded, RANK, axis=1)
    return jnp.concatenate([jnp.where(lane < RANK, folded, other), jnp.where(lane < RANK, other, folded)], axis=0)


def inverse_factor(gram2, between):
    lane = lax.broadcasted_iota(jnp.int32, gram2.shape, 1)
    row = lax.broadcasted_iota(jnp.int32, gram2.shape, 0)
    rows = lax.broadcasted_iota(jnp.int32, (RANK, 1), 0)
    a = jnp.where(lane < RANK, gram2, jnp.where(lane - RANK == row, 1.0, 0.0))
    for k in range(0, RANK, PIVOTS):
        columns = [jnp.broadcast_to(a[:, k + i : k + i + 1], a.shape) for i in range(PIVOTS)]
        lines = [a[k + i : k + i + 1, :] for i in range(PIVOTS)]
        for i in range(PIVOTS):
            here = slice(k + i, k + i + 1)
            factor = jnp.where(rows > k + i, columns[i] * (1.0 / columns[i][here]), 0.0)
            for later in range(i + 1, PIVOTS):
                columns[later] = columns[later] - factor * columns[later][here]
                lines[later] = lines[later] - factor[k + later : k + later + 1] * lines[i]
            a = a - factor * lines[i]
        between(k)
    diagonal = jnp.sum(jnp.where(lane == row, a, 0.0), axis=1, keepdims=True)
    root = lax.rsqrt(diagonal)
    root = root * (1.5 - 0.5 * (diagonal * root) * root)
    return jnp.where(lane < RANK, 0.0, a * root)


def kernel(
    x_ref, dy_ref, e_ref, q_ref, p_out, q_out, err_out,
    dyg, xv, ev, qv, yq, acc, part_p, in_pj, in_py, all_p, in_g, part_x, in_x,
    q_part, in_qc, q_core, in_qx, q_y, in_qy, in_qz, all_qy, all_q, p_keep, q_near,
    send_sem, recv_sem, load_sem,
):
    dp, z = lax.axis_index("dp"), lax.axis_index("mp")
    y, j = lax.div(dp, NJ), lax.rem(dp, NJ)
    x, core = lax.div(j, 2), lax.rem(j, 2)
    counter = iter(range(N_SEMS))
    unsent = []

    at_z = lambda k: (dp, lax.rem(z + k + NZ, NZ))
    at_y = lambda k: (lax.rem(y + k, NY) * NJ + j, z)
    at_j = lambda k: (y * NJ + lax.rem(j + k, NJ), z)
    at_x = lambda k: (y * NJ + lax.rem(x + k, NX) * 2 + core, z)
    at_core = (y * NJ + x * 2 + 1 - core, z)

    def send(src, dst, device):
        n = next(counter)
        copy = pltpu.make_async_remote_copy(
            src_ref=src, dst_ref=dst, send_sem=send_sem.at[n], recv_sem=recv_sem.at[n],
            device_id=device, device_id_type=pl.DeviceIdType.MESH,
        )
        copy.start()
        unsent.append(copy)
        return copy

    def receive(copies):
        while len(unsent) > len(copies):
            unsent.pop(0).wait_send()
        for copy in copies:
            copy.wait_recv()

    loads = [
        pltpu.make_async_copy(src, dst, load_sem.at[n])
        for n, (src, dst) in enumerate(((dy_ref, dyg.at[z]), (q_ref, qv), (x_ref, xv), (e_ref, ev)))
    ]
    for load in loads:
        load.start()

    barrier = pltpu.get_barrier_semaphore()
    peers = [at_z(k) for k in range(1, NZ)] + [at_y(k) for k in range(1, NY)] + [at_j(k) for k in range(1, NJ)]
    for peer in peers:
        pl.semaphore_signal(barrier, inc=1, device_id=peer, device_id_type=pl.DeviceIdType.MESH)

    loads[0].wait()
    loads[1].wait()
    q_halves = jnp.concatenate(split_rows(qv[...]), axis=0)
    yq[z] = split_lanes(mm(dyg[z], q_halves, NT))
    pl.semaphore_wait(barrier, len(peers))

    flows = {
        1: [(h, c) for h in (1, 2, 3) for c in range(CHUNKS)] + [(4, 0), (4, 1)],
        -1: [(h, c) for h in (1, 2, 3) for c in (2, 3, 0, 1)] + [(4, 2), (4, 3)],
    }
    bulk = {}

    def bulk_send(way, hop, c):
        block = lax.rem(z - way * (hop - 1) + NZ, NZ)
        ref = dyg.at[block, pl.ds(c * PIECE, PIECE)]
        source = dy_ref.at[pl.ds(c * PIECE, PIECE)] if hop == 1 else ref
        bulk[way, hop, c] = send(source, ref, at_z(way))
        unsent.pop()

    def first_sends(n):
        for way in (1, -1):
            bulk_send(way, *flows[way][n])

    def bulk_forward(n):
        for way in (1, -1):
            hop, c = flows[way][n]
            bulk[way, hop, c].wait_recv()
            if (hop + 1, c) in flows[way]:
                bulk_send(way, hop + 1, c)
            if n >= 2:
                bulk[(way, *flows[way][n - 2])].wait_send()

    def add_grad(block):
        @pl.loop(0, DOUT // TILE)
        def _(t):
            cols = pl.ds(pl.multiple_of(t * TILE, TILE), TILE)
            acc[:, cols] += mm(xv[block], dyg[block, :, cols], TN)

    right = send(yq.at[z], yq.at[z], at_z(1))
    left = send(yq.at[z], yq.at[z], at_z(-1))
    first_sends(0)
    first_sends(1)
    loads[2].wait()
    loads[3].wait()
    total = mm(q_halves, ev[...], NT) + mm(yq[z], xv[z], TN)
    for hop in (1, 2, 3, 4):
        from_left, from_right = lax.rem(z - hop + NZ, NZ), lax.rem(z + hop, NZ)
        right.wait_recv()
        if hop < 4:
            right = send(yq.at[from_left], yq.at[from_left], at_z(1))
            left.wait_recv()
            if hop < 3:
                left = send(yq.at[from_right], yq.at[from_right], at_z(-1))
            if hop > 1:
                first_sends(hop)
            total += mm(yq[from_right], xv[from_right], TN)
        total += mm(yq[from_left], xv[from_left], TN)
    total = total[:RANK] + total[RANK:]

    for k in range(NJ):
        part_p[k] = total[k * 8 : k * 8 + 8]
    copies = [send(part_p.at[lax.rem(j + k, NJ)], in_pj.at[j], at_j(k)) for k in ORDER]
    in_pj[j] = part_p[j]

    @pl.loop(0, DOUT // TILE)
    def _(t):
        cols = pl.ds(pl.multiple_of(t * TILE, TILE), TILE)
        acc[:, cols] = ev[:, cols].astype(F32) + mm(xv[z], dyg[z, :, cols], TN)

    bulk_forward(0)
    receive(copies)
    in_py[y] = sum(in_pj[k] for k in range(1, NJ)) + in_pj[0]
    copies = [send(in_py.at[y], in_py.at[y], at_y(k)) for k in ORDER]
    bulk_forward(1)
    receive(copies)
    all_p[j] = sum(in_py[k] for k in range(1, NY)) + in_py[0]
    copies = [send(all_p.at[j], all_p.at[j], at_j(k)) for k in ORDER]
    bulk_forward(2)
    receive(copies)
    p_sum = all_p[...].reshape(RANK, FEAT)
    p_twice = jnp.concatenate([p_sum, p_sum], axis=0)

    in_g[z] = fold(mm(p_sum, p_twice, NT, HIGHEST))
    copies = [send(in_g.at[z], in_g.at[z], at_z(k)) for k in ORDER]
    bulk_forward(3)
    add_grad(lax.rem(z + NZ - 1, NZ))
    add_grad(lax.rem(z + 1, NZ))
    receive(copies)
    gram_twice = unfold(sum(in_g[k] for k in range(1, NZ)) + in_g[0])
    steps = {24: 4, 52: 5}
    between = lambda k: bulk_forward(steps[k]) if k in steps else None
    inverse = inverse_factor(gram_twice, between)
    p_t = mm(inverse, p_twice, NN, HIGHEST)
    p_keep[...] = p_t
    p_store = pltpu.make_async_copy(p_keep, p_out, load_sem.at[4])
    p_store.start()
    p_high, p_low = split_rows(p_t)
    p_halves = jnp.concatenate([p_high, p_low], axis=0)

    far_steps = [k for k in ORDER if min(k, NZ - k) > NEAR]
    copies = []
    for k in far_steps:
        block = lax.rem(z + k, NZ)
        part_x[block] = split_lanes(mm(xv[block], p_halves, NT))
        copies.append(send(part_x.at[block], in_x.at[z], at_z(k)))
    bulk_forward(6)
    bulk_forward(7)
    for hop in range(2, NEAR + 1):
        add_grad(lax.rem(z + NZ - hop, NZ))
        add_grad(lax.rem(z + hop, NZ))

    @pl.loop(0, DOUT // TILE)
    def _(t):
        cols = pl.ds(pl.multiple_of(t * TILE, TILE), TILE)
        near_high, near_low = split_rows(acc[:, cols])
        tile = mm(p_halves, near_high, NN)
        q_near[:, cols] = tile[:RANK] + tile[RANK:] + mm(p_high, near_low, NN)

    receive(copies)
    xp = split_lanes(sum(in_x[lax.rem(z + NZ - k, NZ)].astype(F32) for k in far_steps))
    copies = []
    for t in range(DOUT // TILE):
        cols = slice(t * TILE, t * TILE + TILE)
        tile = mm(xp, dyg[z, :, cols], TN)
        tile = tile[:RANK] + tile[RANK:] + q_near[:, cols]
        for k in range(8):
            q_part[k // 4, k % 4, :, cols] = tile[k * 8 : k * 8 + 8]
        copies.append(send(q_part.at[1 - core, :, :, cols], in_qc.at[:, :, cols], at_core))
    receive(copies)
    for k in range(NX):
        q_core[k] = q_part[core, k] + in_qc[k]
    copies = [send(q_core.at[lax.rem(x + k, NX)], in_qx.at[x], at_x(k)) for k in (2, 1, 3)]
    in_qx[x] = q_core[x]
    receive(copies)
    rows = (in_qx[0] + in_qx[1]) + (in_qx[2] + in_qx[3])
    for k in range(NY):
        q_y[k] = rows[:, k * 256 : k * 256 + 256]
    copies = [send(q_y.at[lax.rem(y + k, NY)], in_qy.at[y], at_y(k)) for k in ORDER]
    in_qy[y] = q_y[y]
    bulk_forward(8)
    receive(copies)
    in_qz[z] = sum(in_qy[k] for k in range(1, NY)) + in_qy[0]
    copies = [send(in_qz.at[z], in_qz.at[z], at_z(k)) for k in ORDER]
    bulk_forward(9)
    receive(copies)
    all_qy[y] = sum(in_qz[k] for k in range(1, NZ)) + in_qz[0]
    copies = [send(all_qy.at[y], all_qy.at[y], at_y(k)) for k in ORDER]
    receive(copies)
    mine = core * NX + x
    for k in range(NY):
        all_q[mine, :, k * 256 : k * 256 + 256] = all_qy[k]
    copies = [send(all_q.at[mine], all_q.at[mine], at_x(k)) for k in (2, 1, 3)]
    across = [send(all_q.at[mine], all_q.at[mine], at_core)]
    for k, copy in ((1, copies[1]), (3, copies[2]), (2, copies[0])):
        copy.wait_recv()
        slot = core * NX + lax.rem(x - k + NX, NX)
        across.append(send(all_q.at[slot], all_q.at[slot], at_core))
    bulk_forward(10)
    bulk_forward(11)
    for hop in range(NEAR + 1, 4):
        add_grad(lax.rem(z + NZ - hop, NZ))
        add_grad(lax.rem(z + hop, NZ))
    receive(across)
    q_store = pltpu.make_async_copy(all_q, q_out, load_sem.at[5])
    q_store.start()
    bulk_forward(12)
    bulk_forward(13)
    p_cat = jnp.concatenate([p_high, p_high, p_low], axis=0)
    far = lax.rem(z + 4, NZ)
    for t in range(DOUT // TILE):
        cols = slice(t * TILE, t * TILE + TILE)
        q_high, q_low = split_rows(all_q[:, :, cols].reshape(RANK, TILE))
        approx = mm(p_cat, jnp.concatenate([q_high, q_low, q_high], axis=0), TN)
        err_out[:, cols] = (acc[:, cols] + mm(xv[far], dyg[far, :, cols], TN) - approx).astype(BF16)
    for way in (1, -1):
        for piece in flows[way][-2:]:
            bulk[(way, *piece)].wait_send()
    receive([])
    p_store.wait()
    q_store.wait()


def local(x_input, dy_grad, error_in, q_init):
    anywhere = pl.BlockSpec(memory_space=pl.ANY)
    vmem = lambda *shape, dtype=F32: pltpu.VMEM(shape, dtype)
    p_t, q_t, err = pl.pallas_call(
        kernel,
        out_shape=(
            jax.ShapeDtypeStruct((RANK, FEAT), F32),
            jax.ShapeDtypeStruct((8, 8, DOUT), F32),
            jax.ShapeDtypeStruct((FEAT, DOUT), BF16),
        ),
        in_specs=[pl.BlockSpec(memory_space=pltpu.HBM)] * 4,
        out_specs=(anywhere, anywhere, pl.BlockSpec(memory_space=pltpu.VMEM)),
        scratch_shapes=[
            vmem(NZ, TOK, DOUT, dtype=BF16),
            vmem(NZ, TOK, FEAT, dtype=BF16),
            vmem(FEAT, DOUT, dtype=BF16),
            vmem(RANK, DOUT),
            vmem(NZ, TOK, 2 * RANK, dtype=BF16),
            vmem(FEAT, DOUT),
            vmem(NJ, 8, FEAT), vmem(NJ, 8, FEAT), vmem(NY, 8, FEAT), vmem(NJ, 8, FEAT),
            vmem(NZ, RANK // 2, 2 * RANK),
            vmem(NZ, TOK, 2 * RANK, dtype=BF16), vmem(NZ, TOK, 2 * RANK, dtype=BF16),
            vmem(2, NX, 8, DOUT), vmem(NX, 8, DOUT), vmem(NX, 8, DOUT), vmem(NX, 8, DOUT),
            vmem(NY, 8, FEAT), vmem(NY, 8, FEAT), vmem(NZ, 8, FEAT), vmem(NY, 8, FEAT),
            vmem(8, 8, DOUT),
            vmem(RANK, FEAT),
            vmem(RANK, DOUT),
            pltpu.SemaphoreType.DMA((N_SEMS,)),
            pltpu.SemaphoreType.DMA((N_SEMS,)),
            pltpu.SemaphoreType.DMA((6,)),
        ],
        compiler_params=pltpu.CompilerParams(
            collective_id=0, has_side_effects=True, vmem_limit_bytes=48 * 1024 * 1024
        ),
        cost_estimate=pl.CostEstimate(flops=2 * 10**9, bytes_accessed=6 * 10**6, transcendentals=0),
    )(*(pltpu.with_memory_space_constraint(v, pltpu.HBM) for v in (x_input.reshape(NZ, TOK, FEAT), dy_grad[0], error_in[0], q_init.T)))
    return p_t.T, q_t.reshape(RANK, DOUT).T, err[None]


def solution(mesh):
    in_specs = (P("dp", None, "mp"), P("dp", "mp", None), P("dp", "mp", None), P())
    out_specs = (P("mp", None), P(), P("dp", "mp", None))
    return jax.shard_map(local, mesh=mesh, in_specs=in_specs, out_specs=out_specs, check_vma=False)
```

```python
import jax
import jax.numpy as jnp
from jax import lax
from jax.experimental import pallas as pl
from jax.experimental.pallas import tpu as pltpu
from jax.sharding import PartitionSpec as P

F32, BF16 = jnp.float32, jnp.bfloat16
HIGHEST = lax.Precision.HIGHEST
NZ, NY, NX = 8, 8, 4
NJ = 2 * NX
TOK, FEAT, DOUT, RANK = 192, 256, 2048, 64
CHUNKS = 4
PIECE = TOK // CHUNKS
TILE = 512
PIVOTS = 4
ORDER = (4, 3, 5, 2, 6, 1, 7)
N_SEMS = 128
NEAR = 2

NN = (((1,), (0,)), ((), ()))
NT = (((1,), (1,)), ((), ()))
TN = (((0,), (0,)), ((), ()))


def mm(a, b, dims, precision=None):
    return lax.dot_general(a, b, dims, precision=precision, preferred_element_type=F32)


def split_rows(v):
    high = v.astype(BF16)
    low = (v - high.astype(F32)).astype(BF16)
    return high, low


def split_lanes(v):
    both = v + pltpu.roll(v, RANK, axis=1)
    high = both.astype(BF16).astype(F32)
    lane = lax.broadcasted_iota(jnp.int32, both.shape, 1)
    return jnp.where(lane < RANK, high, both - high).astype(BF16)


def fold(twice):
    half = RANK // 2
    lane = lax.broadcasted_iota(jnp.int32, (half, 2 * RANK), 1)
    return jnp.where(lane < RANK, twice[:half], twice[half:])


def unfold(folded):
    lane = lax.broadcasted_iota(jnp.int32, folded.shape, 1)
    other = pltpu.roll(folded, RANK, axis=1)
    return jnp.concatenate([jnp.where(lane < RANK, folded, other), jnp.where(lane < RANK, other, folded)], axis=0)


def inverse_factor(gram2, between):
    lane = lax.broadcasted_iota(jnp.int32, gram2.shape, 1)
    row = lax.broadcasted_iota(jnp.int32, gram2.shape, 0)
    rows = lax.broadcasted_iota(jnp.int32, (RANK, 1), 0)
    a = jnp.where(lane < RANK, gram2, jnp.where(lane - RANK == row, 1.0, 0.0))
    for k in range(0, RANK, PIVOTS):
        columns = [jnp.broadcast_to(a[:, k + i : k + i + 1], a.shape) for i in range(PIVOTS)]
        lines = [a[k + i : k + i + 1, :] for i in range(PIVOTS)]
        for i in range(PIVOTS):
            here = slice(k + i, k + i + 1)
            factor = jnp.where(rows > k + i, columns[i] * (1.0 / columns[i][here]), 0.0)
            for later in range(i + 1, PIVOTS):
                columns[later] = columns[later] - factor * columns[later][here]
                lines[later] = lines[later] - factor[k + later : k + later + 1] * lines[i]
            a = a - factor * lines[i]
        between(k)
    diagonal = jnp.sum(jnp.where(lane == row, a, 0.0), axis=1, keepdims=True)
    root = lax.rsqrt(diagonal)
    root = root * (1.5 - 0.5 * (diagonal * root) * root)
    return jnp.where(lane < RANK, 0.0, a * root)


def kernel(
    x_ref, dy_ref, e_ref, q_ref, p_out, all_q, acc,
    dyg, xv, ev, qv, yq, part_p, in_pj, in_py, all_p, in_g, part_x, in_x,
    q_part, in_qc, q_core, in_qx, q_y, in_qy, in_qz, all_qy, q_near,
    send_sem, recv_sem, load_sem,
):
    dp, z = lax.axis_index("dp"), lax.axis_index("mp")
    y, j = lax.div(dp, NJ), lax.rem(dp, NJ)
    x, core = lax.div(j, 2), lax.rem(j, 2)
    counter = iter(range(N_SEMS))
    unsent = []

    at_z = lambda k: (dp, lax.rem(z + k + NZ, NZ))
    at_y = lambda k: (lax.rem(y + k, NY) * NJ + j, z)
    at_j = lambda k: (y * NJ + lax.rem(j + k, NJ), z)
    at_x = lambda k: (y * NJ + lax.rem(x + k, NX) * 2 + core, z)
    at_core = (y * NJ + x * 2 + 1 - core, z)

    def send(src, dst, device):
        n = next(counter)
        copy = pltpu.make_async_remote_copy(
            src_ref=src, dst_ref=dst, send_sem=send_sem.at[n], recv_sem=recv_sem.at[n],
            device_id=device, device_id_type=pl.DeviceIdType.MESH,
        )
        copy.start()
        unsent.append(copy)
        return copy

    def receive(copies):
        while len(unsent) > len(copies):
            unsent.pop(0).wait_send()
        for copy in copies:
            copy.wait_recv()

    loads = [
        pltpu.make_async_copy(src, dst, load_sem.at[n])
        for n, (src, dst) in enumerate(((dy_ref, dyg.at[z]), (q_ref, qv), (x_ref, xv), (e_ref, ev)))
    ]
    for load in loads:
        load.start()

    barrier = pltpu.get_barrier_semaphore()
    peers = [at_z(k) for k in range(1, NZ)] + [at_y(k) for k in range(1, NY)] + [at_j(k) for k in range(1, NJ)]
    for peer in peers:
        pl.semaphore_signal(barrier, inc=1, device_id=peer, device_id_type=pl.DeviceIdType.MESH)

    loads[0].wait()
    loads[1].wait()
    q_halves = jnp.concatenate(split_rows(qv[...]), axis=0)
    yq[z] = split_lanes(mm(dyg[z], q_halves, NT))
    pl.semaphore_wait(barrier, len(peers))

    flows = {
        1: [(h, c) for h in (1, 2, 3) for c in range(CHUNKS)] + [(4, 0), (4, 1)],
        -1: [(h, c) for h in (1, 2, 3) for c in (2, 3, 0, 1)] + [(4, 2), (4, 3)],
    }
    bulk = {}

    def bulk_send(way, hop, c):
        block = lax.rem(z - way * (hop - 1) + NZ, NZ)
        ref = dyg.at[block, pl.ds(c * PIECE, PIECE)]
        source = dy_ref.at[pl.ds(c * PIECE, PIECE)] if hop == 1 else ref
        bulk[way, hop, c] = send(source, ref, at_z(way))
        unsent.pop()

    def first_sends(n):
        for way in (1, -1):
            bulk_send(way, *flows[way][n])

    def bulk_wait(n):
        for way in (1, -1):
            bulk[(way, *flows[way][n])].wait_recv()

    def bulk_forward(n, waited=False):
        if not waited:
            bulk_wait(n)
        for way in (1, -1):
            hop, c = flows[way][n]
            if (hop + 1, c) in flows[way]:
                bulk_send(way, hop + 1, c)
            if n >= 2:
                bulk[(way, *flows[way][n - 2])].wait_send()

    def add_grad(block):
        @pl.loop(0, DOUT // TILE)
        def _(t):
            cols = pl.ds(pl.multiple_of(t * TILE, TILE), TILE)
            acc[:, cols] += mm(xv[block], dyg[block, :, cols], TN)

    right = send(yq.at[z], yq.at[z], at_z(1))
    left = send(yq.at[z], yq.at[z], at_z(-1))
    first_sends(0)
    loads[2].wait()
    loads[3].wait()
    total = mm(q_halves, ev[...], NT) + mm(yq[z], xv[z], TN)
    for hop in (1, 2, 3, 4):
        from_left, from_right = lax.rem(z - hop + NZ, NZ), lax.rem(z + hop, NZ)
        right.wait_recv()
        if hop < 4:
            right = send(yq.at[from_left], yq.at[from_left], at_z(1))
            left.wait_recv()
            if hop < 3:
                left = send(yq.at[from_right], yq.at[from_right], at_z(-1))
            if hop > 1:
                first_sends(hop - 1)
            total += mm(yq[from_right], xv[from_right], TN)
        total += mm(yq[from_left], xv[from_left], TN)
    total = total[:RANK] + total[RANK:]

    for k in range(NJ):
        part_p[k] = total[k * 8 : k * 8 + 8]
    copies = [send(part_p.at[lax.rem(j + k, NJ)], in_pj.at[j], at_j(k)) for k in ORDER]
    in_pj[j] = part_p[j]
    first_sends(3)

    @pl.loop(0, DOUT // TILE)
    def _(t):
        cols = pl.ds(pl.multiple_of(t * TILE, TILE), TILE)
        acc[:, cols] = ev[:, cols].astype(F32) + mm(xv[z], dyg[z, :, cols], TN)

    bulk_forward(0)
    receive(copies)
    in_py[y] = sum(in_pj[k] for k in range(1, NJ)) + in_pj[0]
    copies = [send(in_py.at[y], in_py.at[y], at_y(k)) for k in ORDER]
    bulk_forward(1)
    receive(copies)
    all_p[j] = sum(in_py[k] for k in range(1, NY)) + in_py[0]
    copies = [send(all_p.at[j], all_p.at[j], at_j(k)) for k in ORDER]
    bulk_forward(2)
    receive(copies)
    p_sum = all_p[...].reshape(RANK, FEAT)
    p_twice = jnp.concatenate([p_sum, p_sum], axis=0)

    in_g[z] = fold(mm(p_sum, p_twice, NT, HIGHEST))
    copies = [send(in_g.at[z], in_g.at[z], at_z(k)) for k in ORDER]
    bulk_forward(3)
    add_grad(lax.rem(z + NZ - 1, NZ))
    add_grad(lax.rem(z + 1, NZ))
    receive(copies)
    gram_twice = unfold(sum(in_g[k] for k in range(1, NZ)) + in_g[0])
    steps = {24: 4, 52: 5}
    between = lambda k: bulk_forward(steps[k]) if k in steps else None
    inverse = inverse_factor(gram_twice, between)
    p_t = mm(inverse, p_twice, NN, HIGHEST)
    p_out[...] = p_t
    p_high, p_low = split_rows(p_t)
    p_halves = jnp.concatenate([p_high, p_low], axis=0)

    far_steps = [k for k in ORDER if min(k, NZ - k) > NEAR]
    copies = []
    for k in far_steps:
        block = lax.rem(z + k, NZ)
        part_x[block] = split_lanes(mm(xv[block], p_halves, NT))
        copies.append(send(part_x.at[block], in_x.at[z], at_z(k)))
    bulk_forward(6)
    bulk_wait(7)
    for hop in range(2, NEAR + 1):
        add_grad(lax.rem(z + NZ - hop, NZ))
        add_grad(lax.rem(z + hop, NZ))

    @pl.loop(0, DOUT // TILE)
    def _(t):
        cols = pl.ds(pl.multiple_of(t * TILE, TILE), TILE)
        near_high, near_low = split_rows(acc[:, cols])
        tile = mm(p_halves, near_high, NN)
        q_near[:, cols] = tile[:RANK] + tile[RANK:] + mm(p_high, near_low, NN)

    receive(copies)
    bulk_forward(7, waited=True)
    xp = split_lanes(sum(in_x[lax.rem(z + NZ - k, NZ)].astype(F32) for k in far_steps))
    copies = []
    for t in range(DOUT // TILE):
        cols = slice(t * TILE, t * TILE + TILE)
        tile = mm(xp, dyg[z, :, cols], TN)
        tile = tile[:RANK] + tile[RANK:] + q_near[:, cols]
        for k in range(8):
            q_part[k // 4, k % 4, :, cols] = tile[k * 8 : k * 8 + 8]
        copies.append(send(q_part.at[1 - core, :, :, cols], in_qc.at[:, :, cols], at_core))
    bulk_forward(8)
    receive(copies)
    for k in range(NX):
        q_core[k] = q_part[core, k] + in_qc[k]
    copies = [send(q_core.at[lax.rem(x + k, NX)], in_qx.at[x], at_x(k)) for k in (2, 1, 3)]
    in_qx[x] = q_core[x]
    bulk_forward(9)
    receive(copies)
    rows = (in_qx[0] + in_qx[1]) + (in_qx[2] + in_qx[3])
    for k in range(NY):
        q_y[k] = rows[:, k * 256 : k * 256 + 256]
    copies = [send(q_y.at[lax.rem(y + k, NY)], in_qy.at[y], at_y(k)) for k in ORDER]
    in_qy[y] = q_y[y]
    receive(copies)
    in_qz[z] = sum(in_qy[k] for k in range(1, NY)) + in_qy[0]
    copies = [send(in_qz.at[z], in_qz.at[z], at_z(k)) for k in ORDER]
    receive(copies)
    all_qy[y] = sum(in_qz[k] for k in range(1, NZ)) + in_qz[0]
    copies = [send(all_qy.at[y], all_qy.at[y], at_y(k)) for k in ORDER]
    receive(copies)
    mine = core * NX + x
    for k in range(NY):
        all_q[mine, :, k * 256 : k * 256 + 256] = all_qy[k]
    copies = [send(all_q.at[mine], all_q.at[mine], at_x(k)) for k in (2, 1, 3)]
    across = [send(all_q.at[mine], all_q.at[mine], at_core)]
    for k, copy in ((1, copies[1]), (3, copies[2]), (2, copies[0])):
        copy.wait_recv()
        slot = core * NX + lax.rem(x - k + NX, NX)
        across.append(send(all_q.at[slot], all_q.at[slot], at_core))
    bulk_forward(10)
    bulk_forward(11)
    for hop in range(NEAR + 1, 4):
        add_grad(lax.rem(z + NZ - hop, NZ))
        add_grad(lax.rem(z + hop, NZ))
    bulk_forward(12)
    bulk_forward(13)
    add_grad(lax.rem(z + 4, NZ))
    receive(across)
    for way in (1, -1):
        for piece in flows[way][-2:]:
            bulk[(way, *piece)].wait_send()
    receive([])


def finish(acc, p_ref, q_ref, p_out, q_out, err_out, err_v, sem):
    copies = [pltpu.make_async_copy(p_ref, p_out, sem.at[0]), pltpu.make_async_copy(q_ref, q_out, sem.at[1])]
    for copy in copies:
        copy.start()
    p_high, p_low = split_rows(p_ref[...])
    p_cat = jnp.concatenate([p_high, p_high, p_low], axis=0)
    for t in range(DOUT // TILE):
        cols = slice(t * TILE, t * TILE + TILE)
        q_high, q_low = split_rows(q_ref[:, :, cols].reshape(RANK, TILE))
        approx = mm(p_cat, jnp.concatenate([q_high, q_low, q_high], axis=0), TN)
        err_v[:, cols] = (acc[:, cols] - approx).astype(BF16)
        copy = pltpu.make_async_copy(err_v.at[:, cols], err_out.at[:, cols], sem.at[2 + t])
        copy.start()
        copies.append(copy)
    for copy in copies:
        copy.wait()


def local(x_input, dy_grad, error_in, q_init):
    anywhere = pl.BlockSpec(memory_space=pl.ANY)
    vmem = lambda *shape, dtype=F32: pltpu.VMEM(shape, dtype)
    shapes = (
        jax.ShapeDtypeStruct((RANK, FEAT), F32),
        jax.ShapeDtypeStruct((8, 8, DOUT), F32),
        jax.ShapeDtypeStruct((FEAT, DOUT), F32),
    )
    held = [pl.BlockSpec(memory_space=pltpu.VMEM)] * 3
    p_t, q_t, acc = pl.pallas_call(
        kernel,
        out_shape=shapes,
        in_specs=[pl.BlockSpec(memory_space=pltpu.HBM)] * 4,
        out_specs=held,
        scratch_shapes=[
            vmem(NZ, TOK, DOUT, dtype=BF16),
            vmem(NZ, TOK, FEAT, dtype=BF16),
            vmem(FEAT, DOUT, dtype=BF16),
            vmem(RANK, DOUT),
            vmem(NZ, TOK, 2 * RANK, dtype=BF16),
            vmem(NJ, 8, FEAT), vmem(NJ, 8, FEAT), vmem(NY, 8, FEAT), vmem(NJ, 8, FEAT),
            vmem(NZ, RANK // 2, 2 * RANK),
            vmem(NZ, TOK, 2 * RANK, dtype=BF16), vmem(NZ, TOK, 2 * RANK, dtype=BF16),
            vmem(2, NX, 8, DOUT), vmem(NX, 8, DOUT), vmem(NX, 8, DOUT), vmem(NX, 8, DOUT),
            vmem(NY, 8, FEAT), vmem(NY, 8, FEAT), vmem(NZ, 8, FEAT), vmem(NY, 8, FEAT),
            vmem(RANK, DOUT),
            pltpu.SemaphoreType.DMA((N_SEMS,)),
            pltpu.SemaphoreType.DMA((N_SEMS,)),
            pltpu.SemaphoreType.DMA((4,)),
        ],
        compiler_params=pltpu.CompilerParams(
            collective_id=0, has_side_effects=True, vmem_limit_bytes=48 * 1024 * 1024
        ),
        cost_estimate=pl.CostEstimate(flops=2 * 10**9, bytes_accessed=6 * 10**6, transcendentals=0),
    )(*(pltpu.with_memory_space_constraint(v, pltpu.HBM) for v in (x_input.reshape(NZ, TOK, FEAT), dy_grad[0], error_in[0], q_init.T)))
    p_t, q_t, err = pl.pallas_call(
        finish,
        out_shape=(*shapes[:2], jax.ShapeDtypeStruct((FEAT, DOUT), BF16)),
        in_specs=held,
        out_specs=[anywhere] * 3,
        scratch_shapes=[vmem(FEAT, DOUT, dtype=BF16), pltpu.SemaphoreType.DMA((2 + DOUT // TILE,))],
        compiler_params=pltpu.CompilerParams(vmem_limit_bytes=16 * 1024 * 1024),
        cost_estimate=pl.CostEstimate(flops=2 * 10**8, bytes_accessed=2 * 10**6, transcendentals=0),
    )(acc, p_t, q_t)
    return p_t.T, q_t.reshape(RANK, DOUT).T, err[None]


def solution(mesh):
    in_specs = (P("dp", None, "mp"), P("dp", "mp", None), P("dp", "mp", None), P())
    out_specs = (P("mp", None), P(), P("dp", "mp", None))
    return jax.shard_map(local, mesh=mesh, in_specs=in_specs, out_specs=out_specs, check_vma=False)
```

```python
import jax
import jax.numpy as jnp
from jax import lax
from jax.experimental import pallas as pl
from jax.experimental.pallas import tpu as pltpu
from jax.sharding import PartitionSpec as P

F32, BF16 = jnp.float32, jnp.bfloat16
HIGHEST = lax.Precision.HIGHEST
NZ, NY, NX = 8, 8, 4
NJ = 2 * NX
TOK, FEAT, DOUT, RANK = 192, 256, 2048, 64
CHUNKS = 4
PIECE = TOK // CHUNKS
TILE = 512
PIVOTS = 4
ORDER = (4, 3, 5, 2, 6, 1, 7)
N_SEMS = 128
NEAR = 2

NN = (((1,), (0,)), ((), ()))
NT = (((1,), (1,)), ((), ()))
TN = (((0,), (0,)), ((), ()))


def mm(a, b, dims, precision=None):
    return lax.dot_general(a, b, dims, precision=precision, preferred_element_type=F32)


def split_rows(v):
    high = v.astype(BF16)
    low = (v - high.astype(F32)).astype(BF16)
    return high, low


def split_lanes(v):
    both = v + pltpu.roll(v, RANK, axis=1)
    high = both.astype(BF16).astype(F32)
    lane = lax.broadcasted_iota(jnp.int32, both.shape, 1)
    return jnp.where(lane < RANK, high, both - high).astype(BF16)


def inverse_factor(gram2, between):
    lane = lax.broadcasted_iota(jnp.int32, gram2.shape, 1)
    row = lax.broadcasted_iota(jnp.int32, gram2.shape, 0)
    rows = lax.broadcasted_iota(jnp.int32, (RANK, 1), 0)
    a = jnp.where(lane < RANK, gram2, jnp.where(lane - RANK == row, 1.0, 0.0))
    for k in range(0, RANK, PIVOTS):
        columns = [jnp.broadcast_to(a[:, k + i : k + i + 1], a.shape) for i in range(PIVOTS)]
        lines = [a[k + i : k + i + 1, :] for i in range(PIVOTS)]
        for i in range(PIVOTS):
            here = slice(k + i, k + i + 1)
            factor = jnp.where(rows > k + i, columns[i] * (1.0 / columns[i][here]), 0.0)
            for later in range(i + 1, PIVOTS):
                columns[later] = columns[later] - factor * columns[later][here]
                lines[later] = lines[later] - factor[k + later : k + later + 1] * lines[i]
            a = a - factor * lines[i]
        between(k)
    diagonal = jnp.sum(jnp.where(lane == row, a, 0.0), axis=1, keepdims=True)
    root = lax.rsqrt(diagonal)
    root = root * (1.5 - 0.5 * (diagonal * root) * root)
    return jnp.where(lane < RANK, 0.0, a * root)


def kernel(
    x_ref, dy_ref, e_ref, q_ref, p_out, all_q, acc,
    dyg, xv, ev, qv, yq, part_p, in_pj, in_py, all_p, in_g, all_g, part_x, in_x,
    q_part, in_qc, q_core, in_qx, q_y, in_qy, in_qz, all_qy, q_near,
    send_sem, recv_sem, load_sem,
):
    dp, z = lax.axis_index("dp"), lax.axis_index("mp")
    y, j = lax.div(dp, NJ), lax.rem(dp, NJ)
    x, core = lax.div(j, 2), lax.rem(j, 2)
    counter = iter(range(N_SEMS))
    unsent = []

    at_z = lambda k: (dp, lax.rem(z + k + NZ, NZ))
    at_y = lambda k: (lax.rem(y + k, NY) * NJ + j, z)
    at_j = lambda k: (y * NJ + lax.rem(j + k, NJ), z)
    at_x = lambda k: (y * NJ + lax.rem(x + k, NX) * 2 + core, z)
    at_core = (y * NJ + x * 2 + 1 - core, z)

    def send(src, dst, device):
        n = next(counter)
        copy = pltpu.make_async_remote_copy(
            src_ref=src, dst_ref=dst, send_sem=send_sem.at[n], recv_sem=recv_sem.at[n],
            device_id=device, device_id_type=pl.DeviceIdType.MESH,
        )
        copy.start()
        unsent.append(copy)
        return copy

    def receive(copies):
        while len(unsent) > len(copies):
            unsent.pop(0).wait_send()
        for copy in copies:
            copy.wait_recv()

    loads = [
        pltpu.make_async_copy(src, dst, load_sem.at[n])
        for n, (src, dst) in enumerate(((dy_ref, dyg.at[z]), (q_ref, qv), (x_ref, xv), (e_ref, ev)))
    ]
    for load in loads:
        load.start()

    barrier = pltpu.get_barrier_semaphore()
    peers = [at_z(k) for k in range(1, NZ)] + [at_y(k) for k in range(1, NY)] + [at_j(k) for k in range(1, NJ)]
    for peer in peers:
        pl.semaphore_signal(barrier, inc=1, device_id=peer, device_id_type=pl.DeviceIdType.MESH)

    pl.semaphore_wait(barrier, len(peers))

    flows = {
        1: [(h, c) for h in (1, 2, 3) for c in range(CHUNKS)] + [(4, 0), (4, 1)],
        -1: [(h, c) for h in (1, 2, 3) for c in (2, 3, 0, 1)] + [(4, 2), (4, 3)],
    }
    bulk = {}

    def bulk_send(way, hop, c):
        block = lax.rem(z - way * (hop - 1) + NZ, NZ)
        ref = dyg.at[block, pl.ds(c * PIECE, PIECE)]
        source = dy_ref.at[pl.ds(c * PIECE, PIECE)] if hop == 1 else ref
        bulk[way, hop, c] = send(source, ref, at_z(way))
        unsent.pop()

    def first_sends(n):
        for way in (1, -1):
            bulk_send(way, *flows[way][n])

    def bulk_forward(n):
        for way in (1, -1):
            hop, c = flows[way][n]
            bulk[way, hop, c].wait_recv()
            if (hop + 1, c) in flows[way]:
                bulk_send(way, hop + 1, c)
            if n >= 2:
                bulk[(way, *flows[way][n - 2])].wait_send()

    def add_grad(block):
        @pl.loop(0, DOUT // TILE)
        def _(t):
            cols = pl.ds(pl.multiple_of(t * TILE, TILE), TILE)
            acc[:, cols] += mm(xv[block], dyg[block, :, cols], TN)

    first_sends(0)
    loads[0].wait()
    loads[1].wait()
    q_halves = jnp.concatenate(split_rows(qv[...]), axis=0)
    yq[z] = split_lanes(mm(dyg[z], q_halves, NT))
    right = send(yq.at[z], yq.at[z], at_z(1))
    left = send(yq.at[z], yq.at[z], at_z(-1))
    first_sends(1)
    loads[2].wait()
    loads[3].wait()
    total = mm(q_halves, ev[...], NT) + mm(yq[z], xv[z], TN)
    for hop in (1, 2, 3, 4):
        from_left, from_right = lax.rem(z - hop + NZ, NZ), lax.rem(z + hop, NZ)
        right.wait_recv()
        if hop < 4:
            right = send(yq.at[from_left], yq.at[from_left], at_z(1))
            left.wait_recv()
            if hop < 3:
                left = send(yq.at[from_right], yq.at[from_right], at_z(-1))
            if hop > 1:
                first_sends(hop)
            total += mm(yq[from_right], xv[from_right], TN)
        total += mm(yq[from_left], xv[from_left], TN)
    total = total[:RANK] + total[RANK:]

    for k in range(NJ):
        part_p[k] = total[k * 8 : k * 8 + 8]
    copies = [send(part_p.at[lax.rem(j + k, NJ)], in_pj.at[j], at_j(k)) for k in ORDER]
    in_pj[j] = part_p[j]

    @pl.loop(0, DOUT // TILE)
    def _(t):
        cols = pl.ds(pl.multiple_of(t * TILE, TILE), TILE)
        acc[:, cols] = ev[:, cols].astype(F32) + mm(xv[z], dyg[z, :, cols], TN)

    bulk_forward(0)
    receive(copies)
    in_py[y] = sum(in_pj[k] for k in range(1, NJ)) + in_pj[0]
    copies = [send(in_py.at[y], in_py.at[y], at_y(k)) for k in ORDER]
    bulk_forward(1)
    receive(copies)
    all_p[j] = sum(in_py[k] for k in range(1, NY)) + in_py[0]
    copies = [send(all_p.at[j], all_p.at[j], at_j(k)) for k in ORDER]
    bulk_forward(2)
    receive(copies)
    p_sum = all_p[...].reshape(RANK, FEAT)
    p_twice = jnp.concatenate([p_sum, p_sum], axis=0)

    in_g[z] = mm(all_p[j], p_twice, NT, HIGHEST)
    copies = [send(in_g.at[z], in_g.at[z], at_z(k)) for k in ORDER]
    bulk_forward(3)
    add_grad(lax.rem(z + NZ - 1, NZ))
    add_grad(lax.rem(z + 1, NZ))
    receive(copies)
    all_g[j] = sum(in_g[k] for k in range(1, NZ)) + in_g[0]
    copies = [send(all_g.at[j], all_g.at[j], at_j(k)) for k in ORDER]
    bulk_forward(4)
    receive(copies)
    steps = {32: 5}
    between = lambda k: bulk_forward(steps[k]) if k in steps else None
    inverse = inverse_factor(all_g[...].reshape(RANK, 2 * RANK), between)
    p_t = mm(inverse, p_twice, NN, HIGHEST)
    p_out[...] = p_t
    p_high, p_low = split_rows(p_t)
    p_halves = jnp.concatenate([p_high, p_low], axis=0)

    far_steps = [k for k in ORDER if min(k, NZ - k) > NEAR]
    copies = []
    for k in far_steps:
        block = lax.rem(z + k, NZ)
        part_x[block] = split_lanes(mm(xv[block], p_halves, NT))
        copies.append(send(part_x.at[block], in_x.at[z], at_z(k)))
    bulk_forward(6)
    bulk_forward(7)
    for hop in range(2, NEAR + 1):
        add_grad(lax.rem(z + NZ - hop, NZ))
        add_grad(lax.rem(z + hop, NZ))

    @pl.loop(0, DOUT // TILE)
    def _(t):
        cols = pl.ds(pl.multiple_of(t * TILE, TILE), TILE)
        near_high, near_low = split_rows(acc[:, cols])
        tile = mm(p_halves, near_high, NN)
        q_near[:, cols] = tile[:RANK] + tile[RANK:] + mm(p_high, near_low, NN)

    receive(copies)
    bulk_forward(8)
    xp = split_lanes(sum(in_x[lax.rem(z + NZ - k, NZ)].astype(F32) for k in far_steps))
    copies = []
    for t in range(DOUT // TILE):
        cols = slice(t * TILE, t * TILE + TILE)
        tile = mm(xp, dyg[z, :, cols], TN)
        tile = tile[:RANK] + tile[RANK:] + q_near[:, cols]
        for k in range(8):
            q_part[k // 4, k % 4, :, cols] = tile[k * 8 : k * 8 + 8]
        copies.append(send(q_part.at[1 - core, :, :, cols], in_qc.at[:, :, cols], at_core))
    receive(copies)
    for k in range(NX):
        q_core[k] = q_part[core, k] + in_qc[k]
    copies = [send(q_core.at[lax.rem(x + k, NX)], in_qx.at[x], at_x(k)) for k in (2, 1, 3)]
    in_qx[x] = q_core[x]
    bulk_forward(9)
    receive(copies)
    rows = (in_qx[0] + in_qx[1]) + (in_qx[2] + in_qx[3])
    for k in range(NY):
        q_y[k] = rows[:, k * 256 : k * 256 + 256]
    copies = [send(q_y.at[lax.rem(y + k, NY)], in_qy.at[y], at_y(k)) for k in ORDER]
    in_qy[y] = q_y[y]
    receive(copies)
    in_qz[z] = sum(in_qy[k] for k in range(1, NY)) + in_qy[0]
    copies = [send(in_qz.at[z], in_qz.at[z], at_z(k)) for k in ORDER]
    receive(copies)
    all_qy[y] = sum(in_qz[k] for k in range(1, NZ)) + in_qz[0]
    copies = [send(all_qy.at[y], all_qy.at[y], at_y(k)) for k in ORDER]
    receive(copies)
    mine = core * NX + x
    for k in range(NY):
        all_q[mine, :, k * 256 : k * 256 + 256] = all_qy[k]
    copies = [send(all_q.at[mine], all_q.at[mine], at_x(k)) for k in (2, 1, 3)]
    across = [send(all_q.at[mine], all_q.at[mine], at_core)]
    for k, copy in ((1, copies[1]), (3, copies[2]), (2, copies[0])):
        copy.wait_recv()
        slot = core * NX + lax.rem(x - k + NX, NX)
        across.append(send(all_q.at[slot], all_q.at[slot], at_core))
    bulk_forward(10)
    bulk_forward(11)
    for hop in range(NEAR + 1, 4):
        add_grad(lax.rem(z + NZ - hop, NZ))
        add_grad(lax.rem(z + hop, NZ))
    bulk_forward(12)
    bulk_forward(13)
    add_grad(lax.rem(z + 4, NZ))
    receive(across)
    for way in (1, -1):
        for piece in flows[way][-2:]:
            bulk[(way, *piece)].wait_send()
    receive([])


def finish(acc, p_ref, q_ref, p_out, q_out, err_out, err_v, sem):
    copies = [pltpu.make_async_copy(p_ref, p_out, sem.at[0]), pltpu.make_async_copy(q_ref, q_out, sem.at[1])]
    for copy in copies:
        copy.start()
    p_high, p_low = split_rows(p_ref[...])
    p_cat = jnp.concatenate([p_high, p_high, p_low], axis=0)
    for t in range(DOUT // TILE):
        cols = slice(t * TILE, t * TILE + TILE)
        q_high, q_low = split_rows(q_ref[:, :, cols].reshape(RANK, TILE))
        approx = mm(p_cat, jnp.concatenate([q_high, q_low, q_high], axis=0), TN)
        err_v[:, cols] = (acc[:, cols] - approx).astype(BF16)
        copy = pltpu.make_async_copy(err_v.at[:, cols], err_out.at[:, cols], sem.at[2 + t])
        copy.start()
        copies.append(copy)
    for copy in copies:
        copy.wait()


def local(x_input, dy_grad, error_in, q_init):
    anywhere = pl.BlockSpec(memory_space=pl.ANY)
    vmem = lambda *shape, dtype=F32: pltpu.VMEM(shape, dtype)
    shapes = (
        jax.ShapeDtypeStruct((RANK, FEAT), F32),
        jax.ShapeDtypeStruct((8, 8, DOUT), F32),
        jax.ShapeDtypeStruct((FEAT, DOUT), F32),
    )
    held = [pl.BlockSpec(memory_space=pltpu.VMEM)] * 3
    p_t, q_t, acc = pl.pallas_call(
        kernel,
        out_shape=shapes,
        in_specs=[pl.BlockSpec(memory_space=pltpu.HBM)] * 4,
        out_specs=held,
        scratch_shapes=[
            vmem(NZ, TOK, DOUT, dtype=BF16),
            vmem(NZ, TOK, FEAT, dtype=BF16),
            vmem(FEAT, DOUT, dtype=BF16),
            vmem(RANK, DOUT),
            vmem(NZ, TOK, 2 * RANK, dtype=BF16),
            vmem(NJ, 8, FEAT), vmem(NJ, 8, FEAT), vmem(NY, 8, FEAT), vmem(NJ, 8, FEAT),
            vmem(NZ, 8, 2 * RANK), vmem(NJ, 8, 2 * RANK),
            vmem(NZ, TOK, 2 * RANK, dtype=BF16), vmem(NZ, TOK, 2 * RANK, dtype=BF16),
            vmem(2, NX, 8, DOUT), vmem(NX, 8, DOUT), vmem(NX, 8, DOUT), vmem(NX, 8, DOUT),
            vmem(NY, 8, FEAT), vmem(NY, 8, FEAT), vmem(NZ, 8, FEAT), vmem(NY, 8, FEAT),
            vmem(RANK, DOUT),
            pltpu.SemaphoreType.DMA((N_SEMS,)),
            pltpu.SemaphoreType.DMA((N_SEMS,)),
            pltpu.SemaphoreType.DMA((4,)),
        ],
        compiler_params=pltpu.CompilerParams(
            collective_id=0, has_side_effects=True, vmem_limit_bytes=48 * 1024 * 1024
        ),
        cost_estimate=pl.CostEstimate(flops=2 * 10**9, bytes_accessed=6 * 10**6, transcendentals=0),
    )(*(pltpu.with_memory_space_constraint(v, pltpu.HBM) for v in (x_input.reshape(NZ, TOK, FEAT), dy_grad[0], error_in[0], q_init.T)))
    p_t, q_t, err = pl.pallas_call(
        finish,
        out_shape=(*shapes[:2], jax.ShapeDtypeStruct((FEAT, DOUT), BF16)),
        in_specs=held,
        out_specs=[anywhere] * 3,
        scratch_shapes=[vmem(FEAT, DOUT, dtype=BF16), pltpu.SemaphoreType.DMA((2 + DOUT // TILE,))],
        compiler_params=pltpu.CompilerParams(vmem_limit_bytes=16 * 1024 * 1024),
        cost_estimate=pl.CostEstimate(flops=2 * 10**8, bytes_accessed=2 * 10**6, transcendentals=0),
    )(acc, p_t, q_t)
    return p_t.T, q_t.reshape(RANK, DOUT).T, err[None]


def solution(mesh):
    in_specs = (P("dp", None, "mp"), P("dp", "mp", None), P("dp", "mp", None), P())
    out_specs = (P("mp", None), P(), P("dp", "mp", None))
    return jax.shard_map(local, mesh=mesh, in_specs=in_specs, out_specs=out_specs, check_vma=False)
```

```python
import jax
import jax.numpy as jnp
from jax import lax
from jax.experimental import pallas as pl
from jax.experimental.pallas import tpu as pltpu
from jax.sharding import PartitionSpec as P

F32, BF16 = jnp.float32, jnp.bfloat16
HIGHEST = lax.Precision.HIGHEST
NZ, NY, NX = 8, 8, 4
NJ = 2 * NX
TOK, FEAT, DOUT, RANK = 192, 256, 2048, 64
CHUNKS = 4
PIECE = TOK // CHUNKS
TILE = 512
PIVOTS = 4
ORDER = (4, 3, 5, 2, 6, 1, 7)
N_SEMS = 128
NEAR = 2

NN = (((1,), (0,)), ((), ()))
NT = (((1,), (1,)), ((), ()))
TN = (((0,), (0,)), ((), ()))


def mm(a, b, dims, precision=None):
    return lax.dot_general(a, b, dims, precision=precision, preferred_element_type=F32)


def split_rows(v):
    high = v.astype(BF16)
    low = (v - high.astype(F32)).astype(BF16)
    return high, low


def split_lanes(v):
    both = v + pltpu.roll(v, RANK, axis=1)
    high = both.astype(BF16).astype(F32)
    lane = lax.broadcasted_iota(jnp.int32, both.shape, 1)
    return jnp.where(lane < RANK, high, both - high).astype(BF16)


def inverse_factor(gram2, between):
    lane = lax.broadcasted_iota(jnp.int32, gram2.shape, 1)
    row = lax.broadcasted_iota(jnp.int32, gram2.shape, 0)
    rows = lax.broadcasted_iota(jnp.int32, (RANK, 1), 0)
    a = jnp.where(lane < RANK, gram2, jnp.where(lane - RANK == row, 1.0, 0.0))
    for k in range(0, RANK, PIVOTS):
        columns = [jnp.broadcast_to(a[:, k + i : k + i + 1], a.shape) for i in range(PIVOTS)]
        lines = [a[k + i : k + i + 1, :] for i in range(PIVOTS)]
        for i in range(PIVOTS):
            here = slice(k + i, k + i + 1)
            factor = jnp.where(rows > k + i, columns[i] * (1.0 / columns[i][here]), 0.0)
            for later in range(i + 1, PIVOTS):
                columns[later] = columns[later] - factor * columns[later][here]
                lines[later] = lines[later] - factor[k + later : k + later + 1] * lines[i]
            a = a - factor * lines[i]
        between(k)
    diagonal = jnp.sum(jnp.where(lane == row, a, 0.0), axis=1, keepdims=True)
    root = lax.rsqrt(diagonal)
    root = root * (1.5 - 0.5 * (diagonal * root) * root)
    return jnp.where(lane < RANK, 0.0, a * root)


def kernel(
    x_ref, dy_ref, e_ref, q_ref, p_out, all_q, acc,
    dyg, xv, ev, qv, yq, part_p, in_pj, in_py, all_p, in_g, all_g, part_x, in_x,
    q_part, in_qc, q_core, in_qx, q_y, in_qy, in_qz, all_qy, q_near,
    send_sem, recv_sem, load_sem,
):
    dp, z = lax.axis_index("dp"), lax.axis_index("mp")
    y, j = lax.div(dp, NJ), lax.rem(dp, NJ)
    x, core = lax.div(j, 2), lax.rem(j, 2)
    counter = iter(range(N_SEMS))
    unsent = []

    at_z = lambda k: (dp, lax.rem(z + k + NZ, NZ))
    at_y = lambda k: (lax.rem(y + k, NY) * NJ + j, z)
    at_j = lambda k: (y * NJ + lax.rem(j + k, NJ), z)
    at_x = lambda k: (y * NJ + lax.rem(x + k, NX) * 2 + core, z)
    at_core = (y * NJ + x * 2 + 1 - core, z)

    def send(src, dst, device):
        n = next(counter)
        copy = pltpu.make_async_remote_copy(
            src_ref=src, dst_ref=dst, send_sem=send_sem.at[n], recv_sem=recv_sem.at[n],
            device_id=device, device_id_type=pl.DeviceIdType.MESH,
        )
        copy.start()
        unsent.append(copy)
        return copy

    def receive(copies):
        while len(unsent) > len(copies):
            unsent.pop(0).wait_send()
        for copy in copies:
            copy.wait_recv()

    loads = [
        pltpu.make_async_copy(src, dst, load_sem.at[n])
        for n, (src, dst) in enumerate(((dy_ref, dyg.at[z]), (q_ref, qv), (x_ref, xv), (e_ref, ev)))
    ]
    for load in loads:
        load.start()

    barrier = pltpu.get_barrier_semaphore()
    peers = [at_z(k) for k in range(1, NZ)] + [at_y(k) for k in range(1, NY)] + [at_j(k) for k in range(1, NJ)]
    for peer in peers:
        pl.semaphore_signal(barrier, inc=1, device_id=peer, device_id_type=pl.DeviceIdType.MESH)

    pl.semaphore_wait(barrier, len(peers))

    flows = {
        1: [(h, c) for h in (1, 2, 3) for c in range(CHUNKS)] + [(4, 0), (4, 1)],
        -1: [(h, c) for h in (1, 2, 3) for c in (2, 3, 0, 1)] + [(4, 2), (4, 3)],
    }
    bulk = {}

    def bulk_send(way, hop, c):
        block = lax.rem(z - way * (hop - 1) + NZ, NZ)
        ref = dyg.at[block, pl.ds(c * PIECE, PIECE)]
        source = dy_ref.at[pl.ds(c * PIECE, PIECE)] if hop == 1 else ref
        bulk[way, hop, c] = send(source, ref, at_z(way))
        unsent.pop()

    def first_sends(n):
        for way in (1, -1):
            bulk_send(way, *flows[way][n])

    def bulk_forward(n):
        for way in (1, -1):
            hop, c = flows[way][n]
            bulk[way, hop, c].wait_recv()
            if (hop + 1, c) in flows[way]:
                bulk_send(way, hop + 1, c)
            if n >= 2:
                bulk[(way, *flows[way][n - 2])].wait_send()

    def add_grad(block):
        @pl.loop(0, DOUT // TILE)
        def _(t):
            cols = pl.ds(pl.multiple_of(t * TILE, TILE), TILE)
            acc[:, cols] += mm(xv[block], dyg[block, :, cols], TN)

    first_sends(0)
    loads[0].wait()
    loads[1].wait()
    q_halves = jnp.concatenate(split_rows(qv[...]), axis=0)
    yq[z] = split_lanes(mm(dyg[z], q_halves, NT))
    right = send(yq.at[z], yq.at[z], at_z(1))
    left = send(yq.at[z], yq.at[z], at_z(-1))
    first_sends(1)
    loads[2].wait()
    loads[3].wait()
    total = mm(q_halves, ev[...], NT) + mm(yq[z], xv[z], TN)
    for hop in (1, 2, 3, 4):
        from_left, from_right = lax.rem(z - hop + NZ, NZ), lax.rem(z + hop, NZ)
        right.wait_recv()
        if hop < 4:
            right = send(yq.at[from_left], yq.at[from_left], at_z(1))
            left.wait_recv()
            if hop < 3:
                left = send(yq.at[from_right], yq.at[from_right], at_z(-1))
            if hop > 1:
                first_sends(hop)
            total += mm(yq[from_right], xv[from_right], TN)
        total += mm(yq[from_left], xv[from_left], TN)
    total = total[:RANK] + total[RANK:]

    for k in range(NJ):
        part_p[k] = total[k * 8 : k * 8 + 8]
    copies = [send(part_p.at[lax.rem(j + k, NJ)], in_pj.at[j], at_j(k)) for k in ORDER]
    in_pj[j] = part_p[j]

    @pl.loop(0, DOUT // TILE)
    def _(t):
        cols = pl.ds(pl.multiple_of(t * TILE, TILE), TILE)
        acc[:, cols] = ev[:, cols].astype(F32) + mm(xv[z], dyg[z, :, cols], TN)

    bulk_forward(0)
    receive(copies)
    in_py[y] = sum(in_pj[k] for k in range(1, NJ)) + in_pj[0]
    copies = [send(in_py.at[y], in_py.at[y], at_y(k)) for k in ORDER]
    bulk_forward(1)
    receive(copies)
    all_p[j] = sum(in_py[k] for k in range(1, NY)) + in_py[0]
    copies = [send(all_p.at[j], all_p.at[j], at_j(k)) for k in ORDER]
    bulk_forward(2)
    receive(copies)
    p_sum = all_p[...].reshape(RANK, FEAT)
    p_twice = jnp.concatenate([p_sum, p_sum], axis=0)

    in_g[z] = mm(all_p[j], p_twice, NT, HIGHEST)
    copies = [send(in_g.at[z], in_g.at[z], at_z(k)) for k in ORDER]
    bulk_forward(3)
    add_grad(lax.rem(z + NZ - 1, NZ))
    add_grad(lax.rem(z + 1, NZ))
    receive(copies)
    all_g[j] = sum(in_g[k] for k in range(1, NZ)) + in_g[0]
    copies = [send(all_g.at[j], all_g.at[j], at_j(k)) for k in ORDER]
    bulk_forward(4)
    receive(copies)
    steps = {32: 5}
    between = lambda k: bulk_forward(steps[k]) if k in steps else None
    inverse = inverse_factor(all_g[...].reshape(RANK, 2 * RANK), between)
    p_t = mm(inverse, p_twice, NN, HIGHEST)
    p_out[...] = p_t
    p_high, p_low = split_rows(p_t)
    p_halves = jnp.concatenate([p_high, p_low], axis=0)

    block = lax.rem(z + 4, NZ)
    part_x[0] = split_lanes(mm(xv[block], p_halves, NT))
    relay = send(part_x.at[0], in_x.at[2], at_z(-1))
    block = lax.rem(z + 3, NZ)
    part_x[1] = split_lanes(mm(xv[block], p_halves, NT))
    copies = [send(part_x.at[1], in_x.at[0], at_z(3))]
    block = lax.rem(z + 5, NZ)
    own_part = mm(xv[block], p_halves, NT)
    relay.wait_recv()
    part_x[2] = split_lanes(own_part + in_x[2].astype(F32))
    copies.append(send(part_x.at[2], in_x.at[1], at_z(5)))
    bulk_forward(6)
    bulk_forward(7)
    for hop in range(2, NEAR + 1):
        add_grad(lax.rem(z + NZ - hop, NZ))
        add_grad(lax.rem(z + hop, NZ))

    @pl.loop(0, DOUT // TILE)
    def _(t):
        cols = pl.ds(pl.multiple_of(t * TILE, TILE), TILE)
        near_high, near_low = split_rows(acc[:, cols])
        tile = mm(p_halves, near_high, NN)
        q_near[:, cols] = tile[:RANK] + tile[RANK:] + mm(p_high, near_low, NN)

    receive(copies)
    bulk_forward(8)
    xp = split_lanes(in_x[0].astype(F32) + in_x[1].astype(F32))
    copies = []
    for t in range(DOUT // TILE):
        cols = slice(t * TILE, t * TILE + TILE)
        tile = mm(xp, dyg[z, :, cols], TN)
        tile = tile[:RANK] + tile[RANK:] + q_near[:, cols]
        for k in range(8):
            q_part[k // 4, k % 4, :, cols] = tile[k * 8 : k * 8 + 8]
        copies.append(send(q_part.at[1 - core, :, :, cols], in_qc.at[:, :, cols], at_core))
    receive(copies)
    for k in range(NX):
        q_core[k] = q_part[core, k] + in_qc[k]
    copies = [send(q_core.at[lax.rem(x + k, NX)], in_qx.at[x], at_x(k)) for k in (2, 1, 3)]
    in_qx[x] = q_core[x]
    bulk_forward(9)
    receive(copies)
    rows = (in_qx[0] + in_qx[1]) + (in_qx[2] + in_qx[3])
    for k in range(NY):
        q_y[k] = rows[:, k * 256 : k * 256 + 256]
    copies = [send(q_y.at[lax.rem(y + k, NY)], in_qy.at[y], at_y(k)) for k in ORDER]
    in_qy[y] = q_y[y]
    receive(copies)
    in_qz[z] = sum(in_qy[k] for k in range(1, NY)) + in_qy[0]
    copies = [send(in_qz.at[z], in_qz.at[z], at_z(k)) for k in ORDER]
    receive(copies)
    all_qy[y] = sum(in_qz[k] for k in range(1, NZ)) + in_qz[0]
    copies = [send(all_qy.at[y], all_qy.at[y], at_y(k)) for k in ORDER]
    receive(copies)
    mine = core * NX + x
    for k in range(NY):
        all_q[mine, :, k * 256 : k * 256 + 256] = all_qy[k]
    copies = [send(all_q.at[mine], all_q.at[mine], at_x(k)) for k in (2, 1, 3)]
    across = [send(all_q.at[mine], all_q.at[mine], at_core)]
    for k, copy in ((1, copies[1]), (3, copies[2]), (2, copies[0])):
        copy.wait_recv()
        slot = core * NX + lax.rem(x - k + NX, NX)
        across.append(send(all_q.at[slot], all_q.at[slot], at_core))
    bulk_forward(10)
    bulk_forward(11)
    for hop in range(NEAR + 1, 4):
        add_grad(lax.rem(z + NZ - hop, NZ))
        add_grad(lax.rem(z + hop, NZ))
    bulk_forward(12)
    bulk_forward(13)
    add_grad(lax.rem(z + 4, NZ))
    receive(across)
    for way in (1, -1):
        for piece in flows[way][-2:]:
            bulk[(way, *piece)].wait_send()
    receive([])


def finish(acc, p_ref, q_ref, p_out, q_out, err_out, err_v, sem):
    copies = [pltpu.make_async_copy(p_ref, p_out, sem.at[0]), pltpu.make_async_copy(q_ref, q_out, sem.at[1])]
    for copy in copies:
        copy.start()
    p_high, p_low = split_rows(p_ref[...])
    p_cat = jnp.concatenate([p_high, p_high, p_low], axis=0)
    for t in range(DOUT // TILE):
        cols = slice(t * TILE, t * TILE + TILE)
        q_high, q_low = split_rows(q_ref[:, :, cols].reshape(RANK, TILE))
        approx = mm(p_cat, jnp.concatenate([q_high, q_low, q_high], axis=0), TN)
        err_v[:, cols] = (acc[:, cols] - approx).astype(BF16)
        copy = pltpu.make_async_copy(err_v.at[:, cols], err_out.at[:, cols], sem.at[2 + t])
        copy.start()
        copies.append(copy)
    for copy in copies:
        copy.wait()


def local(x_input, dy_grad, error_in, q_init):
    anywhere = pl.BlockSpec(memory_space=pl.ANY)
    vmem = lambda *shape, dtype=F32: pltpu.VMEM(shape, dtype)
    shapes = (
        jax.ShapeDtypeStruct((RANK, FEAT), F32),
        jax.ShapeDtypeStruct((8, 8, DOUT), F32),
        jax.ShapeDtypeStruct((FEAT, DOUT), F32),
    )
    held = [pl.BlockSpec(memory_space=pltpu.VMEM)] * 3
    p_t, q_t, acc = pl.pallas_call(
        kernel,
        out_shape=shapes,
        in_specs=[pl.BlockSpec(memory_space=pltpu.HBM)] * 4,
        out_specs=held,
        scratch_shapes=[
            vmem(NZ, TOK, DOUT, dtype=BF16),
            vmem(NZ, TOK, FEAT, dtype=BF16),
            vmem(FEAT, DOUT, dtype=BF16),
            vmem(RANK, DOUT),
            vmem(NZ, TOK, 2 * RANK, dtype=BF16),
            vmem(NJ, 8, FEAT), vmem(NJ, 8, FEAT), vmem(NY, 8, FEAT), vmem(NJ, 8, FEAT),
            vmem(NZ, 8, 2 * RANK), vmem(NJ, 8, 2 * RANK),
            vmem(3, TOK, 2 * RANK, dtype=BF16), vmem(3, TOK, 2 * RANK, dtype=BF16),
            vmem(2, NX, 8, DOUT), vmem(NX, 8, DOUT), vmem(NX, 8, DOUT), vmem(NX, 8, DOUT),
            vmem(NY, 8, FEAT), vmem(NY, 8, FEAT), vmem(NZ, 8, FEAT), vmem(NY, 8, FEAT),
            vmem(RANK, DOUT),
            pltpu.SemaphoreType.DMA((N_SEMS,)),
            pltpu.SemaphoreType.DMA((N_SEMS,)),
            pltpu.SemaphoreType.DMA((4,)),
        ],
        compiler_params=pltpu.CompilerParams(
            collective_id=0, has_side_effects=True, vmem_limit_bytes=48 * 1024 * 1024
        ),
        cost_estimate=pl.CostEstimate(flops=2 * 10**9, bytes_accessed=6 * 10**6, transcendentals=0),
    )(*(pltpu.with_memory_space_constraint(v, pltpu.HBM) for v in (x_input.reshape(NZ, TOK, FEAT), dy_grad[0], error_in[0], q_init.T)))
    p_t, q_t, err = pl.pallas_call(
        finish,
        out_shape=(*shapes[:2], jax.ShapeDtypeStruct((FEAT, DOUT), BF16)),
        in_specs=held,
        out_specs=[anywhere] * 3,
        scratch_shapes=[vmem(FEAT, DOUT, dtype=BF16), pltpu.SemaphoreType.DMA((2 + DOUT // TILE,))],
        compiler_params=pltpu.CompilerParams(vmem_limit_bytes=16 * 1024 * 1024),
        cost_estimate=pl.CostEstimate(flops=2 * 10**8, bytes_accessed=2 * 10**6, transcendentals=0),
    )(acc, p_t, q_t)
    return p_t.T, q_t.reshape(RANK, DOUT).T, err[None]


def solution(mesh):
    in_specs = (P("dp", None, "mp"), P("dp", "mp", None), P("dp", "mp", None), P())
    out_specs = (P("mp", None), P(), P("dp", "mp", None))
    return jax.shard_map(local, mesh=mesh, in_specs=in_specs, out_specs=out_specs, check_vma=False)
```

```python
import jax
import jax.numpy as jnp
from jax import lax
from jax.experimental import pallas as pl
from jax.experimental.pallas import tpu as pltpu
from jax.sharding import PartitionSpec as P

F32, BF16 = jnp.float32, jnp.bfloat16
HIGHEST = lax.Precision.HIGHEST
NZ, NY, NX = 8, 8, 4
NJ = 2 * NX
TOK, FEAT, DOUT, RANK = 192, 256, 2048, 64
CHUNKS = 4
PIECE = TOK // CHUNKS
TILE = 512
PIVOTS = 4
ORDER = (4, 3, 5, 2, 6, 1, 7)
N_SEMS = 128
NEAR = 2

NN = (((1,), (0,)), ((), ()))
NT = (((1,), (1,)), ((), ()))
TN = (((0,), (0,)), ((), ()))


def mm(a, b, dims, precision=None):
    return lax.dot_general(a, b, dims, precision=precision, preferred_element_type=F32)


def split_rows(v):
    high = v.astype(BF16)
    low = (v - high.astype(F32)).astype(BF16)
    return high, low


def split_lanes(v):
    both = v + pltpu.roll(v, RANK, axis=1)
    high = both.astype(BF16).astype(F32)
    lane = lax.broadcasted_iota(jnp.int32, both.shape, 1)
    return jnp.where(lane < RANK, high, both - high).astype(BF16)


def inverse_factor(gram2, between):
    lane = lax.broadcasted_iota(jnp.int32, gram2.shape, 1)
    row = lax.broadcasted_iota(jnp.int32, gram2.shape, 0)
    rows = lax.broadcasted_iota(jnp.int32, (RANK, 1), 0)
    a = jnp.where(lane < RANK, gram2, jnp.where(lane - RANK == row, 1.0, 0.0))
    for k in range(0, RANK, PIVOTS):
        columns = [jnp.broadcast_to(a[:, k + i : k + i + 1], a.shape) for i in range(PIVOTS)]
        lines = [a[k + i : k + i + 1, :] for i in range(PIVOTS)]
        for i in range(PIVOTS):
            here = slice(k + i, k + i + 1)
            factor = jnp.where(rows > k + i, columns[i] * (1.0 / columns[i][here]), 0.0)
            for later in range(i + 1, PIVOTS):
                columns[later] = columns[later] - factor * columns[later][here]
                lines[later] = lines[later] - factor[k + later : k + later + 1] * lines[i]
            a = a - factor * lines[i]
        between(k)
    diagonal = jnp.sum(jnp.where(lane == row, a, 0.0), axis=1, keepdims=True)
    root = lax.rsqrt(diagonal)
    root = root * (1.5 - 0.5 * (diagonal * root) * root)
    return jnp.where(lane < RANK, 0.0, a * root)


def kernel(
    x_ref, dy_ref, e_ref, q_ref, p_out, all_q, acc,
    dyg, xv, ev, qv, yq, part_p, in_pj, in_py, all_p, in_g, all_g, part_x, in_x,
    q_part, in_qc, q_core, in_qx, q_y, in_qy, in_qz, all_qy, q_near,
    send_sem, recv_sem, load_sem,
):
    dp, z = lax.axis_index("dp"), lax.axis_index("mp")
    y, j = lax.div(dp, NJ), lax.rem(dp, NJ)
    x, core = lax.div(j, 2), lax.rem(j, 2)
    counter = iter(range(N_SEMS))
    unsent = []

    at_z = lambda k: (dp, lax.rem(z + k + NZ, NZ))
    at_y = lambda k: (lax.rem(y + k, NY) * NJ + j, z)
    at_j = lambda k: (y * NJ + lax.rem(j + k, NJ), z)
    at_x = lambda k: (y * NJ + lax.rem(x + k, NX) * 2 + core, z)
    at_core = (y * NJ + x * 2 + 1 - core, z)

    def send(src, dst, device):
        n = next(counter)
        copy = pltpu.make_async_remote_copy(
            src_ref=src, dst_ref=dst, send_sem=send_sem.at[n], recv_sem=recv_sem.at[n],
            device_id=device, device_id_type=pl.DeviceIdType.MESH,
        )
        copy.start()
        unsent.append(copy)
        return copy

    def receive(copies):
        while len(unsent) > len(copies):
            unsent.pop(0).wait_send()
        for copy in copies:
            copy.wait_recv()

    loads = [
        pltpu.make_async_copy(src, dst, load_sem.at[n])
        for n, (src, dst) in enumerate(((dy_ref, dyg.at[z]), (q_ref, qv), (x_ref, xv), (e_ref, ev)))
    ]
    for load in loads:
        load.start()

    barrier = pltpu.get_barrier_semaphore()
    peers = [at_z(k) for k in range(1, NZ)] + [at_y(k) for k in range(1, NY)] + [at_j(k) for k in range(1, NJ)]
    for peer in peers:
        pl.semaphore_signal(barrier, inc=1, device_id=peer, device_id_type=pl.DeviceIdType.MESH)

    pl.semaphore_wait(barrier, len(peers))

    flows = {
        1: [(h, c) for h in (1, 2, 3) for c in range(CHUNKS)] + [(4, 0), (4, 1)],
        -1: [(h, c) for h in (1, 2, 3) for c in (2, 3, 0, 1)] + [(4, 2), (4, 3)],
    }
    bulk = {}

    def bulk_send(way, hop, c):
        block = lax.rem(z - way * (hop - 1) + NZ, NZ)
        ref = dyg.at[block, pl.ds(c * PIECE, PIECE)]
        source = dy_ref.at[pl.ds(c * PIECE, PIECE)] if hop == 1 else ref
        bulk[way, hop, c] = send(source, ref, at_z(way))
        unsent.pop()

    def first_sends(n):
        for way in (1, -1):
            bulk_send(way, *flows[way][n])

    def bulk_forward(n):
        for way in (1, -1):
            hop, c = flows[way][n]
            bulk[way, hop, c].wait_recv()
            if (hop + 1, c) in flows[way]:
                bulk_send(way, hop + 1, c)
            if n >= 2:
                bulk[(way, *flows[way][n - 2])].wait_send()

    def add_grad(block):
        @pl.loop(0, DOUT // TILE)
        def _(t):
            cols = pl.ds(pl.multiple_of(t * TILE, TILE), TILE)
            acc[:, cols] += mm(xv[block], dyg[block, :, cols], TN)

    first_sends(0)
    loads[0].wait()
    loads[1].wait()
    q_halves = jnp.concatenate(split_rows(qv[...]), axis=0)
    yq[z] = split_lanes(mm(dyg[z], q_halves, NT))
    right = send(yq.at[z], yq.at[z], at_z(1))
    left = send(yq.at[z], yq.at[z], at_z(-1))
    first_sends(1)
    loads[2].wait()
    loads[3].wait()
    total = mm(q_halves, ev[...], NT) + mm(yq[z], xv[z], TN)
    for hop in (1, 2, 3, 4):
        from_left, from_right = lax.rem(z - hop + NZ, NZ), lax.rem(z + hop, NZ)
        right.wait_recv()
        if hop < 4:
            right = send(yq.at[from_left], yq.at[from_left], at_z(1))
            left.wait_recv()
            if hop < 3:
                left = send(yq.at[from_right], yq.at[from_right], at_z(-1))
            if hop > 1:
                first_sends(hop)
            total += mm(yq[from_right], xv[from_right], TN)
        total += mm(yq[from_left], xv[from_left], TN)
    total = total[:RANK] + total[RANK:]

    for k in range(NJ):
        part_p[k] = total[k * 8 : k * 8 + 8]
    copies = [send(part_p.at[lax.rem(j + k, NJ)], in_pj.at[j], at_j(k)) for k in ORDER]
    in_pj[j] = part_p[j]

    @pl.loop(0, DOUT // TILE)
    def _(t):
        cols = pl.ds(pl.multiple_of(t * TILE, TILE), TILE)
        acc[:, cols] = ev[:, cols].astype(F32) + mm(xv[z], dyg[z, :, cols], TN)

    bulk_forward(0)
    receive(copies)
    in_py[y] = sum(in_pj[k] for k in range(1, NJ)) + in_pj[0]
    copies = [send(in_py.at[y], in_py.at[y], at_y(k)) for k in ORDER]
    bulk_forward(1)
    receive(copies)
    all_p[j] = sum(in_py[k] for k in range(1, NY)) + in_py[0]
    copies = [send(all_p.at[j], all_p.at[j], at_j(k)) for k in ORDER]
    bulk_forward(2)
    receive(copies)
    p_sum = all_p[...].reshape(RANK, FEAT)
    p_twice = jnp.concatenate([p_sum, p_sum], axis=0)

    in_g[z] = mm(all_p[j], p_twice, NT, HIGHEST)
    copies = [send(in_g.at[z], in_g.at[z], at_z(k)) for k in ORDER]
    bulk_forward(3)
    add_grad(lax.rem(z + NZ - 1, NZ))
    add_grad(lax.rem(z + 1, NZ))
    receive(copies)
    all_g[j] = sum(in_g[k] for k in range(1, NZ)) + in_g[0]
    copies = [send(all_g.at[j], all_g.at[j], at_j(k)) for k in ORDER]
    bulk_forward(4)
    receive(copies)
    steps = {32: 5}
    between = lambda k: bulk_forward(steps[k]) if k in steps else None
    inverse = inverse_factor(all_g[...].reshape(RANK, 2 * RANK), between)
    p_t = mm(inverse, p_twice, NN, HIGHEST)
    p_out[...] = p_t
    p_high, p_low = split_rows(p_t)
    p_halves = jnp.concatenate([p_high, p_low], axis=0)

    block = lax.rem(z + 4, NZ)
    part_x[0] = split_lanes(mm(xv[block], p_halves, NT))
    relay = send(part_x.at[0], in_x.at[2], at_z(-1))
    block = lax.rem(z + 3, NZ)
    part_x[1] = split_lanes(mm(xv[block], p_halves, NT))
    copies = [send(part_x.at[1], in_x.at[0], at_z(3))]
    block = lax.rem(z + 5, NZ)
    own_part = mm(xv[block], p_halves, NT)
    bulk_forward(6)
    relay.wait_recv()
    part_x[2] = split_lanes(own_part + in_x[2].astype(F32))
    copies.append(send(part_x.at[2], in_x.at[1], at_z(5)))
    bulk_forward(7)
    for hop in range(2, NEAR + 1):
        add_grad(lax.rem(z + NZ - hop, NZ))
        add_grad(lax.rem(z + hop, NZ))

    @pl.loop(0, DOUT // TILE)
    def _(t):
        cols = pl.ds(pl.multiple_of(t * TILE, TILE), TILE)
        near_high, near_low = split_rows(acc[:, cols])
        tile = mm(p_halves, near_high, NN)
        q_near[:, cols] = tile[:RANK] + tile[RANK:] + mm(p_high, near_low, NN)

    receive(copies)
    bulk_forward(8)
    xp = split_lanes(in_x[0].astype(F32) + in_x[1].astype(F32))
    copies = []
    for t in range(DOUT // TILE):
        cols = slice(t * TILE, t * TILE + TILE)
        tile = mm(xp, dyg[z, :, cols], TN)
        tile = tile[:RANK] + tile[RANK:] + q_near[:, cols]
        for k in range(8):
            q_part[k // 4, k % 4, :, cols] = tile[k * 8 : k * 8 + 8]
        copies.append(send(q_part.at[1 - core, :, :, cols], in_qc.at[:, :, cols], at_core))
    receive(copies)
    for k in range(NX):
        q_core[k] = q_part[core, k] + in_qc[k]
    copies = [send(q_core.at[lax.rem(x + k, NX)], in_qx.at[x], at_x(k)) for k in (2, 1, 3)]
    in_qx[x] = q_core[x]
    bulk_forward(9)
    receive(copies)
    rows = (in_qx[0] + in_qx[1]) + (in_qx[2] + in_qx[3])
    for k in range(NY):
        q_y[k] = rows[:, k * 256 : k * 256 + 256]
    copies = [send(q_y.at[lax.rem(y + k, NY)], in_qy.at[y], at_y(k)) for k in ORDER]
    in_qy[y] = q_y[y]
    receive(copies)
    in_qz[z] = sum(in_qy[k] for k in range(1, NY)) + in_qy[0]
    copies = [send(in_qz.at[z], in_qz.at[z], at_z(k)) for k in ORDER]
    receive(copies)
    all_qy[y] = sum(in_qz[k] for k in range(1, NZ)) + in_qz[0]
    copies = [send(all_qy.at[y], all_qy.at[y], at_y(k)) for k in ORDER]
    receive(copies)
    mine = core * NX + x
    for k in range(NY):
        all_q[mine, :, k * 256 : k * 256 + 256] = all_qy[k]
    copies = [send(all_q.at[mine], all_q.at[mine], at_x(k)) for k in (2, 1, 3)]
    across = [send(all_q.at[mine], all_q.at[mine], at_core)]
    for k, copy in ((1, copies[1]), (3, copies[2]), (2, copies[0])):
        copy.wait_recv()
        slot = core * NX + lax.rem(x - k + NX, NX)
        across.append(send(all_q.at[slot], all_q.at[slot], at_core))
    bulk_forward(10)
    bulk_forward(11)
    for hop in range(NEAR + 1, 4):
        add_grad(lax.rem(z + NZ - hop, NZ))
        add_grad(lax.rem(z + hop, NZ))
    bulk_forward(12)
    bulk_forward(13)
    add_grad(lax.rem(z + 4, NZ))
    receive(across)
    for way in (1, -1):
        for piece in flows[way][-2:]:
            bulk[(way, *piece)].wait_send()
    receive([])


def finish(acc, p_ref, q_ref, p_out, q_out, err_out, err_v, sem):
    copies = [pltpu.make_async_copy(p_ref, p_out, sem.at[0]), pltpu.make_async_copy(q_ref, q_out, sem.at[1])]
    for copy in copies:
        copy.start()
    p_high, p_low = split_rows(p_ref[...])
    p_cat = jnp.concatenate([p_high, p_high, p_low], axis=0)
    for t in range(DOUT // TILE):
        cols = slice(t * TILE, t * TILE + TILE)
        q_high, q_low = split_rows(q_ref[:, :, cols].reshape(RANK, TILE))
        approx = mm(p_cat, jnp.concatenate([q_high, q_low, q_high], axis=0), TN)
        err_v[:, cols] = (acc[:, cols] - approx).astype(BF16)
        copy = pltpu.make_async_copy(err_v.at[:, cols], err_out.at[:, cols], sem.at[2 + t])
        copy.start()
        copies.append(copy)
    for copy in copies:
        copy.wait()


def local(x_input, dy_grad, error_in, q_init):
    anywhere = pl.BlockSpec(memory_space=pl.ANY)
    vmem = lambda *shape, dtype=F32: pltpu.VMEM(shape, dtype)
    shapes = (
        jax.ShapeDtypeStruct((RANK, FEAT), F32),
        jax.ShapeDtypeStruct((8, 8, DOUT), F32),
        jax.ShapeDtypeStruct((FEAT, DOUT), F32),
    )
    held = [pl.BlockSpec(memory_space=pltpu.VMEM)] * 3
    p_t, q_t, acc = pl.pallas_call(
        kernel,
        out_shape=shapes,
        in_specs=[pl.BlockSpec(memory_space=pltpu.HBM)] * 4,
        out_specs=held,
        scratch_shapes=[
            vmem(NZ, TOK, DOUT, dtype=BF16),
            vmem(NZ, TOK, FEAT, dtype=BF16),
            vmem(FEAT, DOUT, dtype=BF16),
            vmem(RANK, DOUT),
            vmem(NZ, TOK, 2 * RANK, dtype=BF16),
            vmem(NJ, 8, FEAT), vmem(NJ, 8, FEAT), vmem(NY, 8, FEAT), vmem(NJ, 8, FEAT),
            vmem(NZ, 8, 2 * RANK), vmem(NJ, 8, 2 * RANK),
            vmem(3, TOK, 2 * RANK, dtype=BF16), vmem(3, TOK, 2 * RANK, dtype=BF16),
            vmem(2, NX, 8, DOUT), vmem(NX, 8, DOUT), vmem(NX, 8, DOUT), vmem(NX, 8, DOUT),
            vmem(NY, 8, FEAT), vmem(NY, 8, FEAT), vmem(NZ, 8, FEAT), vmem(NY, 8, FEAT),
            vmem(RANK, DOUT),
            pltpu.SemaphoreType.DMA((N_SEMS,)),
            pltpu.SemaphoreType.DMA((N_SEMS,)),
            pltpu.SemaphoreType.DMA((4,)),
        ],
        compiler_params=pltpu.CompilerParams(
            collective_id=0, has_side_effects=True, vmem_limit_bytes=48 * 1024 * 1024
        ),
        cost_estimate=pl.CostEstimate(flops=2 * 10**9, bytes_accessed=6 * 10**6, transcendentals=0),
    )(*(pltpu.with_memory_space_constraint(v, pltpu.HBM) for v in (x_input.reshape(NZ, TOK, FEAT), dy_grad[0], error_in[0], q_init.T)))
    p_t, q_t, err = pl.pallas_call(
        finish,
        out_shape=(*shapes[:2], jax.ShapeDtypeStruct((FEAT, DOUT), BF16)),
        in_specs=held,
        out_specs=[anywhere] * 3,
        scratch_shapes=[vmem(FEAT, DOUT, dtype=BF16), pltpu.SemaphoreType.DMA((2 + DOUT // TILE,))],
        compiler_params=pltpu.CompilerParams(vmem_limit_bytes=16 * 1024 * 1024),
        cost_estimate=pl.CostEstimate(flops=2 * 10**8, bytes_accessed=2 * 10**6, transcendentals=0),
    )(acc, p_t, q_t)
    return p_t.T, q_t.reshape(RANK, DOUT).T, err[None]


def solution(mesh):
    in_specs = (P("dp", None, "mp"), P("dp", "mp", None), P("dp", "mp", None), P())
    out_specs = (P("mp", None), P(), P("dp", "mp", None))
    return jax.shard_map(local, mesh=mesh, in_specs=in_specs, out_specs=out_specs, check_vma=False)
```

```python
import jax
import jax.numpy as jnp
from jax import lax
from jax.experimental import pallas as pl
from jax.experimental.pallas import tpu as pltpu
from jax.sharding import PartitionSpec as P

F32, BF16 = jnp.float32, jnp.bfloat16
HIGHEST = lax.Precision.HIGHEST
NZ, NY, NX = 8, 8, 4
NJ = 2 * NX
TOK, FEAT, DOUT, RANK = 192, 256, 2048, 64
CHUNKS = 4
PIECE = TOK // CHUNKS
TILE = 512
PIVOTS = 4
ORDER = (4, 3, 5, 2, 6, 1, 7)
N_SEMS = 128
NEAR = 2

NN = (((1,), (0,)), ((), ()))
NT = (((1,), (1,)), ((), ()))
TN = (((0,), (0,)), ((), ()))


def mm(a, b, dims, precision=None):
    return lax.dot_general(a, b, dims, precision=precision, preferred_element_type=F32)


def split_rows(v):
    high = v.astype(BF16)
    low = (v - high.astype(F32)).astype(BF16)
    return high, low


def split_lanes(v):
    both = v + pltpu.roll(v, RANK, axis=1)
    high = both.astype(BF16).astype(F32)
    lane = lax.broadcasted_iota(jnp.int32, both.shape, 1)
    return jnp.where(lane < RANK, high, both - high).astype(BF16)


def inverse_factor(gram2, between):
    lane = lax.broadcasted_iota(jnp.int32, gram2.shape, 1)
    row = lax.broadcasted_iota(jnp.int32, gram2.shape, 0)
    rows = lax.broadcasted_iota(jnp.int32, (RANK, 1), 0)
    a = jnp.where(lane < RANK, gram2, jnp.where(lane - RANK == row, 1.0, 0.0))
    for k in range(0, RANK, PIVOTS):
        columns = [jnp.broadcast_to(a[:, k + i : k + i + 1], a.shape) for i in range(PIVOTS)]
        lines = [a[k + i : k + i + 1, :] for i in range(PIVOTS)]
        for i in range(PIVOTS):
            here = slice(k + i, k + i + 1)
            factor = jnp.where(rows > k + i, columns[i] * (1.0 / columns[i][here]), 0.0)
            for later in range(i + 1, PIVOTS):
                columns[later] = columns[later] - factor * columns[later][here]
                lines[later] = lines[later] - factor[k + later : k + later + 1] * lines[i]
            a = a - factor * lines[i]
        between(k)
    diagonal = jnp.sum(jnp.where(lane == row, a, 0.0), axis=1, keepdims=True)
    root = lax.rsqrt(diagonal)
    root = root * (1.5 - 0.5 * (diagonal * root) * root)
    return jnp.where(lane < RANK, 0.0, a * root)


def kernel(
    x_ref, dy_ref, e_ref, q_ref, p_out, all_q, acc,
    dyg, xv, ev, qv, yq, part_p, in_pj, in_py, all_p, in_g, all_g, part_x, in_x,
    q_part, in_qc, q_core, in_qx, q_y, in_qy, in_qz, all_qy, q_near,
    send_sem, recv_sem, load_sem,
):
    dp, z = lax.axis_index("dp"), lax.axis_index("mp")
    y, j = lax.div(dp, NJ), lax.rem(dp, NJ)
    x, core = lax.div(j, 2), lax.rem(j, 2)
    counter = iter(range(N_SEMS))
    unsent = []

    at_z = lambda k: (dp, lax.rem(z + k + NZ, NZ))
    at_y = lambda k: (lax.rem(y + k, NY) * NJ + j, z)
    at_j = lambda k: (y * NJ + lax.rem(j + k, NJ), z)
    at_x = lambda k: (y * NJ + lax.rem(x + k, NX) * 2 + core, z)
    at_core = (y * NJ + x * 2 + 1 - core, z)

    def send(src, dst, device):
        n = next(counter)
        copy = pltpu.make_async_remote_copy(
            src_ref=src, dst_ref=dst, send_sem=send_sem.at[n], recv_sem=recv_sem.at[n],
            device_id=device, device_id_type=pl.DeviceIdType.MESH,
        )
        copy.start()
        unsent.append(copy)
        return copy

    def receive(copies):
        while len(unsent) > len(copies):
            unsent.pop(0).wait_send()
        for copy in copies:
            copy.wait_recv()

    loads = [
        pltpu.make_async_copy(src, dst, load_sem.at[n])
        for n, (src, dst) in enumerate(((dy_ref, dyg.at[z]), (q_ref, qv), (x_ref, xv), (e_ref, ev)))
    ]
    for load in loads:
        load.start()

    barrier = pltpu.get_barrier_semaphore()
    peers = [at_z(k) for k in range(1, NZ)] + [at_y(k) for k in range(1, NY)] + [at_j(k) for k in range(1, NJ)]
    for peer in peers:
        pl.semaphore_signal(barrier, inc=1, device_id=peer, device_id_type=pl.DeviceIdType.MESH)

    pl.semaphore_wait(barrier, len(peers))

    flows = {
        1: [(h, c) for h in (1, 2, 3) for c in range(CHUNKS)] + [(4, 0), (4, 1)],
        -1: [(h, c) for h in (1, 2, 3) for c in (2, 3, 0, 1)] + [(4, 2), (4, 3)],
    }
    bulk = {}

    def bulk_send(way, hop, c):
        block = lax.rem(z - way * (hop - 1) + NZ, NZ)
        ref = dyg.at[block, pl.ds(c * PIECE, PIECE)]
        source = dy_ref.at[pl.ds(c * PIECE, PIECE)] if hop == 1 else ref
        bulk[way, hop, c] = send(source, ref, at_z(way))
        unsent.pop()

    def first_sends(n):
        for way in (1, -1):
            bulk_send(way, *flows[way][n])

    def bulk_forward(n):
        for way in (1, -1):
            hop, c = flows[way][n]
            bulk[way, hop, c].wait_recv()
            if (hop + 1, c) in flows[way]:
                bulk_send(way, hop + 1, c)
            if n >= 2:
                bulk[(way, *flows[way][n - 2])].wait_send()

    def add_grad(block):
        @pl.loop(0, DOUT // TILE)
        def _(t):
            cols = pl.ds(pl.multiple_of(t * TILE, TILE), TILE)
            acc[:, cols] += mm(xv[block], dyg[block, :, cols], TN)

    first_sends(0)
    loads[0].wait()
    loads[1].wait()
    q_halves = jnp.concatenate(split_rows(qv[...]), axis=0)
    yq[z] = split_lanes(mm(dyg[z], q_halves, NT))
    right = send(yq.at[z], yq.at[z], at_z(1))
    left = send(yq.at[z], yq.at[z], at_z(-1))
    first_sends(1)
    loads[2].wait()
    loads[3].wait()
    total = mm(q_halves, ev[...], NT) + mm(yq[z], xv[z], TN)
    for hop in (1, 2, 3, 4):
        from_left, from_right = lax.rem(z - hop + NZ, NZ), lax.rem(z + hop, NZ)
        right.wait_recv()
        if hop < 4:
            right = send(yq.at[from_left], yq.at[from_left], at_z(1))
            left.wait_recv()
            if hop < 3:
                left = send(yq.at[from_right], yq.at[from_right], at_z(-1))
            if hop > 1:
                first_sends(hop)
            total += mm(yq[from_right], xv[from_right], TN)
        total += mm(yq[from_left], xv[from_left], TN)
    total = total[:RANK] + total[RANK:]

    for k in range(NJ):
        part_p[k] = total[k * 8 : k * 8 + 8]
    copies = [send(part_p.at[lax.rem(j + k, NJ)], in_pj.at[j], at_j(k)) for k in ORDER]
    in_pj[j] = part_p[j]

    @pl.loop(0, DOUT // TILE)
    def _(t):
        cols = pl.ds(pl.multiple_of(t * TILE, TILE), TILE)
        acc[:, cols] = ev[:, cols].astype(F32) + mm(xv[z], dyg[z, :, cols], TN)

    bulk_forward(0)
    receive(copies)
    in_py[y] = sum(in_pj[k] for k in range(1, NJ)) + in_pj[0]
    copies = [send(in_py.at[y], in_py.at[y], at_y(k)) for k in ORDER]
    bulk_forward(1)
    receive(copies)
    all_p[j] = sum(in_py[k] for k in range(1, NY)) + in_py[0]
    copies = [send(all_p.at[j], all_p.at[j], at_j(k)) for k in ORDER]
    bulk_forward(2)
    receive(copies)
    p_sum = all_p[...].reshape(RANK, FEAT)
    p_twice = jnp.concatenate([p_sum, p_sum], axis=0)

    in_g[z] = mm(all_p[j], p_twice, NT, HIGHEST)
    copies = [send(in_g.at[z], in_g.at[z], at_z(k)) for k in ORDER]
    bulk_forward(3)
    add_grad(lax.rem(z + NZ - 1, NZ))
    add_grad(lax.rem(z + 1, NZ))
    receive(copies)
    all_g[j] = sum(in_g[k] for k in range(1, NZ)) + in_g[0]
    copies = [send(all_g.at[j], all_g.at[j], at_j(k)) for k in ORDER]
    bulk_forward(4)
    receive(copies)
    steps = {32: 5}
    between = lambda k: bulk_forward(steps[k]) if k in steps else None
    inverse = inverse_factor(all_g[...].reshape(RANK, 2 * RANK), between)
    p_t = mm(inverse, p_twice, NN, HIGHEST)
    p_out[...] = p_t
    p_high, p_low = split_rows(p_t)
    p_halves = jnp.concatenate([p_high, p_low], axis=0)

    block = lax.rem(z + 4, NZ)
    part_x[0] = split_lanes(mm(xv[block], p_halves, NT))
    relay = send(part_x.at[0], in_x.at[2], at_z(-1))
    block = lax.rem(z + 3, NZ)
    part_x[1] = split_lanes(mm(xv[block], p_halves, NT))
    copies = [send(part_x.at[1], in_x.at[0], at_z(3))]
    block = lax.rem(z + 5, NZ)
    own_part = mm(xv[block], p_halves, NT)
    bulk_forward(6)
    relay.wait_recv()
    part_x[2] = split_lanes(own_part + in_x[2].astype(F32))
    copies.append(send(part_x.at[2], in_x.at[1], at_z(5)))
    bulk_forward(7)
    for hop in range(2, NEAR + 1):
        add_grad(lax.rem(z + NZ - hop, NZ))
        add_grad(lax.rem(z + hop, NZ))

    @pl.loop(0, DOUT // TILE)
    def _(t):
        cols = pl.ds(pl.multiple_of(t * TILE, TILE), TILE)
        near_high, near_low = split_rows(acc[:, cols])
        tile = mm(p_halves, near_high, NN)
        q_near[:, cols] = tile[:RANK] + tile[RANK:] + mm(p_high, near_low, NN)

    receive(copies)
    bulk_forward(8)
    xp = split_lanes(in_x[0].astype(F32) + in_x[1].astype(F32))
    copies = []
    for t in range(DOUT // TILE):
        cols = slice(t * TILE, t * TILE + TILE)
        tile = mm(xp, dyg[z, :, cols], TN)
        tile = tile[:RANK] + tile[RANK:] + q_near[:, cols]
        for k in range(8):
            q_part[k // 4, k % 4, :, cols] = tile[k * 8 : k * 8 + 8]
        copies.append(send(q_part.at[1 - core, :, :, cols], in_qc.at[:, :, cols], at_core))
    bulk_forward(9)
    receive(copies)
    for k in range(NX):
        q_core[k] = q_part[core, k] + in_qc[k]
    copies = [send(q_core.at[lax.rem(x + k, NX)], in_qx.at[x], at_x(k)) for k in (2, 1, 3)]
    in_qx[x] = q_core[x]
    receive(copies)
    rows = (in_qx[0] + in_qx[1]) + (in_qx[2] + in_qx[3])
    for k in range(NY):
        q_y[k] = rows[:, k * 256 : k * 256 + 256]
    copies = [send(q_y.at[lax.rem(y + k, NY)], in_qy.at[y], at_y(k)) for k in ORDER]
    in_qy[y] = q_y[y]
    receive(copies)
    in_qz[z] = sum(in_qy[k] for k in range(1, NY)) + in_qy[0]
    copies = [send(in_qz.at[z], in_qz.at[z], at_z(k)) for k in ORDER]
    receive(copies)
    all_qy[y] = sum(in_qz[k] for k in range(1, NZ)) + in_qz[0]
    copies = [send(all_qy.at[y], all_qy.at[y], at_y(k)) for k in ORDER]
    receive(copies)
    mine = core * NX + x
    for k in range(NY):
        all_q[mine, :, k * 256 : k * 256 + 256] = all_qy[k]
    copies = [send(all_q.at[mine], all_q.at[mine], at_x(k)) for k in (2, 1, 3)]
    across = [send(all_q.at[mine], all_q.at[mine], at_core)]
    for k, copy in ((1, copies[1]), (3, copies[2]), (2, copies[0])):
        copy.wait_recv()
        slot = core * NX + lax.rem(x - k + NX, NX)
        across.append(send(all_q.at[slot], all_q.at[slot], at_core))
    bulk_forward(10)
    bulk_forward(11)
    for hop in range(NEAR + 1, 4):
        add_grad(lax.rem(z + NZ - hop, NZ))
        add_grad(lax.rem(z + hop, NZ))
    bulk_forward(12)
    bulk_forward(13)
    add_grad(lax.rem(z + 4, NZ))
    receive(across)
    for way in (1, -1):
        for piece in flows[way][-2:]:
            bulk[(way, *piece)].wait_send()
    receive([])


def finish(acc, p_ref, q_ref, p_out, q_out, err_out, err_v, sem):
    copies = [pltpu.make_async_copy(p_ref, p_out, sem.at[0]), pltpu.make_async_copy(q_ref, q_out, sem.at[1])]
    for copy in copies:
        copy.start()
    p_high, p_low = split_rows(p_ref[...])
    p_cat = jnp.concatenate([p_high, p_high, p_low], axis=0)
    for t in range(DOUT // TILE):
        cols = slice(t * TILE, t * TILE + TILE)
        q_high, q_low = split_rows(q_ref[:, :, cols].reshape(RANK, TILE))
        approx = mm(p_cat, jnp.concatenate([q_high, q_low, q_high], axis=0), TN)
        err_v[:, cols] = (acc[:, cols] - approx).astype(BF16)
        copy = pltpu.make_async_copy(err_v.at[:, cols], err_out.at[:, cols], sem.at[2 + t])
        copy.start()
        copies.append(copy)
    for copy in copies:
        copy.wait()


def local(x_input, dy_grad, error_in, q_init):
    anywhere = pl.BlockSpec(memory_space=pl.ANY)
    vmem = lambda *shape, dtype=F32: pltpu.VMEM(shape, dtype)
    shapes = (
        jax.ShapeDtypeStruct((RANK, FEAT), F32),
        jax.ShapeDtypeStruct((8, 8, DOUT), F32),
        jax.ShapeDtypeStruct((FEAT, DOUT), F32),
    )
    held = [pl.BlockSpec(memory_space=pltpu.VMEM)] * 3
    p_t, q_t, acc = pl.pallas_call(
        kernel,
        out_shape=shapes,
        in_specs=[pl.BlockSpec(memory_space=pltpu.HBM)] * 4,
        out_specs=held,
        scratch_shapes=[
            vmem(NZ, TOK, DOUT, dtype=BF16),
            vmem(NZ, TOK, FEAT, dtype=BF16),
            vmem(FEAT, DOUT, dtype=BF16),
            vmem(RANK, DOUT),
            vmem(NZ, TOK, 2 * RANK, dtype=BF16),
            vmem(NJ, 8, FEAT), vmem(NJ, 8, FEAT), vmem(NY, 8, FEAT), vmem(NJ, 8, FEAT),
            vmem(NZ, 8, 2 * RANK), vmem(NJ, 8, 2 * RANK),
            vmem(3, TOK, 2 * RANK, dtype=BF16), vmem(3, TOK, 2 * RANK, dtype=BF16),
            vmem(2, NX, 8, DOUT), vmem(NX, 8, DOUT), vmem(NX, 8, DOUT), vmem(NX, 8, DOUT),
            vmem(NY, 8, FEAT), vmem(NY, 8, FEAT), vmem(NZ, 8, FEAT), vmem(NY, 8, FEAT),
            vmem(RANK, DOUT),
            pltpu.SemaphoreType.DMA((N_SEMS,)),
            pltpu.SemaphoreType.DMA((N_SEMS,)),
            pltpu.SemaphoreType.DMA((4,)),
        ],
        compiler_params=pltpu.CompilerParams(
            collective_id=0, has_side_effects=True, vmem_limit_bytes=48 * 1024 * 1024
        ),
        cost_estimate=pl.CostEstimate(flops=2 * 10**9, bytes_accessed=6 * 10**6, transcendentals=0),
    )(*(pltpu.with_memory_space_constraint(v, pltpu.HBM) for v in (x_input.reshape(NZ, TOK, FEAT), dy_grad[0], error_in[0], q_init.T)))
    p_t, q_t, err = pl.pallas_call(
        finish,
        out_shape=(*shapes[:2], jax.ShapeDtypeStruct((FEAT, DOUT), BF16)),
        in_specs=held,
        out_specs=[anywhere] * 3,
        scratch_shapes=[vmem(FEAT, DOUT, dtype=BF16), pltpu.SemaphoreType.DMA((2 + DOUT // TILE,))],
        compiler_params=pltpu.CompilerParams(vmem_limit_bytes=16 * 1024 * 1024),
        cost_estimate=pl.CostEstimate(flops=2 * 10**8, bytes_accessed=2 * 10**6, transcendentals=0),
    )(acc, p_t, q_t)
    return p_t.T, q_t.reshape(RANK, DOUT).T, err[None]


def solution(mesh):
    in_specs = (P("dp", None, "mp"), P("dp", "mp", None), P("dp", "mp", None), P())
    out_specs = (P("mp", None), P(), P("dp", "mp", None))
    return jax.shard_map(local, mesh=mesh, in_specs=in_specs, out_specs=out_specs, check_vma=False)
```
